128 devices in a mesh: doc: 8 (over x, core), ctx: 16 (over y, z).
Axes of the slice: x: 4, y: 4, z: 4, core: 2. Of those that a mesh axis runs over, the one named last changes fastest.
Arguments:
- queries: bfloat16 [8, 2048, 4096], P('doc', 'ctx'), may hold values from -8 to 8
- image_kv: bfloat16 [32, 256, 1024], P('doc', 'ctx'), may hold values from -4 to 4
- d_out: bfloat16 [8, 2048, 4096], P('doc', 'ctx'), may hold values from -24 to 24
- attn_gate: float32 [1], replicated, may hold values from 0.4 to 2
- image_slots: int32 [32], replicated, may hold values from 0 to 31, as said below
- spans: int32 [8, 2048, 2], P('doc', 'ctx'), may hold values from 0 to 4, as said below
Outputs:
- d_queries: bfloat16 [8, 2048, 4096], P('doc', 'ctx')
- d_image_kv: float32 [32, 256, 1024], P('doc', 'ctx')
The draws below stay inside these ranges and needn't reach their ends.
Inputs may be any that keep to these rules, and one draw needn't show every extreme that they name: `image_slots`: A permutation of the 32 slots; slots s with s // 4 = g form owner group g. No owner group holds two images of one document. spans[d, t, 0] < spans[d, t, 1]; both never decrease along a document's text; the first token sees image 0 and the last token's second entry is 4.
All inputs are finite; a program needn't handle non-finite values.
Results may differ from the reference program's by a relative error of at most 0.022.
Values may be sent and summed in bfloat16 or wider, within the bound.
No kernel may reach another device: no remote copies, remote signals or barrier semaphores. Data moves between devices by JAX's collectives and lax.ppermute only.
A program may use at most 128 MiB of HBM per device.

```python
import jax
import jax.numpy as jnp
from jax import lax

HQ = 32
KEY_VALUE_HEADS = 4
HEAD_WIDTH = 128
IMAGES_PER_DOC = 4
HEAD_GROUP_SIZE = 8
QW = 4096
KEY_COLUMNS = 512
DOCUMENT_COUNT = 8
TEXT_LENGTH = 2048
IMAGE_ROW_COUNT = 256
SLOTS = 32
N_DOC = 8


def draw_queries(key, part):
    key = jax.random.fold_in(key, 11)
    key_values = jax.random.fold_in(key, 0)
    dimension_numbers = (DOCUMENT_COUNT, TEXT_LENGTH, KEY_VALUE_HEADS, HEAD_GROUP_SIZE, HEAD_WIDTH)
    value_tensor = jnp.clip(jax.random.normal(key_values, dimension_numbers, jnp.float32), -4.0, 4.0)
    return value_tensor.reshape(DOCUMENT_COUNT, TEXT_LENGTH, HQ * HEAD_WIDTH).astype(jnp.bfloat16)


def draw_image_kv(key, part):
    key = jax.random.fold_in(key, 23)
    dimension_numbers = (SLOTS, IMAGE_ROW_COUNT, 2 * KEY_COLUMNS)
    value_tensor = jnp.clip(jax.random.normal(key, dimension_numbers, jnp.float32), -4.0, 4.0)
    return value_tensor.astype(jnp.bfloat16)


def draw_image_slots(key, part):
    key = jax.random.fold_in(key, 37)
    key_offset, key_local = jax.random.split(key)
    group_ids = jnp.arange(N_DOC, dtype=jnp.int32)
    ranking = jax.random.randint(key_offset, (N_DOC,), 0, 1 << 20) * N_DOC + group_ids
    ranking = jnp.where(group_ids == N_DOC - 1, -3, jnp.where(group_ids == 1, -2, jnp.where(group_ids == N_DOC // 2, -1, ranking)))
    offsets = jnp.argsort(ranking, stable=True)[:IMAGES_PER_DOC].astype(jnp.int32)
    scores = jax.random.randint(key_local, (N_DOC, IMAGES_PER_DOC), 0, 1 << 20) * IMAGES_PER_DOC + jnp.arange(IMAGES_PER_DOC, dtype=jnp.int32)[None, :]
    local_order = jnp.argsort(scores, axis=1, stable=True).astype(jnp.int32)
    documents = jnp.arange(DOCUMENT_COUNT, dtype=jnp.int32)[:, None]
    owner_group = (documents + offsets[None, :]) % N_DOC
    columns = jnp.broadcast_to(jnp.arange(IMAGES_PER_DOC, dtype=jnp.int32)[None, :], (DOCUMENT_COUNT, IMAGES_PER_DOC))
    local_slot = local_order[owner_group, columns]
    return (owner_group * IMAGES_PER_DOC + local_slot).reshape(SLOTS).astype(jnp.int32)


def draw_spans(key, part):
    key = jax.random.fold_in(key, 53)
    key_place, key_width = jax.random.split(key)
    place_keys = jax.random.split(key_place, DOCUMENT_COUNT)

    def places(one_key):
        picked_images = jax.random.permutation(one_key, TEXT_LENGTH - 1)[:IMAGES_PER_DOC - 1].astype(jnp.int32) + 1
        return jnp.sort(jnp.concatenate([jnp.zeros((1,), jnp.int32), picked_images]))
    starts = jax.vmap(places)(place_keys)
    position = jnp.arange(TEXT_LENGTH, dtype=jnp.int32)
    span_high = jnp.sum((starts[:, None, :] <= position[None, :, None]).astype(jnp.int32), axis=2)
    widths = jax.random.randint(key_width, (DOCUMENT_COUNT, 1), 1, IMAGES_PER_DOC + 1)
    span_low = jnp.maximum(span_high - widths, 0)
    return jnp.stack([span_low, span_high], axis=2).astype(jnp.int32)


def block_scale(own_key, shape, cuts, low, top_value):
    loudness, own = 1.0, jax.random.fold_in(own_key, 6)
    for axis_at, parts in cuts:
        heights = jnp.exp(jax.random.uniform(jax.random.fold_in(own, axis_at), (parts,), jnp.float32, low / len(cuts), top_value / len(cuts)))
        loudness = loudness * jnp.repeat(heights, shape[axis_at] // parts).reshape([-1 if axis == axis_at else 1 for axis in range(len(shape))])
    return loudness


def bell_draw(stream_key, extent, width, reach, cuts=(), kind=jnp.bfloat16):
    factor_of = block_scale(stream_key, extent, cuts, -0.22, 0.18) if cuts else 1.0
    result = jax.random.normal(stream_key, extent, jnp.float32) * width * factor_of
    return jnp.minimum(jnp.maximum(result, -reach), reach).astype(kind)


def setup_inputs(seed: int = 0) -> dict:
    keys = jax.random.split(jax.random.key(seed), 7)
    queries = draw_queries(jax.random.fold_in(keys[6], 71), 0)
    image_kv = draw_image_kv(jax.random.fold_in(keys[6], 71), 0)
    d_out = bell_draw(keys[2], (DOCUMENT_COUNT, TEXT_LENGTH, QW), 4.0, 24.0, ((0, 8), (1, 16)))
    attn_gate = jnp.clip(jax.random.uniform(keys[3], (1,), jnp.float32, 0.4, 2.0), 0.4, 2.0)
    image_slots = draw_image_slots(jax.random.fold_in(keys[6], 71), 0)
    spans = draw_spans(jax.random.fold_in(keys[6], 71), 0)
    return {"queries": queries, "image_kv": image_kv, "d_out": d_out, "attn_gate": attn_gate, "image_slots": image_slots, "spans": spans}


negative_bound = -1e30


def head_grads(operands):
    q_head, d_head, key_tensor, value_tensor, visible_mask = operands
    score_scale = HEAD_WIDTH ** -0.5
    q_wide = q_head.astype(jnp.float32)
    d_wide = d_head.astype(jnp.float32)
    k_wide = key_tensor.astype(jnp.float32)
    v_wide = value_tensor.astype(jnp.float32)
    mask_now = visible_mask[:, None, :, None]
    scores = jnp.einsum("tgd,jkd->tgjk", q_wide, k_wide) * score_scale
    masked = jnp.where(mask_now, scores, negative_bound)
    row_maximum = jnp.max(masked, axis=(2, 3))
    expo = jnp.where(mask_now, jnp.exp(scores - row_maximum[:, :, None, None]), 0.0)
    row_total_sum = jnp.sum(expo, axis=(2, 3))
    probs = expo / row_total_sum[:, :, None, None]
    probs_low = probs.astype(jnp.bfloat16).astype(jnp.float32)
    attention_output = jnp.einsum("tgjk,jkd->tgd", probs_low, v_wide)
    delta = jnp.sum(d_wide * attention_output, axis=2)
    d_probs = jnp.einsum("tgd,jkd->tgjk", d_wide, v_wide)
    d_scores = (probs * (d_probs - delta[:, :, None, None])).astype(jnp.bfloat16).astype(jnp.float32)
    query_gradient = jnp.einsum("tgjk,jkd->tgd", d_scores, k_wide) * score_scale
    d_keys = jnp.einsum("tgjk,tgd->jkd", d_scores, q_wide) * score_scale
    d_values = jnp.einsum("tgjk,tgd->jkd", probs_low, d_wide)
    return query_gradient, d_keys, d_values


def doc_grads(operands):
    query_row_block, row_gradient, key_value_rows, span_low, span_high = operands
    text_length = query_row_block.shape[0]
    query_split = query_row_block.reshape(text_length, KEY_VALUE_HEADS, HEAD_GROUP_SIZE, HEAD_WIDTH).transpose(1, 0, 2, 3)
    split_gradient = row_gradient.reshape(text_length, KEY_VALUE_HEADS, HEAD_GROUP_SIZE, HEAD_WIDTH).transpose(1, 0, 2, 3)
    key_tensor = key_value_rows[:, :, :KEY_COLUMNS].reshape(IMAGES_PER_DOC, IMAGE_ROW_COUNT, KEY_VALUE_HEADS, HEAD_WIDTH).transpose(2, 0, 1, 3)
    value_tensor = key_value_rows[:, :, KEY_COLUMNS:].reshape(IMAGES_PER_DOC, IMAGE_ROW_COUNT, KEY_VALUE_HEADS, HEAD_WIDTH).transpose(2, 0, 1, 3)
    image_ids = jnp.arange(IMAGES_PER_DOC, dtype=jnp.int32)
    visible_mask = (span_low[:, None] <= image_ids[None, :]) & (image_ids[None, :] < span_high[:, None])
    every_visible_mask = jnp.broadcast_to(visible_mask[None], (KEY_VALUE_HEADS,) + visible_mask.shape)
    query_gradient, d_keys, d_values = lax.map(head_grads, (query_split, split_gradient, key_tensor, value_tensor, every_visible_mask))
    query_gradient = query_gradient.transpose(1, 0, 2, 3).reshape(text_length, QW).astype(jnp.bfloat16)
    d_keys = d_keys.transpose(1, 2, 0, 3).reshape(IMAGES_PER_DOC, IMAGE_ROW_COUNT, KEY_COLUMNS)
    d_values = d_values.transpose(1, 2, 0, 3).reshape(IMAGES_PER_DOC, IMAGE_ROW_COUNT, KEY_COLUMNS)
    return query_gradient, jnp.concatenate([d_keys, d_values], axis=2)


def reference(queries, image_kv, d_out, attn_gate, image_slots, spans):
    d_attn = (jnp.tanh(attn_gate[0]) * d_out.astype(jnp.float32)).astype(jnp.bfloat16)
    doc_slots = image_slots.astype(jnp.int32).reshape(DOCUMENT_COUNT, IMAGES_PER_DOC)
    kv_docs = jnp.take(image_kv, doc_slots, axis=0)
    d_queries, grad_docs = lax.map(doc_grads, (queries, d_attn, kv_docs, spans[:, :, 0], spans[:, :, 1]))
    flat = grad_docs.reshape(SLOTS, IMAGE_ROW_COUNT, 2 * KEY_COLUMNS)
    d_image_kv = jnp.zeros((SLOTS, IMAGE_ROW_COUNT, 2 * KEY_COLUMNS), jnp.float32).at[image_slots.astype(jnp.int32)].set(flat)
    return d_queries, d_image_kv
```

```python
import functools

import jax
import jax.numpy as jnp
from jax import lax
from jax.experimental import pallas as pl
from jax.experimental.pallas import tpu as pltpu
from jax.sharding import PartitionSpec as P

KV_HEADS = 4
WIDTH = 128
GROUP = 8
KEY_COLUMNS = 512
IMAGES = 4
LOW = -1e30
SCALE = WIDTH ** (-0.5)
LOG2E = 1.4426950408889634
VMEM_LIMIT = 48 * 1024 * 1024

SMEM = pltpu.MemorySpace.SMEM
VMEM = pltpu.MemorySpace.VMEM


def pack_kernel(docs, me, slots, kv, out):
    for d in range(docs):
        local = 0
        for j in range(IMAGES):
            s = slots[d * IMAGES + j]
            local += jnp.where(s // IMAGES == me[0], s % IMAGES, 0)
        out[d] = kv[local]


def pick_kernel(me, slots, got, out):
    for j in range(IMAGES):
        out[j] = got[slots[me[0] * IMAGES + j] // IMAGES]


def grad_kernel(steps, gate, spans, q, d_out, keys, values, dq, dkv, acc, keys_t):
    step = pl.program_id(1)
    rows = 2 * WIDTH

    @pl.when(step == 0)
    def _():
        keys_t[...] = keys[...].T

    def rows_of(ref):
        return jnp.concatenate([ref[:, :WIDTH], ref[:, WIDTH:]], axis=0)

    q_rows = rows_of(q)
    factor = jnp.tanh(gate[...])
    d_rows = (rows_of(d_out).astype(jnp.float32) * factor).astype(jnp.bfloat16)
    nt = (((1,), (1,)), ((), ()))
    scores = lax.dot_general(keys[...], q_rows, nt, preferred_element_type=jnp.float32)
    d_probs = lax.dot_general(values[...], d_rows, nt, preferred_element_type=jnp.float32)
    low = jnp.concatenate([spans[0:1, :], spans[0:1, :]], axis=1)
    high = jnp.concatenate([spans[1:2, :], spans[1:2, :]], axis=1)
    scores = scores.reshape(-1, IMAGES, 16, rows)
    d_probs = d_probs.reshape(-1, IMAGES, 16, rows)
    seen = [(low <= j) & (j < high) for j in range(IMAGES)]
    row_max = None
    for j in range(IMAGES):
        top = jnp.max(jnp.max(scores[:, j], axis=0), axis=0, keepdims=True)
        top = jnp.where(seen[j], top, LOW)
        row_max = top if row_max is None else jnp.maximum(row_max, top)
    row_max = row_max * (SCALE * LOG2E)
    terms = []
    total = 0.0
    dots = 0.0
    for j in range(IMAGES):
        term = jnp.exp2(scores[:, j] * (SCALE * LOG2E) - jnp.where(seen[j], row_max, -LOW))
        total += jnp.sum(jnp.sum(term, axis=0), axis=0, keepdims=True)
        dots += jnp.sum(jnp.sum(term * d_probs[:, j], axis=0), axis=0, keepdims=True)
        terms.append(term)
    inverse = 1.0 / total
    delta = dots * inverse
    low_probs = []
    d_scores = []
    for j in range(IMAGES):
        probs = terms[j] * inverse
        low_probs.append(probs.astype(jnp.bfloat16)[:, None])
        d_scores.append((probs * (d_probs[:, j] - delta)).astype(jnp.bfloat16)[:, None])
    low_probs = jnp.concatenate(low_probs, axis=1).reshape(-1, rows)
    d_scores = jnp.concatenate(d_scores, axis=1).reshape(-1, rows)
    d_keys = jnp.dot(d_scores, q_rows, preferred_element_type=jnp.float32)
    d_values = jnp.dot(low_probs, d_rows, preferred_element_type=jnp.float32)
    dq_t = jnp.dot(keys_t[...], d_scores, preferred_element_type=jnp.float32) * SCALE
    dq_rows = dq_t.T.astype(jnp.bfloat16)
    dq[:, :WIDTH] = dq_rows[:WIDTH]
    dq[:, WIDTH:] = dq_rows[WIDTH:]

    @pl.when(step == 0)
    def _():
        acc[:, :WIDTH] = d_keys
        acc[:, WIDTH:] = d_values

    @pl.when(step > 0)
    def _():
        acc[:, :WIDTH] += d_keys
        acc[:, WIDTH:] += d_values

    @pl.when(step == steps - 1)
    def _():
        dkv[:, :WIDTH] = (acc[:, :WIDTH] * SCALE).astype(jnp.bfloat16)
        dkv[:, WIDTH:] = acc[:, WIDTH:].astype(jnp.bfloat16)


def gradients(gate, spans, q, d_out, kv):
    tokens = q.shape[0]
    key_rows = kv.shape[0]
    steps = GROUP // 2
    block = lambda c, i: (0, c * steps + i)
    return pl.pallas_call(
        functools.partial(grad_kernel, steps),
        grid=(KV_HEADS, steps),
        in_specs=[
            pl.BlockSpec((1, 1), lambda c, i: (0, 0)),
            pl.BlockSpec((2, tokens), lambda c, i: (0, 0)),
            pl.BlockSpec((tokens, 2 * WIDTH), block),
            pl.BlockSpec((tokens, 2 * WIDTH), block),
            pl.BlockSpec((key_rows, WIDTH), lambda c, i: (0, c)),
            pl.BlockSpec((key_rows, WIDTH), lambda c, i: (0, KV_HEADS + c)),
        ],
        out_specs=[
            pl.BlockSpec((tokens, 2 * WIDTH), block),
            pl.BlockSpec((key_rows, 2 * WIDTH), lambda c, i: (0, c)),
        ],
        out_shape=[
            jax.ShapeDtypeStruct(q.shape, jnp.bfloat16),
            jax.ShapeDtypeStruct((key_rows, 2 * KEY_COLUMNS), jnp.bfloat16),
        ],
        scratch_shapes=[
            pltpu.VMEM((key_rows, 2 * WIDTH), jnp.float32),
            pltpu.VMEM((WIDTH, key_rows), jnp.bfloat16),
        ],
        compiler_params=pltpu.CompilerParams(vmem_limit_bytes=VMEM_LIMIT),
        name="gradients",
    )(gate, spans, q, d_out, kv, kv)


def sum_kernel(me, slots, got, out):
    out[...] = jnp.zeros_like(out)
    for j in range(IMAGES):
        total = got[0, j].astype(jnp.float32)
        for part in range(1, got.shape[0]):
            total += got[part, j].astype(jnp.float32)
        out[slots[me[0] * IMAGES + j] // IMAGES] = total.astype(jnp.bfloat16)


def place_kernel(docs, me, slots, got, out):
    for s in range(IMAGES):
        doc = 0
        for d in range(docs):
            for j in range(IMAGES):
                doc += jnp.where(slots[d * IMAGES + j] == me[0] * IMAGES + s, d, 0)
        rows = got[doc].astype(jnp.float32)
        for c in range(KV_HEADS):
            at = 2 * c * WIDTH
            out[s, :, c * WIDTH : (c + 1) * WIDTH] = rows[:, at : at + WIDTH]
            out[s, :, KEY_COLUMNS + c * WIDTH : KEY_COLUMNS + (c + 1) * WIDTH] = rows[
                :, at + WIDTH : at + 2 * WIDTH
            ]


def small(kernel, out_shape, name):
    return pl.pallas_call(
        kernel,
        in_specs=[
            pl.BlockSpec(memory_space=SMEM),
            pl.BlockSpec(memory_space=SMEM),
            pl.BlockSpec(memory_space=VMEM),
        ],
        out_specs=pl.BlockSpec(memory_space=VMEM),
        out_shape=out_shape,
        compiler_params=pltpu.CompilerParams(vmem_limit_bytes=VMEM_LIMIT),
        name=name,
    )


def shards(queries, image_kv, d_out, attn_gate, image_slots, spans):
    docs = lax.axis_size("doc")
    texts = lax.axis_size("ctx")
    me = lax.axis_index("doc").astype(jnp.int32)[None]
    images, rows, columns = image_kv.shape
    block = jax.ShapeDtypeStruct((docs, rows, columns), jnp.bfloat16)
    send = small(functools.partial(pack_kernel, docs), block, "pack")(me, image_slots, image_kv)
    got = lax.all_to_all(send, "doc", 0, 0)
    local = small(pick_kernel, jax.ShapeDtypeStruct(image_kv.shape, jnp.bfloat16), "pick")(
        me, image_slots, got
    )
    kv = lax.all_to_all(jnp.broadcast_to(local[None], (texts,) + local.shape), "ctx", 0, 0)
    d_queries, d_kv = gradients(
        attn_gate.reshape(1, 1),
        spans[0].T,
        queries[0],
        d_out[0],
        kv.reshape(texts * images * rows, columns),
    )
    parts = lax.all_to_all(d_kv.reshape(texts, images, rows, columns), "ctx", 0, 0)
    send = small(sum_kernel, block, "sum")(me, image_slots, parts)
    got = lax.all_to_all(send, "doc", 0, 0)
    d_image_kv = small(
        functools.partial(place_kernel, docs),
        jax.ShapeDtypeStruct(image_kv.shape, jnp.float32),
        "place",
    )(me, image_slots, got)
    return d_queries[None], d_image_kv


def solution(mesh):
    return jax.shard_map(
        shards,
        mesh=mesh,
        in_specs=(
            P("doc", "ctx", None),
            P("doc", "ctx", None),
            P("doc", "ctx", None),
            P(),
            P(),
            P("doc", "ctx", None),
        ),
        out_specs=(P("doc", "ctx", None), P("doc", "ctx", None)),
        check_vma=False,
    )
```

```python
import functools

import jax
import jax.numpy as jnp
from jax import lax
from jax.experimental import pallas as pl
from jax.experimental.pallas import tpu as pltpu
from jax.sharding import PartitionSpec as P

KV_HEADS = 4
WIDTH = 128
GROUP = 8
KEY_COLUMNS = 512
IMAGES = 4
LOW = -1e30
SCALE = WIDTH ** (-0.5)
LOG2E = 1.4426950408889634
LINE = 4
BLOCK_HEADS = 2
PAD = 16
VMEM_LIMIT = 48 * 1024 * 1024

SMEM = pltpu.MemorySpace.SMEM
VMEM = pltpu.MemorySpace.VMEM


def pack_kernel(docs, me, slots, kv, out):
    for d in range(docs):
        local = 0
        for j in range(IMAGES):
            s = slots[d * IMAGES + j]
            local += jnp.where(s // IMAGES == me[0], s % IMAGES, 0)
        out[d] = kv[local]


def pick_kernel(me, slots, got, out):
    for j in range(IMAGES):
        rows = got[slots[me[0] * IMAGES + j] // IMAGES]
        heads = [
            jnp.concatenate(
                [
                    rows[:, c * WIDTH : (c + 1) * WIDTH],
                    rows[:, KEY_COLUMNS + c * WIDTH : KEY_COLUMNS + (c + 1) * WIDTH],
                ],
                axis=1,
            )
            for c in range(KV_HEADS)
        ]
        along_z = me[0] % 2 == 0
        for y in range(LINE):
            for z in range(LINE):
                out[y * LINE + z, j] = jnp.where(along_z, heads[z], heads[y])


def payload_kernel(q, d_out, spans, out):
    tokens = q.shape[0]
    for c in range(KV_HEADS):
        columns = slice(c * GROUP * WIDTH, (c + 1) * GROUP * WIDTH)
        out[c, :tokens] = q[:, columns]
        out[c, tokens : 2 * tokens] = d_out[:, columns]
        out[c, 2 * tokens :] = jnp.zeros_like(out[c, 2 * tokens :])
        out[c, 2 * tokens : 2 * tokens + 2, :tokens] = spans[...].astype(jnp.bfloat16)


def softmax_gradients(scores, d_probs, seen):
    keys, rows = scores.shape
    scores = scores.reshape(-1, IMAGES, 16, rows)
    d_probs = d_probs.reshape(-1, IMAGES, 16, rows)
    row_max = None
    for j in range(IMAGES):
        top = jnp.max(jnp.max(scores[:, j], axis=0), axis=0, keepdims=True)
        top = jnp.where(seen[j], top, LOW)
        row_max = top if row_max is None else jnp.maximum(row_max, top)
    row_max = row_max * (SCALE * LOG2E)
    terms = []
    total = 0.0
    dots = 0.0
    for j in range(IMAGES):
        term = jnp.exp2(scores[:, j] * (SCALE * LOG2E) - jnp.where(seen[j], row_max, -LOW))
        total += jnp.sum(jnp.sum(term, axis=0), axis=0, keepdims=True)
        dots += jnp.sum(jnp.sum(term * d_probs[:, j], axis=0), axis=0, keepdims=True)
        terms.append(term)
    inverse = 1.0 / total
    delta = dots * inverse
    low_probs = []
    d_scores = []
    for j in range(IMAGES):
        probs = terms[j] * inverse
        low_probs.append(probs.astype(jnp.bfloat16)[:, None])
        d_scores.append((probs * (d_probs[:, j] - delta)).astype(jnp.bfloat16)[:, None])
    low_probs = jnp.concatenate(low_probs, axis=1).reshape(keys, rows)
    d_scores = jnp.concatenate(d_scores, axis=1).reshape(keys, rows)
    return low_probs, d_scores


def grad_kernel(gate, kv, piece, dq, dkv, keys_t, probs, d_scores, q_rows, d_rows, acc):
    step = pl.program_id(0)
    tokens = dq.shape[1]
    block = BLOCK_HEADS * tokens

    @pl.when(step == 0)
    def _():
        keys_t[...] = kv[:, :WIDTH].T
        acc[...] = jnp.zeros_like(acc)

    factor = jnp.tanh(gate[...])
    for h in range(GROUP):
        rows, columns = slice(h * tokens, (h + 1) * tokens), slice(h * WIDTH, (h + 1) * WIDTH)
        q_rows[rows] = piece[0, :tokens, columns]
        wide = piece[0, tokens : 2 * tokens, columns].astype(jnp.float32)
        d_rows[rows] = (wide * factor).astype(jnp.bfloat16)
    low = piece[0, 2 * tokens : 2 * tokens + 1, :tokens].astype(jnp.float32)
    high = piece[0, 2 * tokens + 1 : 2 * tokens + 2, :tokens].astype(jnp.float32)
    low = jnp.concatenate([low] * BLOCK_HEADS, axis=1)
    high = jnp.concatenate([high] * BLOCK_HEADS, axis=1)
    seen = [(low <= j) & (j < high) for j in range(IMAGES)]
    transposed = (((1,), (1,)), ((), ()))
    for at in range(0, GROUP * tokens, block):
        rows = slice(at, at + block)
        scores = lax.dot_general(
            kv[:, :WIDTH], q_rows[rows], transposed, preferred_element_type=jnp.float32
        )
        d_probs = lax.dot_general(
            kv[:, WIDTH:], d_rows[rows], transposed, preferred_element_type=jnp.float32
        )
        probs[:, rows], d_scores[:, rows] = softmax_gradients(scores, d_probs, seen)
    acc[:, :WIDTH] += jnp.dot(d_scores[...], q_rows[...], preferred_element_type=jnp.float32)
    acc[:, WIDTH:] += jnp.dot(probs[...], d_rows[...], preferred_element_type=jnp.float32)
    dq_t = jnp.dot(keys_t[...], d_scores[...], preferred_element_type=jnp.float32) * SCALE
    dq_rows = dq_t.T.astype(jnp.bfloat16)
    for h in range(GROUP):
        dq[0, :, h * WIDTH : (h + 1) * WIDTH] = dq_rows[h * tokens : (h + 1) * tokens]

    @pl.when(step == LINE - 1)
    def _():
        dkv[:, :WIDTH] = (acc[:, :WIDTH] * SCALE).astype(jnp.bfloat16)
        dkv[:, WIDTH:] = acc[:, WIDTH:].astype(jnp.bfloat16)


def gradients(gate, kv, pieces):
    key_rows = kv.shape[0]
    tokens = (pieces.shape[1] - PAD) // 2
    width = pieces.shape[2]
    rows = GROUP * tokens
    return pl.pallas_call(
        grad_kernel,
        grid=(LINE,),
        in_specs=[
            pl.BlockSpec((1, 1), lambda i: (0, 0)),
            pl.BlockSpec(kv.shape, lambda i: (0, 0)),
            pl.BlockSpec((1,) + pieces.shape[1:], lambda i: (i, 0, 0)),
        ],
        out_specs=[
            pl.BlockSpec((1, tokens, width), lambda i: (i, 0, 0)),
            pl.BlockSpec(kv.shape, lambda i: (0, 0)),
        ],
        out_shape=[
            jax.ShapeDtypeStruct((LINE, tokens, width), jnp.bfloat16),
            jax.ShapeDtypeStruct(kv.shape, jnp.bfloat16),
        ],
        scratch_shapes=[
            pltpu.VMEM((WIDTH, key_rows), jnp.bfloat16),
            pltpu.VMEM((key_rows, rows), jnp.bfloat16),
            pltpu.VMEM((key_rows, rows), jnp.bfloat16),
            pltpu.VMEM((rows, WIDTH), jnp.bfloat16),
            pltpu.VMEM((rows, WIDTH), jnp.bfloat16),
            pltpu.VMEM(kv.shape, jnp.float32),
        ],
        compiler_params=pltpu.CompilerParams(vmem_limit_bytes=VMEM_LIMIT),
        cost_estimate=pl.CostEstimate(
            flops=10 * LINE * rows * key_rows * WIDTH,
            bytes_accessed=4 * 1024 * 1024,
            transcendentals=LINE * rows * key_rows,
        ),
        name="gradients",
    )(gate, kv, pieces)


def sum_kernel(me, slots, got, out):
    out[...] = jnp.zeros_like(out)
    along_z = me[0] % 2 == 0
    for j in range(IMAGES):
        owner = slots[me[0] * IMAGES + j] // IMAGES
        for c in range(KV_HEADS):
            total = 0.0
            for line in range(LINE):
                at = jnp.where(along_z, line * LINE + c, c * LINE + line)
                total += got[at, j].astype(jnp.float32)
            out[owner, :, c * WIDTH : (c + 1) * WIDTH] = total[:, :WIDTH].astype(jnp.bfloat16)
            out[owner, :, KEY_COLUMNS + c * WIDTH : KEY_COLUMNS + (c + 1) * WIDTH] = total[
                :, WIDTH:
            ].astype(jnp.bfloat16)


def place_kernel(docs, me, slots, got, out):
    for s in range(IMAGES):
        doc = 0
        for d in range(docs):
            for j in range(IMAGES):
                doc += jnp.where(slots[d * IMAGES + j] == me[0] * IMAGES + s, d, 0)
        out[s] = got[doc].astype(jnp.float32)


def small(kernel, out_shape, name):
    return pl.pallas_call(
        kernel,
        in_specs=[
            pl.BlockSpec(memory_space=SMEM),
            pl.BlockSpec(memory_space=SMEM),
            pl.BlockSpec(memory_space=VMEM),
        ],
        out_specs=pl.BlockSpec(memory_space=VMEM),
        out_shape=out_shape,
        compiler_params=pltpu.CompilerParams(vmem_limit_bytes=VMEM_LIMIT),
        name=name,
    )


def line_groups(docs):
    groups = []
    for d in range(docs):
        for a in range(LINE):
            if d % 2 == 0:
                groups.append([d * LINE * LINE + a * LINE + b for b in range(LINE)])
            else:
                groups.append([d * LINE * LINE + b * LINE + a for b in range(LINE)])
    return groups


def shards(queries, image_kv, d_out, attn_gate, image_slots, spans):
    docs = lax.axis_size("doc")
    texts = lax.axis_size("ctx")
    me = lax.axis_index("doc").astype(jnp.int32)[None]
    images, rows, columns = image_kv.shape
    tokens, width = queries.shape[1] , queries.shape[2] // KV_HEADS
    groups = line_groups(docs)
    both = ("doc", "ctx")
    payload = pl.pallas_call(
        payload_kernel,
        out_shape=jax.ShapeDtypeStruct((LINE, 2 * tokens + PAD, width), jnp.bfloat16),
        compiler_params=pltpu.CompilerParams(vmem_limit_bytes=VMEM_LIMIT),
        name="payload",
    )(queries[0], d_out[0], spans[0].T)
    pieces = lax.all_to_all(payload, both, 0, 0, axis_index_groups=groups)
    block = jax.ShapeDtypeStruct((docs, rows, columns), jnp.bfloat16)
    send = small(functools.partial(pack_kernel, docs), block, "pack")(me, image_slots, image_kv)
    got = lax.all_to_all(send, "doc", 0, 0)
    one_head = jax.ShapeDtypeStruct((texts, images, rows, 2 * WIDTH), jnp.bfloat16)
    send = small(pick_kernel, one_head, "pick")(me, image_slots, got)
    kv = lax.all_to_all(send, "ctx", 0, 0).reshape(texts * images * rows, 2 * WIDTH)
    dq, dkv = gradients(attn_gate.reshape(1, 1), kv, pieces)
    parts = lax.all_to_all(dkv.reshape(texts, images, rows, 2 * WIDTH), "ctx", 0, 0)
    back = lax.all_to_all(dq, both, 0, 0, axis_index_groups=groups)
    d_queries = back.transpose(1, 0, 2).reshape(1, tokens, LINE * width)
    send = small(sum_kernel, block, "sum")(me, image_slots, parts)
    got = lax.all_to_all(send, "doc", 0, 0)
    d_image_kv = small(
        functools.partial(place_kernel, docs),
        jax.ShapeDtypeStruct(image_kv.shape, jnp.float32),
        "place",
    )(me, image_slots, got)
    return d_queries, d_image_kv


def solution(mesh):
    return jax.shard_map(
        shards,
        mesh=mesh,
        in_specs=(
            P("doc", "ctx", None),
            P("doc", "ctx", None),
            P("doc", "ctx", None),
            P(),
            P(),
            P("doc", "ctx", None),
        ),
        out_specs=(P("doc", "ctx", None), P("doc", "ctx", None)),
        check_vma=False,
    )
```

```python
import functools

import jax
import jax.numpy as jnp
from jax import lax
from jax.experimental import pallas as pl
from jax.experimental.pallas import tpu as pltpu
from jax.sharding import PartitionSpec as P

KV_HEADS = 4
WIDTH = 128
GROUP = 8
KEY_COLUMNS = 512
IMAGES = 4
LOW = -1e30
SCALE = WIDTH ** (-0.5)
LOG2E = 1.4426950408889634
LINE = 4
BLOCK_HEADS = 2
PAD = 16
VMEM_LIMIT = 48 * 1024 * 1024

SMEM = pltpu.MemorySpace.SMEM
VMEM = pltpu.MemorySpace.VMEM


def pack_kernel(docs, me, slots, kv, out):
    for d in range(docs):
        local = 0
        for j in range(IMAGES):
            s = slots[d * IMAGES + j]
            local += jnp.where(s // IMAGES == me[0], s % IMAGES, 0)
        out[d] = kv[local]


def pick_kernel(me, slots, got, out):
    for j in range(IMAGES):
        rows = got[slots[me[0] * IMAGES + j] // IMAGES]
        heads = [
            jnp.concatenate(
                [
                    rows[:, c * WIDTH : (c + 1) * WIDTH],
                    rows[:, KEY_COLUMNS + c * WIDTH : KEY_COLUMNS + (c + 1) * WIDTH],
                ],
                axis=1,
            )
            for c in range(KV_HEADS)
        ]
        along_z = me[0] % 2 == 0
        for y in range(LINE):
            for z in range(LINE):
                out[y * LINE + z, j] = jnp.where(along_z, heads[z], heads[y])


def payload_kernel(me, q, d_out, spans, *outs):
    tokens = q.shape[0]
    width = q.shape[1] // KV_HEADS
    for k, out in enumerate(outs):
        columns = pl.ds(pl.multiple_of(lax.rem(me[1] + k, LINE) * width, WIDTH), width)
        out[:tokens] = q[:, columns]
        out[tokens : 2 * tokens] = d_out[:, columns]
        out[2 * tokens :] = jnp.zeros_like(out[2 * tokens :])
        out[2 * tokens : 2 * tokens + 2, :tokens] = spans[...].astype(jnp.bfloat16)


def merge_kernel(me, *refs):
    *parts, out = refs
    width = out.shape[1] // KV_HEADS
    for k, part in enumerate(parts):
        columns = pl.ds(pl.multiple_of(lax.rem(me[1] + k, LINE) * width, WIDTH), width)
        out[:, columns] = part[...]


def softmax_gradients(scores, d_probs, seen):
    keys, rows = scores.shape
    scores = scores.reshape(-1, IMAGES, 16, rows)
    d_probs = d_probs.reshape(-1, IMAGES, 16, rows)
    row_max = None
    for j in range(IMAGES):
        top = jnp.max(jnp.max(scores[:, j], axis=0), axis=0, keepdims=True)
        top = jnp.where(seen[j], top, LOW)
        row_max = top if row_max is None else jnp.maximum(row_max, top)
    row_max = row_max * (SCALE * LOG2E)
    terms = []
    total = 0.0
    dots = 0.0
    for j in range(IMAGES):
        term = jnp.exp2(scores[:, j] * (SCALE * LOG2E) - jnp.where(seen[j], row_max, -LOW))
        total += jnp.sum(jnp.sum(term, axis=0), axis=0, keepdims=True)
        dots += jnp.sum(jnp.sum(term * d_probs[:, j], axis=0), axis=0, keepdims=True)
        terms.append(term)
    inverse = 1.0 / total
    delta = dots * inverse
    low_probs = []
    d_scores = []
    for j in range(IMAGES):
        probs = terms[j] * inverse
        low_probs.append(probs.astype(jnp.bfloat16)[:, None])
        d_scores.append((probs * (d_probs[:, j] - delta)).astype(jnp.bfloat16)[:, None])
    low_probs = jnp.concatenate(low_probs, axis=1).reshape(keys, rows)
    d_scores = jnp.concatenate(d_scores, axis=1).reshape(keys, rows)
    return low_probs, d_scores


def grad_kernel(gate, kv, *refs):
    pieces, dqs, dkv = refs[:LINE], refs[LINE : 2 * LINE], refs[2 * LINE]
    keys_t, probs, d_scores, q_rows, d_rows, spans, acc = refs[2 * LINE + 1 :]
    step = pl.program_id(0)
    tokens = dqs[0].shape[0]
    block = BLOCK_HEADS * tokens

    @pl.when(step == 0)
    def _():
        keys_t[...] = kv[:, :WIDTH].T
        acc[...] = jnp.zeros_like(acc)

    for k, piece in enumerate(pieces):

        @pl.when(step == k)
        def _(piece=piece):
            factor = jnp.tanh(gate[...])
            for h in range(GROUP):
                rows, columns = slice(h * tokens, (h + 1) * tokens), slice(h * WIDTH, (h + 1) * WIDTH)
                q_rows[rows] = piece[:tokens, columns]
                wide = piece[tokens : 2 * tokens, columns].astype(jnp.float32)
                d_rows[rows] = (wide * factor).astype(jnp.bfloat16)
            spans[...] = piece[2 * tokens :, :tokens].astype(jnp.float32)

    low = jnp.concatenate([spans[0:1]] * BLOCK_HEADS, axis=1)
    high = jnp.concatenate([spans[1:2]] * BLOCK_HEADS, axis=1)
    seen = [(low <= j) & (j < high) for j in range(IMAGES)]
    transposed = (((1,), (1,)), ((), ()))
    for at in range(0, GROUP * tokens, block):
        rows = slice(at, at + block)
        scores = lax.dot_general(
            kv[:, :WIDTH], q_rows[rows], transposed, preferred_element_type=jnp.float32
        )
        d_probs = lax.dot_general(
            kv[:, WIDTH:], d_rows[rows], transposed, preferred_element_type=jnp.float32
        )
        probs[:, rows], d_scores[:, rows] = softmax_gradients(scores, d_probs, seen)
    acc[:, :WIDTH] += jnp.dot(d_scores[...], q_rows[...], preferred_element_type=jnp.float32)
    acc[:, WIDTH:] += jnp.dot(probs[...], d_rows[...], preferred_element_type=jnp.float32)
    dq_t = jnp.dot(keys_t[...], d_scores[...], preferred_element_type=jnp.float32) * SCALE
    dq_rows = dq_t.T.astype(jnp.bfloat16)
    for k, dq in enumerate(dqs):

        @pl.when(step == k)
        def _(dq=dq):
            for h in range(GROUP):
                dq[:, h * WIDTH : (h + 1) * WIDTH] = dq_rows[h * tokens : (h + 1) * tokens]

    @pl.when(step == LINE - 1)
    def _():
        dkv[:, :WIDTH] = (acc[:, :WIDTH] * SCALE).astype(jnp.bfloat16)
        dkv[:, WIDTH:] = acc[:, WIDTH:].astype(jnp.bfloat16)


def gradients(gate, kv, pieces):
    key_rows = kv.shape[0]
    tokens = (pieces[0].shape[0] - PAD) // 2
    width = pieces[0].shape[1]
    rows = GROUP * tokens
    whole = lambda shape: pl.BlockSpec(shape, lambda i: (0, 0))
    return pl.pallas_call(
        grad_kernel,
        grid=(LINE,),
        in_specs=[whole((1, 1)), whole(kv.shape)] + [whole(p.shape) for p in pieces],
        out_specs=[whole((tokens, width))] * LINE + [whole(kv.shape)],
        out_shape=[jax.ShapeDtypeStruct((tokens, width), jnp.bfloat16)] * LINE
        + [jax.ShapeDtypeStruct(kv.shape, jnp.bfloat16)],
        scratch_shapes=[
            pltpu.VMEM((WIDTH, key_rows), jnp.bfloat16),
            pltpu.VMEM((key_rows, rows), jnp.bfloat16),
            pltpu.VMEM((key_rows, rows), jnp.bfloat16),
            pltpu.VMEM((rows, WIDTH), jnp.bfloat16),
            pltpu.VMEM((rows, WIDTH), jnp.bfloat16),
            pltpu.VMEM((PAD, tokens), jnp.float32),
            pltpu.VMEM(kv.shape, jnp.float32),
        ],
        compiler_params=pltpu.CompilerParams(vmem_limit_bytes=VMEM_LIMIT),
        cost_estimate=pl.CostEstimate(
            flops=10 * LINE * rows * key_rows * WIDTH,
            bytes_accessed=4 * 1024 * 1024,
            transcendentals=LINE * rows * key_rows,
        ),
        name="gradients",
    )(gate, kv, *pieces)


def sum_kernel(me, slots, got, out):
    out[...] = jnp.zeros_like(out)
    along_z = me[0] % 2 == 0
    for j in range(IMAGES):
        owner = slots[me[0] * IMAGES + j] // IMAGES
        for c in range(KV_HEADS):
            total = 0.0
            for line in range(LINE):
                at = jnp.where(along_z, line * LINE + c, c * LINE + line)
                total += got[at, j].astype(jnp.float32)
            out[owner, :, c * WIDTH : (c + 1) * WIDTH] = total[:, :WIDTH].astype(jnp.bfloat16)
            out[owner, :, KEY_COLUMNS + c * WIDTH : KEY_COLUMNS + (c + 1) * WIDTH] = total[
                :, WIDTH:
            ].astype(jnp.bfloat16)


def place_kernel(docs, me, slots, got, out):
    for s in range(IMAGES):
        doc = 0
        for d in range(docs):
            for j in range(IMAGES):
                doc += jnp.where(slots[d * IMAGES + j] == me[0] * IMAGES + s, d, 0)
        out[s] = got[doc].astype(jnp.float32)


def small(kernel, out_shape, name):
    return pl.pallas_call(
        kernel,
        in_specs=[
            pl.BlockSpec(memory_space=SMEM),
            pl.BlockSpec(memory_space=SMEM),
            pl.BlockSpec(memory_space=VMEM),
        ],
        out_specs=pl.BlockSpec(memory_space=VMEM),
        out_shape=out_shape,
        compiler_params=pltpu.CompilerParams(vmem_limit_bytes=VMEM_LIMIT),
        name=name,
    )


def shift(docs, k):
    pairs = []
    for d in range(docs):
        for a in range(LINE):
            for b in range(LINE):
                to = (b + k) % LINE
                ends = (a * LINE + b, a * LINE + to) if d % 2 == 0 else (b * LINE + a, to * LINE + a)
                pairs.append((d * LINE * LINE + ends[0], d * LINE * LINE + ends[1]))
    return pairs


def shards(queries, image_kv, d_out, attn_gate, image_slots, spans):
    docs = lax.axis_size("doc")
    texts = lax.axis_size("ctx")
    doc = lax.axis_index("doc").astype(jnp.int32)
    text = lax.axis_index("ctx").astype(jnp.int32)
    me = jnp.stack([doc, jnp.where(doc % 2 == 0, text % LINE, text // LINE)])
    images, rows, columns = image_kv.shape
    tokens, width = queries.shape[1], queries.shape[2] // KV_HEADS
    both = ("doc", "ctx")
    params = pltpu.CompilerParams(vmem_limit_bytes=VMEM_LIMIT)
    pieces = pl.pallas_call(
        payload_kernel,
        in_specs=[pl.BlockSpec(memory_space=SMEM)] + [pl.BlockSpec(memory_space=VMEM)] * 3,
        out_specs=[pl.BlockSpec(memory_space=VMEM)] * LINE,
        out_shape=[jax.ShapeDtypeStruct((2 * tokens + PAD, width), jnp.bfloat16)] * LINE,
        compiler_params=params,
        name="payload",
    )(me, queries[0], d_out[0], spans[0].T)
    pieces = [pieces[0]] + [lax.ppermute(pieces[k], both, shift(docs, k)) for k in range(1, LINE)]
    block = jax.ShapeDtypeStruct((docs, rows, columns), jnp.bfloat16)
    send = small(functools.partial(pack_kernel, docs), block, "pack")(me, image_slots, image_kv)
    got = lax.all_to_all(send, "doc", 0, 0)
    one_head = jax.ShapeDtypeStruct((texts, images, rows, 2 * WIDTH), jnp.bfloat16)
    send = small(pick_kernel, one_head, "pick")(me, image_slots, got)
    kv = lax.all_to_all(send, "ctx", 0, 0).reshape(texts * images * rows, 2 * WIDTH)
    *dqs, dkv = gradients(attn_gate.reshape(1, 1), kv, pieces)
    dqs = [dqs[0]] + [lax.ppermute(dqs[k], both, shift(docs, -k)) for k in range(1, LINE)]
    parts = lax.all_to_all(dkv.reshape(texts, images, rows, 2 * WIDTH), "ctx", 0, 0)
    send = small(sum_kernel, block, "sum")(me, image_slots, parts)
    got = lax.all_to_all(send, "doc", 0, 0)
    d_image_kv = small(
        functools.partial(place_kernel, docs),
        jax.ShapeDtypeStruct(image_kv.shape, jnp.float32),
        "place",
    )(me, image_slots, got)
    d_queries = pl.pallas_call(
        merge_kernel,
        in_specs=[pl.BlockSpec(memory_space=SMEM)] + [pl.BlockSpec(memory_space=VMEM)] * LINE,
        out_specs=pl.BlockSpec(memory_space=VMEM),
        out_shape=jax.ShapeDtypeStruct(queries.shape[1:], jnp.bfloat16),
        compiler_params=params,
        name="merge",
    )(me, *dqs)
    return d_queries[None], d_image_kv


def solution(mesh):
    return jax.shard_map(
        shards,
        mesh=mesh,
        in_specs=(
            P("doc", "ctx", None),
            P("doc", "ctx", None),
            P("doc", "ctx", None),
            P(),
            P(),
            P("doc", "ctx", None),
        ),
        out_specs=(P("doc", "ctx", None), P("doc", "ctx", None)),
        check_vma=False,
    )
```

```python
import functools

import jax
import jax.numpy as jnp
from jax import lax
from jax.experimental import pallas as pl
from jax.experimental.pallas import tpu as pltpu
from jax.sharding import PartitionSpec as P

KV_HEADS = 4
WIDTH = 128
GROUP = 8
KEY_COLUMNS = 512
IMAGES = 4
LOW = -1e30
SCALE = WIDTH ** (-0.5)
LOG2E = 1.4426950408889634
LINE = 4
BLOCK_HEADS = 2
PAD = 16
VMEM_LIMIT = 48 * 1024 * 1024

SMEM = pltpu.MemorySpace.SMEM
VMEM = pltpu.MemorySpace.VMEM


def pack_kernel(docs, me, slots_any, kv, out, slots, sems):
    fetch = pltpu.make_async_copy(slots_any, slots, sems.at[docs])
    fetch.start()
    fetch.wait()
    copies = []
    for d in range(docs):
        local = 0
        for j in range(IMAGES):
            s = slots[d * IMAGES + j]
            local += jnp.where(s // IMAGES == me[0], s % IMAGES, 0)
        copies.append(pltpu.make_async_copy(kv.at[local], out.at[d], sems.at[d]))
        copies[-1].start()
    for copy in copies:
        copy.wait()


def pick_kernel(me, slots, got, out, heads, sems):
    for j in range(IMAGES):
        owner = slots[me[0] * IMAGES + j] // IMAGES
        for c in range(KV_HEADS):
            columns = slice(c * WIDTH, (c + 1) * WIDTH)
            heads[c, j, :, :WIDTH] = got[owner, :, columns]
            columns = slice(KEY_COLUMNS + c * WIDTH, KEY_COLUMNS + (c + 1) * WIDTH)
            heads[c, j, :, WIDTH:] = got[owner, :, columns]
    along_z = me[0] % 2 == 0
    copies = []
    for y in range(LINE):
        for z in range(LINE):
            head = jnp.where(along_z, z, y)
            at = y * LINE + z
            copies.append(pltpu.make_async_copy(heads.at[head], out.at[at], sems.at[at]))
            copies[-1].start()
    for copy in copies:
        copy.wait()


def payload_kernel(me, q, d_out, spans, *refs):
    outs, wide, sems = refs[:LINE], refs[LINE], refs[LINE + 1]
    tokens = q.shape[0]
    width = q.shape[1] // KV_HEADS
    copies = []
    for k in [1, 2, 3, 0]:
        columns = pl.ds(pl.multiple_of(lax.rem(me[1] + k, LINE) * width, WIDTH), width)
        copies += [
            pltpu.make_async_copy(q.at[:, columns], outs[k].at[:tokens], sems.at[3 * k]),
            pltpu.make_async_copy(
                d_out.at[:, columns], outs[k].at[tokens : 2 * tokens], sems.at[3 * k + 1]
            ),
        ]
    for copy in copies:
        copy.start()
    wide[...] = jnp.zeros_like(wide)
    wide[:2, :tokens] = spans[...].astype(jnp.bfloat16)
    for k in range(LINE):
        copies.append(pltpu.make_async_copy(wide, outs[k].at[2 * tokens :], sems.at[3 * k + 2]))
        copies[-1].start()
    for copy in copies:
        copy.wait()


def merge_kernel(me, *refs):
    parts, out, sems = refs[:LINE], refs[LINE], refs[LINE + 1]
    width = out.shape[1] // KV_HEADS
    copies = []
    for k, part in enumerate(parts):
        columns = pl.ds(pl.multiple_of(lax.rem(me[1] + k, LINE) * width, WIDTH), width)
        copies.append(pltpu.make_async_copy(part, out.at[:, columns], sems.at[k]))
        copies[-1].start()
    for copy in copies:
        copy.wait()


def softmax_gradients(scores, d_probs, seen):
    keys, rows = scores.shape
    scores = scores.reshape(-1, IMAGES, 16, rows)
    d_probs = d_probs.reshape(-1, IMAGES, 16, rows)
    row_max = None
    for j in range(IMAGES):
        top = jnp.max(jnp.max(scores[:, j], axis=0), axis=0, keepdims=True)
        top = jnp.where(seen[j], top, LOW)
        row_max = top if row_max is None else jnp.maximum(row_max, top)
    row_max = row_max * (SCALE * LOG2E)
    terms = []
    total = 0.0
    dots = 0.0
    for j in range(IMAGES):
        term = jnp.exp2(scores[:, j] * (SCALE * LOG2E) - jnp.where(seen[j], row_max, -LOW))
        total += jnp.sum(jnp.sum(term, axis=0), axis=0, keepdims=True)
        dots += jnp.sum(jnp.sum(term * d_probs[:, j], axis=0), axis=0, keepdims=True)
        terms.append(term)
    inverse = 1.0 / total
    delta = dots * inverse
    low_probs = []
    d_scores = []
    for j in range(IMAGES):
        probs = terms[j] * inverse
        low_probs.append(probs.astype(jnp.bfloat16)[:, None])
        d_scores.append((probs * (d_probs[:, j] - delta)).astype(jnp.bfloat16)[:, None])
    low_probs = jnp.concatenate(low_probs, axis=1).reshape(keys, rows)
    d_scores = jnp.concatenate(d_scores, axis=1).reshape(keys, rows)
    return low_probs, d_scores


def grad_kernel(gate, kv, *refs):
    pieces, dqs, dkv = refs[:LINE], refs[LINE : 2 * LINE], refs[2 * LINE]
    keys_t, probs, d_scores, q_rows, d_rows, spans, acc = refs[2 * LINE + 1 :]
    step = pl.program_id(0)
    tokens = dqs[0].shape[0]
    block = BLOCK_HEADS * tokens

    @pl.when(step == 0)
    def _():
        keys_t[...] = kv[:, :WIDTH].T
        acc[...] = jnp.zeros_like(acc)

    for k, piece in enumerate(pieces):

        @pl.when(step == k)
        def _(piece=piece):
            factor = jnp.tanh(gate[...])
            for h in range(GROUP):
                rows, columns = slice(h * tokens, (h + 1) * tokens), slice(h * WIDTH, (h + 1) * WIDTH)
                q_rows[rows] = piece[:tokens, columns]
                wide = piece[tokens : 2 * tokens, columns].astype(jnp.float32)
                d_rows[rows] = (wide * factor).astype(jnp.bfloat16)
            spans[...] = piece[2 * tokens :, :tokens].astype(jnp.float32)

    low = jnp.concatenate([spans[0:1]] * BLOCK_HEADS, axis=1)
    high = jnp.concatenate([spans[1:2]] * BLOCK_HEADS, axis=1)
    seen = [(low <= j) & (j < high) for j in range(IMAGES)]
    transposed = (((1,), (1,)), ((), ()))
    for at in range(0, GROUP * tokens, block):
        rows = slice(at, at + block)
        scores = lax.dot_general(
            kv[:, :WIDTH], q_rows[rows], transposed, preferred_element_type=jnp.float32
        )
        d_probs = lax.dot_general(
            kv[:, WIDTH:], d_rows[rows], transposed, preferred_element_type=jnp.float32
        )
        probs[:, rows], d_scores[:, rows] = softmax_gradients(scores, d_probs, seen)
    acc[:, :WIDTH] += jnp.dot(d_scores[...], q_rows[...], preferred_element_type=jnp.float32)
    acc[:, WIDTH:] += jnp.dot(probs[...], d_rows[...], preferred_element_type=jnp.float32)
    dq_t = jnp.dot(keys_t[...], d_scores[...], preferred_element_type=jnp.float32) * SCALE
    dq_rows = dq_t.T.astype(jnp.bfloat16)
    for k, dq in enumerate(dqs):

        @pl.when(step == k)
        def _(dq=dq):
            for h in range(GROUP):
                dq[:, h * WIDTH : (h + 1) * WIDTH] = dq_rows[h * tokens : (h + 1) * tokens]

    @pl.when(step == LINE - 1)
    def _():
        dkv[:, :WIDTH] = (acc[:, :WIDTH] * SCALE).astype(jnp.bfloat16)
        dkv[:, WIDTH:] = acc[:, WIDTH:].astype(jnp.bfloat16)


def gradients(gate, kv, pieces):
    key_rows = kv.shape[0]
    tokens = (pieces[0].shape[0] - PAD) // 2
    width = pieces[0].shape[1]
    rows = GROUP * tokens
    whole = lambda shape: pl.BlockSpec(shape, lambda i: (0, 0))
    return pl.pallas_call(
        grad_kernel,
        grid=(LINE,),
        in_specs=[whole((1, 1)), whole(kv.shape)] + [whole(p.shape) for p in pieces],
        out_specs=[whole((tokens, width))] * LINE + [whole(kv.shape)],
        out_shape=[jax.ShapeDtypeStruct((tokens, width), jnp.bfloat16)] * LINE
        + [jax.ShapeDtypeStruct(kv.shape, jnp.bfloat16)],
        scratch_shapes=[
            pltpu.VMEM((WIDTH, key_rows), jnp.bfloat16),
            pltpu.VMEM((key_rows, rows), jnp.bfloat16),
            pltpu.VMEM((key_rows, rows), jnp.bfloat16),
            pltpu.VMEM((rows, WIDTH), jnp.bfloat16),
            pltpu.VMEM((rows, WIDTH), jnp.bfloat16),
            pltpu.VMEM((PAD, tokens), jnp.float32),
            pltpu.VMEM(kv.shape, jnp.float32),
        ],
        compiler_params=pltpu.CompilerParams(vmem_limit_bytes=VMEM_LIMIT),
        cost_estimate=pl.CostEstimate(
            flops=10 * LINE * rows * key_rows * WIDTH,
            bytes_accessed=4 * 1024 * 1024,
            transcendentals=LINE * rows * key_rows,
        ),
        name="gradients",
    )(gate, kv, *pieces)


def sum_kernel(me, slots, got, out):
    out[...] = jnp.zeros_like(out)
    along_z = me[0] % 2 == 0
    for j in range(IMAGES):
        owner = slots[me[0] * IMAGES + j] // IMAGES
        for c in range(KV_HEADS):
            total = 0.0
            for line in range(LINE):
                at = jnp.where(along_z, line * LINE + c, c * LINE + line)
                total += got[at, j].astype(jnp.float32)
            out[owner, :, c * WIDTH : (c + 1) * WIDTH] = total[:, :WIDTH].astype(jnp.bfloat16)
            out[owner, :, KEY_COLUMNS + c * WIDTH : KEY_COLUMNS + (c + 1) * WIDTH] = total[
                :, WIDTH:
            ].astype(jnp.bfloat16)


def place_kernel(docs, me, slots, got, out):
    for s in range(IMAGES):
        doc = 0
        for d in range(docs):
            for j in range(IMAGES):
                doc += jnp.where(slots[d * IMAGES + j] == me[0] * IMAGES + s, d, 0)
        out[s] = got[doc].astype(jnp.float32)


def small(kernel, out_shape, name):
    return pl.pallas_call(
        kernel,
        in_specs=[
            pl.BlockSpec(memory_space=SMEM),
            pl.BlockSpec(memory_space=SMEM),
            pl.BlockSpec(memory_space=VMEM),
        ],
        out_specs=pl.BlockSpec(memory_space=VMEM),
        out_shape=out_shape,
        compiler_params=pltpu.CompilerParams(vmem_limit_bytes=VMEM_LIMIT),
        name=name,
    )


def shift(docs, k):
    pairs = []
    for d in range(docs):
        for a in range(LINE):
            for b in range(LINE):
                to = (b + k) % LINE
                ends = (a * LINE + b, a * LINE + to) if d % 2 == 0 else (b * LINE + a, to * LINE + a)
                pairs.append((d * LINE * LINE + ends[0], d * LINE * LINE + ends[1]))
    return pairs


def shards(queries, image_kv, d_out, attn_gate, image_slots, spans):
    docs = lax.axis_size("doc")
    texts = lax.axis_size("ctx")
    doc = lax.axis_index("doc").astype(jnp.int32)
    text = lax.axis_index("ctx").astype(jnp.int32)
    me = jnp.stack([doc, jnp.where(doc % 2 == 0, text % LINE, text // LINE)])
    images, rows, columns = image_kv.shape
    tokens, width = queries.shape[1], queries.shape[2] // KV_HEADS
    both = ("doc", "ctx")
    anywhere = pl.BlockSpec(memory_space=pl.ANY)
    in_smem = pl.BlockSpec(memory_space=SMEM)
    block = jax.ShapeDtypeStruct((docs, rows, columns), jnp.bfloat16)
    send = pl.pallas_call(
        functools.partial(pack_kernel, docs),
        in_specs=[in_smem, anywhere, anywhere],
        out_specs=anywhere,
        out_shape=block,
        scratch_shapes=[
            pltpu.SMEM(image_slots.shape, jnp.int32),
            pltpu.SemaphoreType.DMA((docs + 1,)),
        ],
        name="pack",
    )(me, image_slots, image_kv)
    got = lax.all_to_all(send, "doc", 0, 0)
    pieces = pl.pallas_call(
        payload_kernel,
        in_specs=[in_smem, anywhere, anywhere, pl.BlockSpec(memory_space=VMEM)],
        out_specs=[anywhere] * LINE,
        out_shape=[jax.ShapeDtypeStruct((2 * tokens + PAD, width), jnp.bfloat16)] * LINE,
        scratch_shapes=[
            pltpu.VMEM((PAD, width), jnp.bfloat16),
            pltpu.SemaphoreType.DMA((3 * LINE,)),
        ],
        name="payload",
    )(me, queries[0], d_out[0], spans[0].T)
    pieces = [pieces[0]] + [lax.ppermute(pieces[k], both, shift(docs, k)) for k in range(1, LINE)]
    send = pl.pallas_call(
        pick_kernel,
        in_specs=[in_smem, in_smem, pl.BlockSpec(memory_space=VMEM)],
        out_specs=anywhere,
        out_shape=jax.ShapeDtypeStruct((texts, images, rows, 2 * WIDTH), jnp.bfloat16),
        scratch_shapes=[
            pltpu.VMEM((KV_HEADS, images, rows, 2 * WIDTH), jnp.bfloat16),
            pltpu.SemaphoreType.DMA((texts,)),
        ],
        name="pick",
    )(me, image_slots, got)
    kv = lax.all_to_all(send, "ctx", 0, 0).reshape(texts * images * rows, 2 * WIDTH)
    *dqs, dkv = gradients(attn_gate.reshape(1, 1), kv, pieces)
    dqs = [dqs[0]] + [lax.ppermute(dqs[k], both, shift(docs, -k)) for k in range(1, LINE)]
    parts = lax.all_to_all(dkv.reshape(texts, images, rows, 2 * WIDTH), "ctx", 0, 0)
    send = small(sum_kernel, block, "sum")(me, image_slots, parts)
    got = lax.all_to_all(send, "doc", 0, 0)
    d_image_kv = small(
        functools.partial(place_kernel, docs),
        jax.ShapeDtypeStruct(image_kv.shape, jnp.float32),
        "place",
    )(me, image_slots, got)
    d_queries = pl.pallas_call(
        merge_kernel,
        in_specs=[in_smem] + [anywhere] * LINE,
        out_specs=anywhere,
        out_shape=jax.ShapeDtypeStruct(queries.shape[1:], jnp.bfloat16),
        scratch_shapes=[pltpu.SemaphoreType.DMA((LINE,))],
        name="merge",
    )(me, *dqs)
    return d_queries[None], d_image_kv


def solution(mesh):
    return jax.shard_map(
        shards,
        mesh=mesh,
        in_specs=(
            P("doc", "ctx", None),
            P("doc", "ctx", None),
            P("doc", "ctx", None),
            P(),
            P(),
            P("doc", "ctx", None),
        ),
        out_specs=(P("doc", "ctx", None), P("doc", "ctx", None)),
        check_vma=False,
    )
```

```python
import functools

import jax
import jax.numpy as jnp
from jax import lax
from jax.experimental import pallas as pl
from jax.experimental.pallas import tpu as pltpu
from jax.sharding import PartitionSpec as P

KV_HEADS = 4
WIDTH = 128
GROUP = 8
KEY_COLUMNS = 512
IMAGES = 4
LOW = -1e30
SCALE = WIDTH ** (-0.5)
LOG2E = 1.4426950408889634
LINE = 4
BLOCK_HEADS = 2
PAD = 16
VMEM_LIMIT = 48 * 1024 * 1024

SMEM = pltpu.MemorySpace.SMEM
VMEM = pltpu.MemorySpace.VMEM
HBM = pltpu.MemorySpace.HBM


def place_on_line():
    doc, text = lax.axis_index("doc"), lax.axis_index("ctx")
    return doc, jnp.where(doc % 2 == 0, text % LINE, text // LINE)


def pack_kernel(docs, slots_any, kv, out, slots, held, sems):
    fetch_slots = pltpu.make_async_copy(slots_any, slots, sems.at[docs])
    fetch = pltpu.make_async_copy(kv, held, sems.at[docs + 1])
    fetch_slots.start()
    fetch.start()
    fetch_slots.wait()
    doc, _ = place_on_line()
    copies = []
    for d in range(docs):
        local = 0
        for j in range(IMAGES):
            s = slots[d * IMAGES + j]
            local += jnp.where(s // IMAGES == doc, s % IMAGES, 0)
        copies.append(pltpu.make_async_copy(held.at[local], out.at[d], sems.at[d]))
    fetch.wait()
    for copy in copies:
        copy.start()
    for copy in copies:
        copy.wait()


def pick_kernel(slots, got, out):
    doc, _ = place_on_line()
    for j in range(IMAGES):
        rows = got[slots[doc * IMAGES + j] // IMAGES]
        heads = [
            jnp.concatenate(
                [
                    rows[:, c * WIDTH : (c + 1) * WIDTH],
                    rows[:, KEY_COLUMNS + c * WIDTH : KEY_COLUMNS + (c + 1) * WIDTH],
                ],
                axis=1,
            )
            for c in range(KV_HEADS)
        ]
        along_z = doc % 2 == 0
        for y in range(LINE):
            for z in range(LINE):
                out[y * LINE + z, j] = jnp.where(along_z, heads[z], heads[y])


def payload_kernel(q, d_out, spans, *refs):
    outs, held, sems = refs[:LINE], refs[LINE], refs[LINE + 1]
    tokens = q.shape[0]
    width = q.shape[1] // KV_HEADS
    _, place = place_on_line()
    order = [2, 1, 3, 0]
    fetches = []
    for k in order:
        columns = pl.ds(pl.multiple_of(lax.rem(place + k, LINE) * width, WIDTH), width)
        pair = [
            pltpu.make_async_copy(q.at[:, columns], held.at[k, :tokens], sems.at[3 * k]),
            pltpu.make_async_copy(
                d_out.at[:, columns], held.at[k, tokens : 2 * tokens], sems.at[3 * k + 1]
            ),
        ]
        for copy in pair:
            copy.start()
        fetches.append(pair)
    for k in order:
        held[k, 2 * tokens :] = jnp.zeros_like(held[k, 2 * tokens :])
        held[k, 2 * tokens : 2 * tokens + 2, :tokens] = spans[...].astype(jnp.bfloat16)
    copies = []
    for k, pair in zip(order, fetches):
        for copy in pair:
            copy.wait()
        copies.append(pltpu.make_async_copy(held.at[k], outs[k], sems.at[3 * k + 2]))
        copies[-1].start()
    for copy in copies:
        copy.wait()


def merge_kernel(*refs):
    _, place = place_on_line()
    *parts, out = refs
    width = out.shape[1] // KV_HEADS
    for k, part in enumerate(parts):
        columns = pl.ds(pl.multiple_of(lax.rem(place + k, LINE) * width, WIDTH), width)
        out[:, columns] = part[...]


def softmax_gradients(scores, d_probs, seen):
    keys, rows = scores.shape
    scores = scores.reshape(-1, IMAGES, 16, rows)
    d_probs = d_probs.reshape(-1, IMAGES, 16, rows)
    row_max = None
    for j in range(IMAGES):
        top = jnp.max(jnp.max(scores[:, j], axis=0), axis=0, keepdims=True)
        top = jnp.where(seen[j], top, LOW)
        row_max = top if row_max is None else jnp.maximum(row_max, top)
    row_max = row_max * (SCALE * LOG2E)
    terms = []
    total = 0.0
    dots = 0.0
    for j in range(IMAGES):
        term = jnp.exp2(scores[:, j] * (SCALE * LOG2E) - jnp.where(seen[j], row_max, -LOW))
        total += jnp.sum(jnp.sum(term, axis=0), axis=0, keepdims=True)
        dots += jnp.sum(jnp.sum(term * d_probs[:, j], axis=0), axis=0, keepdims=True)
        terms.append(term)
    inverse = 1.0 / total
    delta = dots * inverse
    low_probs = []
    d_scores = []
    for j in range(IMAGES):
        probs = terms[j] * inverse
        low_probs.append(probs.astype(jnp.bfloat16)[:, None])
        d_scores.append((probs * (d_probs[:, j] - delta)).astype(jnp.bfloat16)[:, None])
    low_probs = jnp.concatenate(low_probs, axis=1).reshape(keys, rows)
    d_scores = jnp.concatenate(d_scores, axis=1).reshape(keys, rows)
    return low_probs, d_scores


def grad_kernel(gate, kv_any, *refs):
    pieces, dqs, dkv_any = refs[:LINE], refs[LINE : 2 * LINE], refs[2 * LINE]
    kv, held, dq, dkv, keys_t, probs, d_scores, q_rows, d_rows, acc, sems = refs[2 * LINE + 1 :]
    tokens = dqs[0].shape[0]
    block = BLOCK_HEADS * tokens
    fetch_kv = pltpu.make_async_copy(kv_any, kv, sems.at[2 * LINE])
    fetch_kv.start()
    for k in range(LINE):
        pltpu.make_async_copy(pieces[k], held.at[k], sems.at[k]).start()
    fetch_kv.wait()
    keys_t[...] = kv[:, :WIDTH].T
    acc[...] = jnp.zeros_like(acc)
    factor = jnp.tanh(gate[...])
    transposed = (((1,), (1,)), ((), ()))

    def work(step, carry):
        pltpu.make_async_copy(pieces[0], held.at[step], sems.at[step]).wait()
        for h in range(GROUP):
            rows, columns = slice(h * tokens, (h + 1) * tokens), slice(h * WIDTH, (h + 1) * WIDTH)
            q_rows[rows] = held[step, :tokens, columns]
            wide = held[step, tokens : 2 * tokens, columns].astype(jnp.float32)
            d_rows[rows] = (wide * factor).astype(jnp.bfloat16)
        spans = held[step, 2 * tokens :, :tokens].astype(jnp.float32)
        low = jnp.concatenate([spans[0:1]] * BLOCK_HEADS, axis=1)
        high = jnp.concatenate([spans[1:2]] * BLOCK_HEADS, axis=1)
        seen = [(low <= j) & (j < high) for j in range(IMAGES)]
        for at in range(0, GROUP * tokens, block):
            rows = slice(at, at + block)
            scores = lax.dot_general(
                kv[:, :WIDTH], q_rows[rows], transposed, preferred_element_type=jnp.float32
            )
            d_probs = lax.dot_general(
                kv[:, WIDTH:], d_rows[rows], transposed, preferred_element_type=jnp.float32
            )
            probs[:, rows], d_scores[:, rows] = softmax_gradients(scores, d_probs, seen)
        acc[:, :WIDTH] += jnp.dot(d_scores[...], q_rows[...], preferred_element_type=jnp.float32)
        acc[:, WIDTH:] += jnp.dot(probs[...], d_rows[...], preferred_element_type=jnp.float32)
        dq_t = jnp.dot(keys_t[...], d_scores[...], preferred_element_type=jnp.float32) * SCALE
        dq_rows = dq_t.T.astype(jnp.bfloat16)
        for h in range(GROUP):
            dq[step, :, h * WIDTH : (h + 1) * WIDTH] = dq_rows[h * tokens : (h + 1) * tokens]
        for k in range(LINE):

            @pl.when(step == k)
            def _():
                pltpu.make_async_copy(dq.at[k], dqs[k], sems.at[LINE + k]).start()

        return carry

    lax.fori_loop(0, LINE, work, 0)
    dkv[:, :WIDTH] = (acc[:, :WIDTH] * SCALE).astype(jnp.bfloat16)
    dkv[:, WIDTH:] = acc[:, WIDTH:].astype(jnp.bfloat16)
    give = pltpu.make_async_copy(dkv, dkv_any, sems.at[2 * LINE])
    give.start()
    for k in range(LINE):
        pltpu.make_async_copy(dq.at[k], dqs[k], sems.at[LINE + k]).wait()
    give.wait()


def gradients(gate, kv, pieces):
    key_rows = kv.shape[0]
    tokens = (pieces[0].shape[0] - PAD) // 2
    width = pieces[0].shape[1]
    rows = GROUP * tokens
    in_hbm = pl.BlockSpec(memory_space=HBM)
    return pl.pallas_call(
        grad_kernel,
        in_specs=[pl.BlockSpec(memory_space=VMEM)] + [in_hbm] * (LINE + 1),
        out_specs=[in_hbm] * (LINE + 1),
        out_shape=[jax.ShapeDtypeStruct((tokens, width), jnp.bfloat16)] * LINE
        + [jax.ShapeDtypeStruct(kv.shape, jnp.bfloat16)],
        scratch_shapes=[
            pltpu.VMEM(kv.shape, jnp.bfloat16),
            pltpu.VMEM((LINE,) + pieces[0].shape, jnp.bfloat16),
            pltpu.VMEM((LINE, tokens, width), jnp.bfloat16),
            pltpu.VMEM(kv.shape, jnp.bfloat16),
            pltpu.VMEM((WIDTH, key_rows), jnp.bfloat16),
            pltpu.VMEM((key_rows, rows), jnp.bfloat16),
            pltpu.VMEM((key_rows, rows), jnp.bfloat16),
            pltpu.VMEM((rows, WIDTH), jnp.bfloat16),
            pltpu.VMEM((rows, WIDTH), jnp.bfloat16),
            pltpu.VMEM(kv.shape, jnp.float32),
            pltpu.SemaphoreType.DMA((2 * LINE + 1,)),
        ],
        compiler_params=pltpu.CompilerParams(vmem_limit_bytes=VMEM_LIMIT),
        cost_estimate=pl.CostEstimate(
            flops=10 * LINE * rows * key_rows * WIDTH,
            bytes_accessed=4 * 1024 * 1024,
            transcendentals=LINE * rows * key_rows,
        ),
        name="gradients",
    )(gate, kv, *pieces)


def sum_kernel(slots, got, out):
    doc, _ = place_on_line()
    out[...] = jnp.zeros_like(out)
    along_z = doc % 2 == 0
    for j in range(IMAGES):
        owner = slots[doc * IMAGES + j] // IMAGES
        for c in range(KV_HEADS):
            total = 0.0
            for line in range(LINE):
                at = jnp.where(along_z, line * LINE + c, c * LINE + line)
                total += got[at, j].astype(jnp.float32)
            out[owner, :, c * WIDTH : (c + 1) * WIDTH] = total[:, :WIDTH].astype(jnp.bfloat16)
            out[owner, :, KEY_COLUMNS + c * WIDTH : KEY_COLUMNS + (c + 1) * WIDTH] = total[
                :, WIDTH:
            ].astype(jnp.bfloat16)


def place_kernel(docs, slots, got, out):
    doc_here, _ = place_on_line()
    for s in range(IMAGES):
        doc = 0
        for d in range(docs):
            for j in range(IMAGES):
                doc += jnp.where(slots[d * IMAGES + j] == doc_here * IMAGES + s, d, 0)
        out[s] = got[doc].astype(jnp.float32)


def small(kernel, out_shape, name):
    return pl.pallas_call(
        kernel,
        in_specs=[
            pl.BlockSpec(memory_space=SMEM),
            pl.BlockSpec(memory_space=VMEM),
        ],
        out_specs=pl.BlockSpec(memory_space=VMEM),
        out_shape=out_shape,
        compiler_params=pltpu.CompilerParams(vmem_limit_bytes=VMEM_LIMIT),
        name=name,
    )


def shift(docs, k):
    pairs = []
    for d in range(docs):
        for a in range(LINE):
            for b in range(LINE):
                to = (b + k) % LINE
                ends = (a * LINE + b, a * LINE + to) if d % 2 == 0 else (b * LINE + a, to * LINE + a)
                pairs.append((d * LINE * LINE + ends[0], d * LINE * LINE + ends[1]))
    return pairs


def shards(queries, image_kv, d_out, attn_gate, image_slots, spans):
    docs = lax.axis_size("doc")
    texts = lax.axis_size("ctx")
    images, rows, columns = image_kv.shape
    tokens, width = queries.shape[1], queries.shape[2] // KV_HEADS
    both = ("doc", "ctx")
    in_hbm = pl.BlockSpec(memory_space=HBM)
    in_vmem = pl.BlockSpec(memory_space=VMEM)
    params = pltpu.CompilerParams(vmem_limit_bytes=VMEM_LIMIT)
    block = jax.ShapeDtypeStruct((docs, rows, columns), jnp.bfloat16)
    send = pl.pallas_call(
        functools.partial(pack_kernel, docs),
        in_specs=[in_hbm, in_hbm],
        out_specs=in_hbm,
        out_shape=block,
        scratch_shapes=[
            pltpu.SMEM(image_slots.shape, jnp.int32),
            pltpu.VMEM(image_kv.shape, jnp.bfloat16),
            pltpu.SemaphoreType.DMA((docs + 2,)),
        ],
        compiler_params=params,
        name="pack",
    )(image_slots, image_kv)
    got = lax.all_to_all(send, "doc", 0, 0)
    pieces = pl.pallas_call(
        payload_kernel,
        in_specs=[in_hbm, in_hbm, in_vmem],
        out_specs=[in_hbm] * LINE,
        out_shape=[jax.ShapeDtypeStruct((2 * tokens + PAD, width), jnp.bfloat16)] * LINE,
        scratch_shapes=[
            pltpu.VMEM((LINE, 2 * tokens + PAD, width), jnp.bfloat16),
            pltpu.SemaphoreType.DMA((3 * LINE,)),
        ],
        compiler_params=params,
        name="payload",
    )(queries[0], d_out[0], spans[0].T)
    pieces = [pieces[0]] + [lax.ppermute(pieces[k], both, shift(docs, k)) for k in range(1, LINE)]
    one_head = jax.ShapeDtypeStruct((texts, images, rows, 2 * WIDTH), jnp.bfloat16)
    send = small(pick_kernel, one_head, "pick")(image_slots, got)
    kv = lax.all_to_all(send, "ctx", 0, 0).reshape(texts * images * rows, 2 * WIDTH)
    *dqs, dkv = gradients(attn_gate.reshape(1, 1), kv, pieces)
    dqs = [dqs[0]] + [lax.ppermute(dqs[k], both, shift(docs, -k)) for k in range(1, LINE)]
    parts = lax.all_to_all(dkv.reshape(texts, images, rows, 2 * WIDTH), "ctx", 0, 0)
    send = small(sum_kernel, block, "sum")(image_slots, parts)
    got = lax.all_to_all(send, "doc", 0, 0)
    d_image_kv = small(
        functools.partial(place_kernel, docs),
        jax.ShapeDtypeStruct(image_kv.shape, jnp.float32),
        "place",
    )(image_slots, got)
    d_queries = pl.pallas_call(
        merge_kernel,
        in_specs=[in_vmem] * LINE,
        out_specs=in_vmem,
        out_shape=jax.ShapeDtypeStruct(queries.shape[1:], jnp.bfloat16),
        compiler_params=params,
        name="merge",
    )(*dqs)
    return d_queries[None], d_image_kv


def solution(mesh):
    return jax.shard_map(
        shards,
        mesh=mesh,
        in_specs=(
            P("doc", "ctx", None),
            P("doc", "ctx", None),
            P("doc", "ctx", None),
            P(),
            P(),
            P("doc", "ctx", None),
        ),
        out_specs=(P("doc", "ctx", None), P("doc", "ctx", None)),
        check_vma=False,
    )
```

```python
import functools

import jax
import jax.numpy as jnp
from jax import lax
from jax.experimental import pallas as pl
from jax.experimental.pallas import tpu as pltpu
from jax.sharding import PartitionSpec as P

KV_HEADS = 4
WIDTH = 128
GROUP = 8
KEY_COLUMNS = 512
IMAGES = 4
LOW = -1e30
SCALE = WIDTH ** (-0.5)
LOG2E = 1.4426950408889634
LINE = 4
BLOCK_HEADS = 2
PAD = 16
VMEM_LIMIT = 48 * 1024 * 1024
GRADIENT_VMEM = 60 * 1024 * 1024

SMEM = pltpu.MemorySpace.SMEM
VMEM = pltpu.MemorySpace.VMEM
HBM = pltpu.MemorySpace.HBM


def place_on_line():
    doc, text = lax.axis_index("doc"), lax.axis_index("ctx")
    return doc, jnp.where(doc % 2 == 0, text % LINE, text // LINE)


def pack_kernel(docs, slots_any, kv, out, slots, held, sems):
    fetch_slots = pltpu.make_async_copy(slots_any, slots, sems.at[docs])
    fetch = pltpu.make_async_copy(kv, held, sems.at[docs + 1])
    fetch_slots.start()
    fetch.start()
    fetch_slots.wait()
    doc, _ = place_on_line()
    copies = []
    for d in range(docs):
        local = 0
        for j in range(IMAGES):
            s = slots[d * IMAGES + j]
            local += jnp.where(s // IMAGES == doc, s % IMAGES, 0)
        copies.append(pltpu.make_async_copy(held.at[local], out.at[d], sems.at[d]))
    fetch.wait()
    for copy in copies:
        copy.start()
    for copy in copies:
        copy.wait()


def pick_kernel(slots, got, out):
    doc, _ = place_on_line()
    for j in range(IMAGES):
        rows = got[slots[doc * IMAGES + j] // IMAGES]
        heads = [
            jnp.concatenate(
                [
                    rows[:, c * WIDTH : (c + 1) * WIDTH],
                    rows[:, KEY_COLUMNS + c * WIDTH : KEY_COLUMNS + (c + 1) * WIDTH],
                ],
                axis=1,
            )
            for c in range(KV_HEADS)
        ]
        along_z = doc % 2 == 0
        for y in range(LINE):
            for z in range(LINE):
                out[y * LINE + z, j] = jnp.where(along_z, heads[z], heads[y])


def payload_kernel(q, d_out, spans_any, *refs):
    outs, held, spans, sems = refs[:LINE], refs[LINE], refs[LINE + 1], refs[LINE + 2]
    tokens = q.shape[0]
    width = q.shape[1] // KV_HEADS
    _, place = place_on_line()
    order = [2, 1, 3, 0]
    fetch_spans = pltpu.make_async_copy(spans_any, spans, sems.at[3 * LINE])
    fetch_spans.start()
    fetches = []
    for k in order:
        columns = pl.ds(pl.multiple_of(lax.rem(place + k, LINE) * width, WIDTH), width)
        pair = [
            pltpu.make_async_copy(q.at[:, columns], held.at[k, :tokens], sems.at[3 * k]),
            pltpu.make_async_copy(
                d_out.at[:, columns], held.at[k, tokens : 2 * tokens], sems.at[3 * k + 1]
            ),
        ]
        for copy in pair:
            copy.start()
        fetches.append(pair)
    fetch_spans.wait()
    for k in order:
        held[k, 2 * tokens :] = jnp.zeros_like(held[k, 2 * tokens :])
        held[k, 2 * tokens : 2 * tokens + 2, :tokens] = spans[...].astype(jnp.bfloat16)
    copies = []
    for k, pair in zip(order, fetches):
        for copy in pair:
            copy.wait()
        copies.append(pltpu.make_async_copy(held.at[k], outs[k], sems.at[3 * k + 2]))
        copies[-1].start()
    for copy in copies:
        copy.wait()


def merge_kernel(*refs):
    _, place = place_on_line()
    *parts, out = refs
    width = out.shape[1] // KV_HEADS
    for k, part in enumerate(parts):
        columns = pl.ds(pl.multiple_of(lax.rem(place + k, LINE) * width, WIDTH), width)
        out[:, columns] = part[...]


def softmax_gradients(scores, d_probs, seen):
    keys, rows = scores.shape
    scores = scores.reshape(-1, IMAGES, 16, rows)
    d_probs = d_probs.reshape(-1, IMAGES, 16, rows)
    row_max = None
    for j in range(IMAGES):
        top = jnp.max(jnp.max(scores[:, j], axis=0), axis=0, keepdims=True)
        top = jnp.where(seen[j], top, LOW)
        row_max = top if row_max is None else jnp.maximum(row_max, top)
    row_max = row_max * (SCALE * LOG2E)
    terms = []
    total = 0.0
    dots = 0.0
    for j in range(IMAGES):
        term = jnp.exp2(scores[:, j] * (SCALE * LOG2E) - jnp.where(seen[j], row_max, -LOW))
        total += jnp.sum(jnp.sum(term, axis=0), axis=0, keepdims=True)
        dots += jnp.sum(jnp.sum(term * d_probs[:, j], axis=0), axis=0, keepdims=True)
        terms.append(term)
    inverse = 1.0 / total
    delta = dots * inverse
    low_probs = []
    d_scores = []
    for j in range(IMAGES):
        probs = terms[j] * inverse
        low_probs.append(probs.astype(jnp.bfloat16)[:, None])
        d_scores.append((probs * (d_probs[:, j] - delta)).astype(jnp.bfloat16)[:, None])
    low_probs = jnp.concatenate(low_probs, axis=1).reshape(keys, rows)
    d_scores = jnp.concatenate(d_scores, axis=1).reshape(keys, rows)
    return low_probs, d_scores


def grad_kernel(gate, kv_any, *refs):
    pieces, dqs, dkv_any = refs[:LINE], refs[LINE : 2 * LINE], refs[2 * LINE]
    kv, held, dq, dkv, keys_t, probs, d_scores, q_rows, d_rows, acc, sems = refs[2 * LINE + 1 :]
    tokens = dqs[0].shape[0]
    block = BLOCK_HEADS * tokens
    fetch_kv = pltpu.make_async_copy(kv_any, kv, sems.at[2 * LINE])
    fetch_kv.start()
    for k in range(LINE):
        pltpu.make_async_copy(pieces[k], held.at[k], sems.at[k]).start()
    fetch_kv.wait()
    keys_t[...] = kv[:, :WIDTH].T
    acc[...] = jnp.zeros_like(acc)
    factor = jnp.tanh(gate[...])
    transposed = (((1,), (1,)), ((), ()))

    def work(step, carry):
        pltpu.make_async_copy(pieces[0], held.at[step], sems.at[step]).wait()
        for h in range(GROUP):
            rows, columns = slice(h * tokens, (h + 1) * tokens), slice(h * WIDTH, (h + 1) * WIDTH)
            q_rows[rows] = held[step, :tokens, columns]
            wide = held[step, tokens : 2 * tokens, columns].astype(jnp.float32)
            d_rows[rows] = (wide * factor).astype(jnp.bfloat16)
        spans = held[step, 2 * tokens :, :tokens].astype(jnp.float32)
        low = jnp.concatenate([spans[0:1]] * BLOCK_HEADS, axis=1)
        high = jnp.concatenate([spans[1:2]] * BLOCK_HEADS, axis=1)
        seen = [(low <= j) & (j < high) for j in range(IMAGES)]
        for at in range(0, GROUP * tokens, block):
            rows = slice(at, at + block)
            scores = lax.dot_general(
                kv[:, :WIDTH], q_rows[rows], transposed, preferred_element_type=jnp.float32
            )
            d_probs = lax.dot_general(
                kv[:, WIDTH:], d_rows[rows], transposed, preferred_element_type=jnp.float32
            )
            probs[:, rows], d_scores[:, rows] = softmax_gradients(scores, d_probs, seen)
        acc[:, :WIDTH] += jnp.dot(d_scores[...], q_rows[...], preferred_element_type=jnp.float32)
        acc[:, WIDTH:] += jnp.dot(probs[...], d_rows[...], preferred_element_type=jnp.float32)
        dq_t = jnp.dot(keys_t[...], d_scores[...], preferred_element_type=jnp.float32) * SCALE
        dq_rows = dq_t.T.astype(jnp.bfloat16)
        for h in range(GROUP):
            dq[step, :, h * WIDTH : (h + 1) * WIDTH] = dq_rows[h * tokens : (h + 1) * tokens]
        for k in range(LINE):

            @pl.when(step == k)
            def _():
                pltpu.make_async_copy(dq.at[k], dqs[k], sems.at[LINE + k]).start()

        return carry

    lax.fori_loop(0, LINE, work, 0)
    dkv[:, :WIDTH] = (acc[:, :WIDTH] * SCALE).astype(jnp.bfloat16)
    dkv[:, WIDTH:] = acc[:, WIDTH:].astype(jnp.bfloat16)
    give = pltpu.make_async_copy(dkv, dkv_any, sems.at[2 * LINE])
    give.start()
    for k in range(LINE):
        pltpu.make_async_copy(dq.at[k], dqs[k], sems.at[LINE + k]).wait()
    give.wait()


def gradients(gate, kv, pieces):
    key_rows = kv.shape[0]
    tokens = (pieces[0].shape[0] - PAD) // 2
    width = pieces[0].shape[1]
    rows = GROUP * tokens
    in_hbm = pl.BlockSpec(memory_space=HBM)
    return pl.pallas_call(
        grad_kernel,
        in_specs=[pl.BlockSpec(memory_space=VMEM)] + [in_hbm] * (LINE + 1),
        out_specs=[in_hbm] * (LINE + 1),
        out_shape=[jax.ShapeDtypeStruct((tokens, width), jnp.bfloat16)] * LINE
        + [jax.ShapeDtypeStruct(kv.shape, jnp.bfloat16)],
        scratch_shapes=[
            pltpu.VMEM(kv.shape, jnp.bfloat16),
            pltpu.VMEM((LINE,) + pieces[0].shape, jnp.bfloat16),
            pltpu.VMEM((LINE, tokens, width), jnp.bfloat16),
            pltpu.VMEM(kv.shape, jnp.bfloat16),
            pltpu.VMEM((WIDTH, key_rows), jnp.bfloat16),
            pltpu.VMEM((key_rows, rows), jnp.bfloat16),
            pltpu.VMEM((key_rows, rows), jnp.bfloat16),
            pltpu.VMEM((rows, WIDTH), jnp.bfloat16),
            pltpu.VMEM((rows, WIDTH), jnp.bfloat16),
            pltpu.VMEM(kv.shape, jnp.float32),
            pltpu.SemaphoreType.DMA((2 * LINE + 1,)),
        ],
        compiler_params=pltpu.CompilerParams(vmem_limit_bytes=GRADIENT_VMEM),
        cost_estimate=pl.CostEstimate(
            flops=10 * LINE * rows * key_rows * WIDTH,
            bytes_accessed=4 * 1024 * 1024,
            transcendentals=LINE * rows * key_rows,
        ),
        name="gradients",
    )(gate, kv, *pieces)


def sum_kernel(slots, got, out):
    doc, _ = place_on_line()
    out[...] = jnp.zeros_like(out)
    along_z = doc % 2 == 0
    for j in range(IMAGES):
        owner = slots[doc * IMAGES + j] // IMAGES
        for c in range(KV_HEADS):
            total = 0.0
            for line in range(LINE):
                at = jnp.where(along_z, line * LINE + c, c * LINE + line)
                total += got[at, j].astype(jnp.float32)
            out[owner, :, c * WIDTH : (c + 1) * WIDTH] = total[:, :WIDTH].astype(jnp.bfloat16)
            out[owner, :, KEY_COLUMNS + c * WIDTH : KEY_COLUMNS + (c + 1) * WIDTH] = total[
                :, WIDTH:
            ].astype(jnp.bfloat16)


def place_kernel(docs, slots, got, out):
    doc_here, _ = place_on_line()
    for s in range(IMAGES):
        doc = 0
        for d in range(docs):
            for j in range(IMAGES):
                doc += jnp.where(slots[d * IMAGES + j] == doc_here * IMAGES + s, d, 0)
        out[s] = got[doc].astype(jnp.float32)


def small(kernel, out_shape, name):
    return pl.pallas_call(
        kernel,
        in_specs=[
            pl.BlockSpec(memory_space=SMEM),
            pl.BlockSpec(memory_space=VMEM),
        ],
        out_specs=pl.BlockSpec(memory_space=VMEM),
        out_shape=out_shape,
        compiler_params=pltpu.CompilerParams(vmem_limit_bytes=VMEM_LIMIT),
        name=name,
    )


def shift(docs, k):
    pairs = []
    for d in range(docs):
        for a in range(LINE):
            for b in range(LINE):
                to = (b + k) % LINE
                ends = (a * LINE + b, a * LINE + to) if d % 2 == 0 else (b * LINE + a, to * LINE + a)
                pairs.append((d * LINE * LINE + ends[0], d * LINE * LINE + ends[1]))
    return pairs


def shards(queries, image_kv, d_out, attn_gate, image_slots, spans):
    docs = lax.axis_size("doc")
    texts = lax.axis_size("ctx")
    images, rows, columns = image_kv.shape
    tokens, width = queries.shape[1], queries.shape[2] // KV_HEADS
    both = ("doc", "ctx")
    in_hbm = pl.BlockSpec(memory_space=HBM)
    in_vmem = pl.BlockSpec(memory_space=VMEM)
    params = pltpu.CompilerParams(vmem_limit_bytes=VMEM_LIMIT)
    block = jax.ShapeDtypeStruct((docs, rows, columns), jnp.bfloat16)
    send = pl.pallas_call(
        functools.partial(pack_kernel, docs),
        in_specs=[in_hbm, in_hbm],
        out_specs=in_hbm,
        out_shape=block,
        scratch_shapes=[
            pltpu.SMEM(image_slots.shape, jnp.int32),
            pltpu.VMEM(image_kv.shape, jnp.bfloat16),
            pltpu.SemaphoreType.DMA((docs + 2,)),
        ],
        name="pack",
    )(image_slots, image_kv)
    got = lax.all_to_all(send, "doc", 0, 0)
    pieces = pl.pallas_call(
        payload_kernel,
        in_specs=[in_hbm, in_hbm, in_hbm],
        out_specs=[in_hbm] * LINE,
        out_shape=[jax.ShapeDtypeStruct((2 * tokens + PAD, width), jnp.bfloat16)] * LINE,
        scratch_shapes=[
            pltpu.VMEM((LINE, 2 * tokens + PAD, width), jnp.bfloat16),
            pltpu.VMEM((2, tokens), jnp.int32),
            pltpu.SemaphoreType.DMA((3 * LINE + 1,)),
        ],
        name="payload",
    )(queries[0], d_out[0], spans[0].T)
    pieces = [pieces[0]] + [lax.ppermute(pieces[k], both, shift(docs, k)) for k in range(1, LINE)]
    one_head = jax.ShapeDtypeStruct((texts, images, rows, 2 * WIDTH), jnp.bfloat16)
    send = small(pick_kernel, one_head, "pick")(image_slots, got)
    kv = lax.all_to_all(send, "ctx", 0, 0).reshape(texts * images * rows, 2 * WIDTH)
    *dqs, dkv = gradients(attn_gate.reshape(1, 1), kv, pieces)
    dqs = [dqs[0]] + [lax.ppermute(dqs[k], both, shift(docs, -k)) for k in range(1, LINE)]
    parts = lax.all_to_all(dkv.reshape(texts, images, rows, 2 * WIDTH), "ctx", 0, 0)
    send = small(sum_kernel, block, "sum")(image_slots, parts)
    got = lax.all_to_all(send, "doc", 0, 0)
    d_image_kv = small(
        functools.partial(place_kernel, docs),
        jax.ShapeDtypeStruct(image_kv.shape, jnp.float32),
        "place",
    )(image_slots, got)
    d_queries = pl.pallas_call(
        merge_kernel,
        in_specs=[in_vmem] * LINE,
        out_specs=in_vmem,
        out_shape=jax.ShapeDtypeStruct(queries.shape[1:], jnp.bfloat16),
        compiler_params=params,
        name="merge",
    )(*dqs)
    return d_queries[None], d_image_kv


def solution(mesh):
    return jax.shard_map(
        shards,
        mesh=mesh,
        in_specs=(
            P("doc", "ctx", None),
            P("doc", "ctx", None),
            P("doc", "ctx", None),
            P(),
            P(),
            P("doc", "ctx", None),
        ),
        out_specs=(P("doc", "ctx", None), P("doc", "ctx", None)),
        check_vma=False,
    )
```

```python
import functools

import jax
import jax.numpy as jnp
from jax import lax
from jax.experimental import pallas as pl
from jax.experimental.pallas import tpu as pltpu
from jax.sharding import PartitionSpec as P

KV_HEADS = 4
WIDTH = 128
GROUP = 8
KEY_COLUMNS = 512
IMAGES = 4
LOW = -1e30
SCALE = WIDTH ** (-0.5)
LOG2E = 1.4426950408889634
LINE = 4
BLOCK_HEADS = 2
PAD = 16
VMEM_LIMIT = 48 * 1024 * 1024
GRADIENT_VMEM = 60 * 1024 * 1024

SMEM = pltpu.MemorySpace.SMEM
VMEM = pltpu.MemorySpace.VMEM
HBM = pltpu.MemorySpace.HBM


def place_on_line():
    doc, text = lax.axis_index("doc"), lax.axis_index("ctx")
    return doc, jnp.where(doc % 2 == 0, text % LINE, text // LINE)


def pack_kernel(docs, slots_any, kv, out, slots, held, sems):
    fetch_slots = pltpu.make_async_copy(slots_any, slots, sems.at[docs])
    fetch = pltpu.make_async_copy(kv, held, sems.at[docs + 1])
    fetch_slots.start()
    fetch.start()
    fetch_slots.wait()
    doc, _ = place_on_line()
    copies = []
    for d in range(docs):
        local = 0
        for j in range(IMAGES):
            s = slots[d * IMAGES + j]
            local += jnp.where(s // IMAGES == doc, s % IMAGES, 0)
        copies.append(pltpu.make_async_copy(held.at[local], out.at[d], sems.at[d]))
    fetch.wait()
    for copy in copies:
        copy.start()
    for copy in copies:
        copy.wait()


def pick_kernel(slots, got, out):
    doc, _ = place_on_line()
    for j in range(IMAGES):
        rows = got[slots[doc * IMAGES + j] // IMAGES]
        heads = [
            jnp.concatenate(
                [
                    rows[:, c * WIDTH : (c + 1) * WIDTH],
                    rows[:, KEY_COLUMNS + c * WIDTH : KEY_COLUMNS + (c + 1) * WIDTH],
                ],
                axis=1,
            )
            for c in range(KV_HEADS)
        ]
        along_z = doc % 2 == 0
        for y in range(LINE):
            for z in range(LINE):
                out[y * LINE + z, j] = jnp.where(along_z, heads[z], heads[y])


def payload_kernel(q, d_out, spans_any, *refs):
    outs, held, spans, sems = refs[:LINE], refs[LINE], refs[LINE + 1], refs[LINE + 2]
    tokens = q.shape[0]
    width = q.shape[1] // KV_HEADS
    _, place = place_on_line()
    order = [2, 1, 3, 0]
    fetch_spans = pltpu.make_async_copy(spans_any, spans, sems.at[3 * LINE])
    fetch_spans.start()
    fetches = []
    for k in order:
        columns = pl.ds(pl.multiple_of(lax.rem(place + k, LINE) * width, WIDTH), width)
        pair = [
            pltpu.make_async_copy(q.at[:, columns], held.at[k, :tokens], sems.at[3 * k]),
            pltpu.make_async_copy(
                d_out.at[:, columns], held.at[k, tokens : 2 * tokens], sems.at[3 * k + 1]
            ),
        ]
        for copy in pair:
            copy.start()
        fetches.append(pair)
    fetch_spans.wait()
    for k in order:
        held[k, 2 * tokens :] = jnp.zeros_like(held[k, 2 * tokens :])
        held[k, 2 * tokens : 2 * tokens + 2, :tokens] = spans[...].astype(jnp.bfloat16)
    copies = []
    for k, pair in zip(order, fetches):
        for copy in pair:
            copy.wait()
        copies.append(pltpu.make_async_copy(held.at[k], outs[k], sems.at[3 * k + 2]))
        copies[-1].start()
    for copy in copies:
        copy.wait()


def merge_kernel(*refs):
    _, place = place_on_line()
    *parts, out = refs
    width = out.shape[1] // KV_HEADS
    for k, part in enumerate(parts):
        columns = pl.ds(pl.multiple_of(lax.rem(place + k, LINE) * width, WIDTH), width)
        out[:, columns] = part[...]


def softmax_gradients(scores, d_probs, seen):
    keys, rows = scores.shape
    scores = scores.reshape(-1, IMAGES, 16, rows)
    d_probs = d_probs.reshape(-1, IMAGES, 16, rows)
    row_max = None
    for j in range(IMAGES):
        top = jnp.max(jnp.max(scores[:, j], axis=0), axis=0, keepdims=True)
        top = jnp.where(seen[j], top, LOW)
        row_max = top if row_max is None else jnp.maximum(row_max, top)
    row_max = row_max * SCALE
    terms = []
    lows = []
    total = 0.0
    dots = 0.0
    for j in range(IMAGES):
        term = jnp.exp(scores[:, j] * SCALE - jnp.where(seen[j], row_max, -LOW))
        total += jnp.sum(jnp.sum(term, axis=0), axis=0, keepdims=True)
        dots += jnp.sum(jnp.sum(term * d_probs[:, j], axis=0), axis=0, keepdims=True)
        terms.append(term)
        lows.append(d_probs[:, j].astype(jnp.bfloat16))
    inverse = 1.0 / total
    delta = (dots * inverse).astype(jnp.bfloat16)
    low_probs = []
    d_scores = []
    for j in range(IMAGES):
        probs = (terms[j] * inverse).astype(jnp.bfloat16)
        low_probs.append(probs[:, None])
        d_scores.append((probs * (lows[j] - delta))[:, None])
    low_probs = jnp.concatenate(low_probs, axis=1).reshape(keys, rows)
    d_scores = jnp.concatenate(d_scores, axis=1).reshape(keys, rows)
    return low_probs, d_scores


def grad_kernel(count, first, last, gate, kv_any, *refs):
    pieces, refs = refs[:count], refs[count:]
    so_far, refs = (None, refs) if first else (refs[0], refs[1:])
    dqs, dkv_any, refs = refs[:count], refs[count], refs[count + 1 :]
    kv, held, dq, dkv, keys_t, probs, d_scores, q_rows, d_rows, acc, sems = refs
    tokens = dqs[0].shape[0]
    block = BLOCK_HEADS * tokens
    fetch_kv = pltpu.make_async_copy(kv_any, kv, sems.at[2 * count])
    fetch_kv.start()
    for k in range(count):
        pltpu.make_async_copy(pieces[k], held.at[k], sems.at[k]).start()
    if not first:
        fetch_sums = pltpu.make_async_copy(so_far, acc, sems.at[2 * count + 1])
        fetch_sums.start()
    fetch_kv.wait()
    keys_t[...] = kv[:, :WIDTH].T
    if first:
        acc[...] = jnp.zeros_like(acc)
    else:
        fetch_sums.wait()
    factor = jnp.tanh(gate[...])
    transposed = (((1,), (1,)), ((), ()))

    def work(step, carry):
        pltpu.make_async_copy(pieces[0], held.at[step], sems.at[step]).wait()
        for h in range(GROUP):
            rows, columns = slice(h * tokens, (h + 1) * tokens), slice(h * WIDTH, (h + 1) * WIDTH)
            q_rows[rows] = held[step, :tokens, columns]
            wide = held[step, tokens : 2 * tokens, columns].astype(jnp.float32)
            d_rows[rows] = (wide * factor).astype(jnp.bfloat16)
        spans = held[step, 2 * tokens :, :tokens].astype(jnp.float32)
        low = jnp.concatenate([spans[0:1]] * BLOCK_HEADS, axis=1)
        high = jnp.concatenate([spans[1:2]] * BLOCK_HEADS, axis=1)
        seen = [(low <= j) & (j < high) for j in range(IMAGES)]
        for at in range(0, GROUP * tokens, block):
            rows = slice(at, at + block)
            scores = lax.dot_general(
                kv[:, :WIDTH], q_rows[rows], transposed, preferred_element_type=jnp.float32
            )
            d_probs = lax.dot_general(
                kv[:, WIDTH:], d_rows[rows], transposed, preferred_element_type=jnp.float32
            )
            probs[:, rows], d_scores[:, rows] = softmax_gradients(scores, d_probs, seen)
        acc[:, :WIDTH] += jnp.dot(d_scores[...], q_rows[...], preferred_element_type=jnp.float32)
        acc[:, WIDTH:] += jnp.dot(probs[...], d_rows[...], preferred_element_type=jnp.float32)
        dq_t = jnp.dot(keys_t[...], d_scores[...], preferred_element_type=jnp.float32) * SCALE
        dq_rows = dq_t.T.astype(jnp.bfloat16)
        for h in range(GROUP):
            dq[step, :, h * WIDTH : (h + 1) * WIDTH] = dq_rows[h * tokens : (h + 1) * tokens]
        for k in range(count):

            @pl.when(step == k)
            def _():
                pltpu.make_async_copy(dq.at[k], dqs[k], sems.at[count + k]).start()

        return carry

    lax.fori_loop(0, count, work, 0)
    if last:
        dkv[:, :WIDTH] = (acc[:, :WIDTH] * SCALE).astype(jnp.bfloat16)
        dkv[:, WIDTH:] = acc[:, WIDTH:].astype(jnp.bfloat16)
    give = pltpu.make_async_copy(dkv if last else acc, dkv_any, sems.at[2 * count])
    give.start()
    for k in range(count):
        pltpu.make_async_copy(dq.at[k], dqs[k], sems.at[count + k]).wait()
    give.wait()


def gradients(gate, kv, pieces, so_far=None, last=True):
    key_rows = kv.shape[0]
    count = len(pieces)
    first = so_far is None
    tokens = (pieces[0].shape[0] - PAD) // 2
    width = pieces[0].shape[1]
    rows = GROUP * tokens
    in_hbm = pl.BlockSpec(memory_space=HBM)
    operands = list(pieces) + ([] if first else [so_far])
    return pl.pallas_call(
        functools.partial(grad_kernel, count, first, last),
        in_specs=[pl.BlockSpec(memory_space=VMEM)] + [in_hbm] * (len(operands) + 1),
        out_specs=[in_hbm] * (count + 1),
        out_shape=[jax.ShapeDtypeStruct((tokens, width), jnp.bfloat16)] * count
        + [jax.ShapeDtypeStruct(kv.shape, jnp.bfloat16 if last else jnp.float32)],
        scratch_shapes=[
            pltpu.VMEM(kv.shape, jnp.bfloat16),
            pltpu.VMEM((count,) + pieces[0].shape, jnp.bfloat16),
            pltpu.VMEM((count, tokens, width), jnp.bfloat16),
            pltpu.VMEM(kv.shape, jnp.bfloat16),
            pltpu.VMEM((WIDTH, key_rows), jnp.bfloat16),
            pltpu.VMEM((key_rows, rows), jnp.bfloat16),
            pltpu.VMEM((key_rows, rows), jnp.bfloat16),
            pltpu.VMEM((rows, WIDTH), jnp.bfloat16),
            pltpu.VMEM((rows, WIDTH), jnp.bfloat16),
            pltpu.VMEM(kv.shape, jnp.float32),
            pltpu.SemaphoreType.DMA((2 * count + 2,)),
        ],
        compiler_params=pltpu.CompilerParams(vmem_limit_bytes=GRADIENT_VMEM),
        cost_estimate=pl.CostEstimate(
            flops=10 * count * rows * key_rows * WIDTH,
            bytes_accessed=4 * 1024 * 1024,
            transcendentals=count * rows * key_rows,
        ),
        name="gradients",
    )(gate, kv, *operands)


def sum_kernel(slots, got, out):
    doc, _ = place_on_line()
    out[...] = jnp.zeros_like(out)
    along_z = doc % 2 == 0
    for j in range(IMAGES):
        owner = slots[doc * IMAGES + j] // IMAGES
        for c in range(KV_HEADS):
            total = 0.0
            for line in range(LINE):
                at = jnp.where(along_z, line * LINE + c, c * LINE + line)
                total += got[at, j].astype(jnp.float32)
            out[owner, :, c * WIDTH : (c + 1) * WIDTH] = total[:, :WIDTH].astype(jnp.bfloat16)
            out[owner, :, KEY_COLUMNS + c * WIDTH : KEY_COLUMNS + (c + 1) * WIDTH] = total[
                :, WIDTH:
            ].astype(jnp.bfloat16)


def place_kernel(docs, slots, got, out):
    doc_here, _ = place_on_line()
    for s in range(IMAGES):
        doc = 0
        for d in range(docs):
            for j in range(IMAGES):
                doc += jnp.where(slots[d * IMAGES + j] == doc_here * IMAGES + s, d, 0)
        out[s] = got[doc].astype(jnp.float32)


def small(kernel, out_shape, name):
    return pl.pallas_call(
        kernel,
        in_specs=[
            pl.BlockSpec(memory_space=SMEM),
            pl.BlockSpec(memory_space=VMEM),
        ],
        out_specs=pl.BlockSpec(memory_space=VMEM),
        out_shape=out_shape,
        compiler_params=pltpu.CompilerParams(vmem_limit_bytes=VMEM_LIMIT),
        name=name,
    )


def shift(docs, k):
    pairs = []
    for d in range(docs):
        for a in range(LINE):
            for b in range(LINE):
                to = (b + k) % LINE
                ends = (a * LINE + b, a * LINE + to) if d % 2 == 0 else (b * LINE + a, to * LINE + a)
                pairs.append((d * LINE * LINE + ends[0], d * LINE * LINE + ends[1]))
    return pairs


def shards(queries, image_kv, d_out, attn_gate, image_slots, spans):
    docs = lax.axis_size("doc")
    texts = lax.axis_size("ctx")
    images, rows, columns = image_kv.shape
    tokens, width = queries.shape[1], queries.shape[2] // KV_HEADS
    both = ("doc", "ctx")
    in_hbm = pl.BlockSpec(memory_space=HBM)
    in_vmem = pl.BlockSpec(memory_space=VMEM)
    params = pltpu.CompilerParams(vmem_limit_bytes=VMEM_LIMIT)
    block = jax.ShapeDtypeStruct((docs, rows, columns), jnp.bfloat16)
    send = pl.pallas_call(
        functools.partial(pack_kernel, docs),
        in_specs=[in_hbm, in_hbm],
        out_specs=in_hbm,
        out_shape=block,
        scratch_shapes=[
            pltpu.SMEM(image_slots.shape, jnp.int32),
            pltpu.VMEM(image_kv.shape, jnp.bfloat16),
            pltpu.SemaphoreType.DMA((docs + 2,)),
        ],
        name="pack",
    )(image_slots, image_kv)
    got = lax.all_to_all(send, "doc", 0, 0)
    pieces = pl.pallas_call(
        payload_kernel,
        in_specs=[in_hbm, in_hbm, in_hbm],
        out_specs=[in_hbm] * LINE,
        out_shape=[jax.ShapeDtypeStruct((2 * tokens + PAD, width), jnp.bfloat16)] * LINE,
        scratch_shapes=[
            pltpu.VMEM((LINE, 2 * tokens + PAD, width), jnp.bfloat16),
            pltpu.VMEM((2, tokens), jnp.int32),
            pltpu.SemaphoreType.DMA((3 * LINE + 1,)),
        ],
        name="payload",
    )(queries[0], d_out[0], spans[0].T)
    one_head = jax.ShapeDtypeStruct((texts, images, rows, 2 * WIDTH), jnp.bfloat16)
    send = small(pick_kernel, one_head, "pick")(image_slots, got)
    own, after, far, before = pieces
    after = lax.ppermute(after, both, shift(docs, 1))
    before = lax.ppermute(before, both, shift(docs, -1))
    far, send = lax.optimization_barrier((far, send))
    far = lax.ppermute(far, both, shift(docs, 2))
    kv = lax.all_to_all(send, "ctx", 0, 0).reshape(texts * images * rows, 2 * WIDTH)
    gate = attn_gate.reshape(1, 1)
    dq_own, dq_after, dq_before, sums = gradients(gate, kv, [own, after, before], last=False)
    dq_far, dkv = gradients(gate, kv, [far], so_far=sums)
    dq_after = lax.ppermute(dq_after, both, shift(docs, -1))
    dq_before = lax.ppermute(dq_before, both, shift(docs, 1))
    dq_far = lax.ppermute(dq_far, both, shift(docs, 2))
    dqs = [dq_own, dq_after, dq_far, dq_before]
    parts = lax.all_to_all(dkv.reshape(texts, images, rows, 2 * WIDTH), "ctx", 0, 0)
    send = small(sum_kernel, block, "sum")(image_slots, parts)
    got = lax.all_to_all(send, "doc", 0, 0)
    d_image_kv = small(
        functools.partial(place_kernel, docs),
        jax.ShapeDtypeStruct(image_kv.shape, jnp.float32),
        "place",
    )(image_slots, got)
    d_queries = pl.pallas_call(
        merge_kernel,
        in_specs=[in_vmem] * LINE,
        out_specs=in_vmem,
        out_shape=jax.ShapeDtypeStruct(queries.shape[1:], jnp.bfloat16),
        compiler_params=params,
        name="merge",
    )(*dqs)
    return d_queries[None], d_image_kv


def solution(mesh):
    return jax.shard_map(
        shards,
        mesh=mesh,
        in_specs=(
            P("doc", "ctx", None),
            P("doc", "ctx", None),
            P("doc", "ctx", None),
            P(),
            P(),
            P("doc", "ctx", None),
        ),
        out_specs=(P("doc", "ctx", None), P("doc", "ctx", None)),
        check_vma=False,
    )
```

```python
import functools

import jax
import jax.numpy as jnp
from jax import lax
from jax.experimental import pallas as pl
from jax.experimental.pallas import tpu as pltpu
from jax.sharding import PartitionSpec as P

KV_HEADS = 4
WIDTH = 128
GROUP = 8
KEY_COLUMNS = 512
IMAGES = 4
LOW = -1e30
SCALE = WIDTH ** (-0.5)
LOG2E = 1.4426950408889634
GRID = 4
BLOCK = 4
BATCH_HEADS = 2
PAD = 16
VMEM_LIMIT = 48 * 1024 * 1024
GRADIENT_VMEM = 60 * 1024 * 1024

SMEM = pltpu.MemorySpace.SMEM
VMEM = pltpu.MemorySpace.VMEM
HBM = pltpu.MemorySpace.HBM


def place_in_block():
    doc, text = lax.axis_index("doc"), lax.axis_index("ctx")
    place = (text // GRID % 2) * 2 + text % GRID % 2
    return doc, jnp.where(doc % 2 == 0, place, 3 - place)


def pack_kernel(docs, slots_any, kv, out, slots, held, sems):
    fetch_slots = pltpu.make_async_copy(slots_any, slots, sems.at[docs])
    fetch = pltpu.make_async_copy(kv, held, sems.at[docs + 1])
    fetch_slots.start()
    fetch.start()
    fetch_slots.wait()
    doc, _ = place_in_block()
    copies = []
    for d in range(docs):
        local = 0
        for j in range(IMAGES):
            s = slots[d * IMAGES + j]
            local += jnp.where(s // IMAGES == doc, s % IMAGES, 0)
        copies.append(pltpu.make_async_copy(held.at[local], out.at[d], sems.at[d]))
    fetch.wait()
    for copy in copies:
        copy.start()
    for copy in copies:
        copy.wait()


def pick_kernel(slots, got, out):
    doc, _ = place_in_block()
    for j in range(IMAGES):
        rows = got[slots[doc * IMAGES + j] // IMAGES]
        heads = [
            jnp.concatenate(
                [
                    rows[:, c * WIDTH : (c + 1) * WIDTH],
                    rows[:, KEY_COLUMNS + c * WIDTH : KEY_COLUMNS + (c + 1) * WIDTH],
                ],
                axis=1,
            )
            for c in range(KV_HEADS)
        ]
        for y in range(GRID):
            for z in range(GRID):
                place = y % 2 * 2 + z % 2
                out[y * GRID + z, j] = jnp.where(doc % 2 == 0, heads[place], heads[3 - place])


def payload_kernel(q, d_out, spans_any, *refs):
    outs, held, spans, sems = refs[:BLOCK], refs[BLOCK], refs[BLOCK + 1], refs[BLOCK + 2]
    tokens = q.shape[0]
    width = q.shape[1] // KV_HEADS
    _, place = place_in_block()
    order = [3, 1, 2, 0]
    fetch_spans = pltpu.make_async_copy(spans_any, spans, sems.at[3 * BLOCK])
    fetch_spans.start()
    fetches = []
    for k in order:
        columns = pl.ds(pl.multiple_of((place ^ k) * width, WIDTH), width)
        pair = [
            pltpu.make_async_copy(q.at[:, columns], held.at[k, :tokens], sems.at[3 * k]),
            pltpu.make_async_copy(
                d_out.at[:, columns], held.at[k, tokens : 2 * tokens], sems.at[3 * k + 1]
            ),
        ]
        for copy in pair:
            copy.start()
        fetches.append(pair)
    fetch_spans.wait()
    for k in order:
        held[k, 2 * tokens :] = jnp.zeros_like(held[k, 2 * tokens :])
        held[k, 2 * tokens : 2 * tokens + 2, :tokens] = spans[...].astype(jnp.bfloat16)
    copies = []
    for k, pair in zip(order, fetches):
        for copy in pair:
            copy.wait()
        copies.append(pltpu.make_async_copy(held.at[k], outs[k], sems.at[3 * k + 2]))
        copies[-1].start()
    for copy in copies:
        copy.wait()


def merge_kernel(*refs):
    _, place = place_in_block()
    *parts, out = refs
    width = out.shape[1] // KV_HEADS
    for k, part in enumerate(parts):
        columns = pl.ds(pl.multiple_of((place ^ k) * width, WIDTH), width)
        out[:, columns] = part[...]


def softmax_gradients(scores, d_probs, seen):
    keys, rows = scores.shape
    scores = scores.reshape(-1, IMAGES, 16, rows)
    d_probs = d_probs.reshape(-1, IMAGES, 16, rows)
    row_max = None
    for j in range(IMAGES):
        top = jnp.max(jnp.max(scores[:, j], axis=0), axis=0, keepdims=True)
        top = jnp.where(seen[j], top, LOW)
        row_max = top if row_max is None else jnp.maximum(row_max, top)
    row_max = row_max * SCALE
    terms = []
    lows = []
    total = 0.0
    dots = 0.0
    for j in range(IMAGES):
        term = jnp.exp(scores[:, j] * SCALE - jnp.where(seen[j], row_max, -LOW))
        total += jnp.sum(jnp.sum(term, axis=0), axis=0, keepdims=True)
        dots += jnp.sum(jnp.sum(term * d_probs[:, j], axis=0), axis=0, keepdims=True)
        terms.append(term)
        lows.append(d_probs[:, j].astype(jnp.bfloat16))
    inverse = 1.0 / total
    delta = (dots * inverse).astype(jnp.bfloat16)
    low_probs = []
    d_scores = []
    for j in range(IMAGES):
        probs = (terms[j] * inverse).astype(jnp.bfloat16)
        low_probs.append(probs[:, None])
        d_scores.append((probs * (lows[j] - delta))[:, None])
    low_probs = jnp.concatenate(low_probs, axis=1).reshape(keys, rows)
    d_scores = jnp.concatenate(d_scores, axis=1).reshape(keys, rows)
    return low_probs, d_scores


def grad_kernel(count, first, last, gate, kv_any, *refs):
    pieces, refs = refs[:count], refs[count:]
    so_far, refs = (None, refs) if first else (refs[0], refs[1:])
    dqs, dkv_any, refs = refs[:count], refs[count], refs[count + 1 :]
    kv, held, dq, dkv, keys_t, probs, d_scores, q_rows, d_rows, acc, sems = refs
    tokens = dqs[0].shape[0]
    block = BATCH_HEADS * tokens
    fetch_kv = pltpu.make_async_copy(kv_any, kv, sems.at[2 * count])
    fetch_kv.start()
    for k in range(count):
        pltpu.make_async_copy(pieces[k], held.at[k], sems.at[k]).start()
    if not first:
        fetch_sums = pltpu.make_async_copy(so_far, acc, sems.at[2 * count + 1])
        fetch_sums.start()
    fetch_kv.wait()
    keys_t[...] = kv[:, :WIDTH].T
    if first:
        acc[...] = jnp.zeros_like(acc)
    else:
        fetch_sums.wait()
    factor = jnp.tanh(gate[...])
    transposed = (((1,), (1,)), ((), ()))

    def work(step, carry):
        pltpu.make_async_copy(pieces[0], held.at[step], sems.at[step]).wait()
        for h in range(GROUP):
            rows, columns = slice(h * tokens, (h + 1) * tokens), slice(h * WIDTH, (h + 1) * WIDTH)
            q_rows[rows] = held[step, :tokens, columns]
            wide = held[step, tokens : 2 * tokens, columns].astype(jnp.float32)
            d_rows[rows] = (wide * factor).astype(jnp.bfloat16)
        spans = held[step, 2 * tokens :, :tokens].astype(jnp.float32)
        low = jnp.concatenate([spans[0:1]] * BATCH_HEADS, axis=1)
        high = jnp.concatenate([spans[1:2]] * BATCH_HEADS, axis=1)
        seen = [(low <= j) & (j < high) for j in range(IMAGES)]
        for at in range(0, GROUP * tokens, block):
            rows = slice(at, at + block)
            scores = lax.dot_general(
                kv[:, :WIDTH], q_rows[rows], transposed, preferred_element_type=jnp.float32
            )
            d_probs = lax.dot_general(
                kv[:, WIDTH:], d_rows[rows], transposed, preferred_element_type=jnp.float32
            )
            probs[:, rows], d_scores[:, rows] = softmax_gradients(scores, d_probs, seen)
        acc[:, :WIDTH] += jnp.dot(d_scores[...], q_rows[...], preferred_element_type=jnp.float32)
        acc[:, WIDTH:] += jnp.dot(probs[...], d_rows[...], preferred_element_type=jnp.float32)
        dq_t = jnp.dot(keys_t[...], d_scores[...], preferred_element_type=jnp.float32) * SCALE
        dq_rows = dq_t.T.astype(jnp.bfloat16)
        for h in range(GROUP):
            dq[step, :, h * WIDTH : (h + 1) * WIDTH] = dq_rows[h * tokens : (h + 1) * tokens]
        for k in range(count):

            @pl.when(step == k)
            def _():
                pltpu.make_async_copy(dq.at[k], dqs[k], sems.at[count + k]).start()

        return carry

    lax.fori_loop(0, count, work, 0)
    if last:
        dkv[:, :WIDTH] = (acc[:, :WIDTH] * SCALE).astype(jnp.bfloat16)
        dkv[:, WIDTH:] = acc[:, WIDTH:].astype(jnp.bfloat16)
    give = pltpu.make_async_copy(dkv if last else acc, dkv_any, sems.at[2 * count])
    give.start()
    for k in range(count):
        pltpu.make_async_copy(dq.at[k], dqs[k], sems.at[count + k]).wait()
    give.wait()


def gradients(gate, kv, pieces, so_far=None, last=True):
    key_rows = kv.shape[0]
    count = len(pieces)
    first = so_far is None
    tokens = (pieces[0].shape[0] - PAD) // 2
    width = pieces[0].shape[1]
    rows = GROUP * tokens
    in_hbm = pl.BlockSpec(memory_space=HBM)
    operands = list(pieces) + ([] if first else [so_far])
    return pl.pallas_call(
        functools.partial(grad_kernel, count, first, last),
        in_specs=[pl.BlockSpec(memory_space=VMEM)] + [in_hbm] * (len(operands) + 1),
        out_specs=[in_hbm] * (count + 1),
        out_shape=[jax.ShapeDtypeStruct((tokens, width), jnp.bfloat16)] * count
        + [jax.ShapeDtypeStruct(kv.shape, jnp.bfloat16 if last else jnp.float32)],
        scratch_shapes=[
            pltpu.VMEM(kv.shape, jnp.bfloat16),
            pltpu.VMEM((count,) + pieces[0].shape, jnp.bfloat16),
            pltpu.VMEM((count, tokens, width), jnp.bfloat16),
            pltpu.VMEM(kv.shape, jnp.bfloat16),
            pltpu.VMEM((WIDTH, key_rows), jnp.bfloat16),
            pltpu.VMEM((key_rows, rows), jnp.bfloat16),
            pltpu.VMEM((key_rows, rows), jnp.bfloat16),
            pltpu.VMEM((rows, WIDTH), jnp.bfloat16),
            pltpu.VMEM((rows, WIDTH), jnp.bfloat16),
            pltpu.VMEM(kv.shape, jnp.float32),
            pltpu.SemaphoreType.DMA((2 * count + 2,)),
        ],
        compiler_params=pltpu.CompilerParams(vmem_limit_bytes=GRADIENT_VMEM),
        cost_estimate=pl.CostEstimate(
            flops=10 * count * rows * key_rows * WIDTH,
            bytes_accessed=4 * 1024 * 1024,
            transcendentals=count * rows * key_rows,
        ),
        name="gradients",
    )(gate, kv, *operands)


def sum_kernel(slots, got, out):
    doc, _ = place_in_block()
    out[...] = jnp.zeros_like(out)
    for j in range(IMAGES):
        owner = slots[doc * IMAGES + j] // IMAGES
        for c in range(KV_HEADS):
            total = 0.0
            place = jnp.where(doc % 2 == 0, c, 3 - c)
            for y in range(0, GRID, 2):
                for z in range(0, GRID, 2):
                    at = (place // 2 + y) * GRID + place % 2 + z
                    total += got[at, j].astype(jnp.float32)
            out[owner, :, c * WIDTH : (c + 1) * WIDTH] = total[:, :WIDTH].astype(jnp.bfloat16)
            out[owner, :, KEY_COLUMNS + c * WIDTH : KEY_COLUMNS + (c + 1) * WIDTH] = total[
                :, WIDTH:
            ].astype(jnp.bfloat16)


def place_kernel(docs, slots, got, out):
    doc_here, _ = place_in_block()
    for s in range(IMAGES):
        doc = 0
        for d in range(docs):
            for j in range(IMAGES):
                doc += jnp.where(slots[d * IMAGES + j] == doc_here * IMAGES + s, d, 0)
        out[s] = got[doc].astype(jnp.float32)


def small(kernel, out_shape, name):
    return pl.pallas_call(
        kernel,
        in_specs=[
            pl.BlockSpec(memory_space=SMEM),
            pl.BlockSpec(memory_space=VMEM),
        ],
        out_specs=pl.BlockSpec(memory_space=VMEM),
        out_shape=out_shape,
        compiler_params=pltpu.CompilerParams(vmem_limit_bytes=VMEM_LIMIT),
        name=name,
    )


def swap(docs, k):
    pairs = []
    for d in range(docs):
        for y in range(GRID):
            for z in range(GRID):
                v, w = (y + d % 2) ^ (k // 2), (z + d % 2) ^ (k % 2)
                to = (v - d % 2) % GRID * GRID + (w - d % 2) % GRID
                pairs.append((d * GRID * GRID + y * GRID + z, d * GRID * GRID + to))
    return pairs


def shards(queries, image_kv, d_out, attn_gate, image_slots, spans):
    docs = lax.axis_size("doc")
    texts = lax.axis_size("ctx")
    images, rows, columns = image_kv.shape
    tokens, width = queries.shape[1], queries.shape[2] // KV_HEADS
    both = ("doc", "ctx")
    in_hbm = pl.BlockSpec(memory_space=HBM)
    in_vmem = pl.BlockSpec(memory_space=VMEM)
    params = pltpu.CompilerParams(vmem_limit_bytes=VMEM_LIMIT)
    block = jax.ShapeDtypeStruct((docs, rows, columns), jnp.bfloat16)
    send = pl.pallas_call(
        functools.partial(pack_kernel, docs),
        in_specs=[in_hbm, in_hbm],
        out_specs=in_hbm,
        out_shape=block,
        scratch_shapes=[
            pltpu.SMEM(image_slots.shape, jnp.int32),
            pltpu.VMEM(image_kv.shape, jnp.bfloat16),
            pltpu.SemaphoreType.DMA((docs + 2,)),
        ],
        name="pack",
    )(image_slots, image_kv)
    got = lax.all_to_all(send, "doc", 0, 0)
    pieces = pl.pallas_call(
        payload_kernel,
        in_specs=[in_hbm, in_hbm, in_hbm],
        out_specs=[in_hbm] * BLOCK,
        out_shape=[jax.ShapeDtypeStruct((2 * tokens + PAD, width), jnp.bfloat16)] * BLOCK,
        scratch_shapes=[
            pltpu.VMEM((BLOCK, 2 * tokens + PAD, width), jnp.bfloat16),
            pltpu.VMEM((2, tokens), jnp.int32),
            pltpu.SemaphoreType.DMA((3 * BLOCK + 1,)),
        ],
        name="payload",
    )(queries[0], d_out[0], spans[0].T)
    one_head = jax.ShapeDtypeStruct((texts, images, rows, 2 * WIDTH), jnp.bfloat16)
    send = small(pick_kernel, one_head, "pick")(image_slots, got)
    pieces = [pieces[0]] + [lax.ppermute(pieces[k], both, swap(docs, k)) for k in range(1, BLOCK)]
    kv = lax.all_to_all(send, "ctx", 0, 0).reshape(texts * images * rows, 2 * WIDTH)
    *dqs, dkv = gradients(attn_gate.reshape(1, 1), kv, pieces)
    dqs = [dqs[0]] + [lax.ppermute(dqs[k], both, swap(docs, k)) for k in range(1, BLOCK)]
    parts = lax.all_to_all(dkv.reshape(texts, images, rows, 2 * WIDTH), "ctx", 0, 0)
    send = small(sum_kernel, block, "sum")(image_slots, parts)
    got = lax.all_to_all(send, "doc", 0, 0)
    d_image_kv = small(
        functools.partial(place_kernel, docs),
        jax.ShapeDtypeStruct(image_kv.shape, jnp.float32),
        "place",
    )(image_slots, got)
    d_queries = pl.pallas_call(
        merge_kernel,
        in_specs=[in_vmem] * BLOCK,
        out_specs=in_vmem,
        out_shape=jax.ShapeDtypeStruct(queries.shape[1:], jnp.bfloat16),
        compiler_params=params,
        name="merge",
    )(*dqs)
    return d_queries[None], d_image_kv


def solution(mesh):
    return jax.shard_map(
        shards,
        mesh=mesh,
        in_specs=(
            P("doc", "ctx", None),
            P("doc", "ctx", None),
            P("doc", "ctx", None),
            P(),
            P(),
            P("doc", "ctx", None),
        ),
        out_specs=(P("doc", "ctx", None), P("doc", "ctx", None)),
        check_vma=False,
    )
```

```python
import functools

import jax
import jax.numpy as jnp
from jax import lax
from jax.experimental import pallas as pl
from jax.experimental.pallas import tpu as pltpu
from jax.sharding import PartitionSpec as P

KV_HEADS = 4
WIDTH = 128
GROUP = 8
KEY_COLUMNS = 512
IMAGES = 4
LOW = -1e30
SCALE = WIDTH ** (-0.5)
LOG2E = 1.4426950408889634
GRID = 4
BLOCK = 4
BATCH_HEADS = 2
PAD = 16
VMEM_LIMIT = 48 * 1024 * 1024
GRADIENT_VMEM = 60 * 1024 * 1024

SMEM = pltpu.MemorySpace.SMEM
VMEM = pltpu.MemorySpace.VMEM
HBM = pltpu.MemorySpace.HBM


def place_in_block():
    doc, text = lax.axis_index("doc"), lax.axis_index("ctx")
    place = (text // GRID % 2) * 2 + text % GRID % 2
    return doc, jnp.where(doc % 2 == 0, place, 3 - place)


def pack_kernel(docs, slots_any, kv, out, slots, held, sems):
    fetch_slots = pltpu.make_async_copy(slots_any, slots, sems.at[docs])
    fetch = pltpu.make_async_copy(kv, held, sems.at[docs + 1])
    fetch_slots.start()
    fetch.start()
    fetch_slots.wait()
    doc, _ = place_in_block()
    copies = []
    for d in range(docs):
        local = 0
        for j in range(IMAGES):
            s = slots[d * IMAGES + j]
            local += jnp.where(s // IMAGES == doc, s % IMAGES, 0)
        copies.append(pltpu.make_async_copy(held.at[local], out.at[d], sems.at[d]))
    fetch.wait()
    for copy in copies:
        copy.start()
    for copy in copies:
        copy.wait()


def pick_kernel(slots, got, out):
    doc, _ = place_in_block()
    for j in range(IMAGES):
        rows = got[slots[doc * IMAGES + j] // IMAGES]
        heads = [
            jnp.concatenate(
                [
                    rows[:, c * WIDTH : (c + 1) * WIDTH],
                    rows[:, KEY_COLUMNS + c * WIDTH : KEY_COLUMNS + (c + 1) * WIDTH],
                ],
                axis=1,
            )
            for c in range(KV_HEADS)
        ]
        for y in range(GRID):
            for z in range(GRID):
                place = y % 2 * 2 + z % 2
                out[y * GRID + z, j] = jnp.where(doc % 2 == 0, heads[place], heads[3 - place])


def payload_kernel(q, d_out, spans_any, *refs):
    outs, held, spans, sems = refs[:BLOCK], refs[BLOCK], refs[BLOCK + 1], refs[BLOCK + 2]
    tokens = q.shape[0]
    width = q.shape[1] // KV_HEADS
    _, place = place_in_block()
    order = [3, 1, 2, 0]
    fetch_spans = pltpu.make_async_copy(spans_any, spans, sems.at[3 * BLOCK])
    fetch_spans.start()
    fetches = []
    for k in order:
        columns = pl.ds(pl.multiple_of((place ^ k) * width, WIDTH), width)
        pair = [
            pltpu.make_async_copy(q.at[:, columns], held.at[k, :tokens], sems.at[3 * k]),
            pltpu.make_async_copy(
                d_out.at[:, columns], held.at[k, tokens : 2 * tokens], sems.at[3 * k + 1]
            ),
        ]
        for copy in pair:
            copy.start()
        fetches.append(pair)
    fetch_spans.wait()
    for k in order:
        held[k, 2 * tokens :] = jnp.zeros_like(held[k, 2 * tokens :])
        held[k, 2 * tokens : 2 * tokens + 2, :tokens] = spans[...].astype(jnp.bfloat16)
    copies = []
    for k, pair in zip(order, fetches):
        for copy in pair:
            copy.wait()
        copies.append(pltpu.make_async_copy(held.at[k], outs[k], sems.at[3 * k + 2]))
        copies[-1].start()
    for copy in copies:
        copy.wait()


def merge_kernel(*refs):
    _, place = place_in_block()
    *parts, out = refs
    width = out.shape[1] // KV_HEADS
    for k, part in enumerate(parts):
        columns = pl.ds(pl.multiple_of((place ^ k) * width, WIDTH), width)
        out[:, columns] = part[...]


def softmax_gradients(scores, d_probs, seen):
    keys, rows = scores.shape
    scores = scores.reshape(-1, IMAGES, 16, rows)
    d_probs = d_probs.reshape(-1, IMAGES, 16, rows)
    row_max = None
    for j in range(IMAGES):
        top = jnp.max(jnp.max(scores[:, j], axis=0), axis=0, keepdims=True)
        top = jnp.where(seen[j], top, LOW)
        row_max = top if row_max is None else jnp.maximum(row_max, top)
    row_max = row_max * SCALE
    terms = []
    lows = []
    total = 0.0
    dots = 0.0
    for j in range(IMAGES):
        term = jnp.exp(scores[:, j] * SCALE - jnp.where(seen[j], row_max, -LOW))
        total += jnp.sum(jnp.sum(term, axis=0), axis=0, keepdims=True)
        dots += jnp.sum(jnp.sum(term * d_probs[:, j], axis=0), axis=0, keepdims=True)
        terms.append(term)
        lows.append(d_probs[:, j].astype(jnp.bfloat16))
    inverse = 1.0 / total
    delta = (dots * inverse).astype(jnp.bfloat16)
    low_probs = []
    d_scores = []
    for j in range(IMAGES):
        probs = (terms[j] * inverse).astype(jnp.bfloat16)
        low_probs.append(probs[:, None])
        d_scores.append((probs * (lows[j] - delta))[:, None])
    low_probs = jnp.concatenate(low_probs, axis=1).reshape(keys, rows)
    d_scores = jnp.concatenate(d_scores, axis=1).reshape(keys, rows)
    return low_probs, d_scores


def grad_kernel(count, first, last, gate, kv_any, *refs):
    pieces, refs = refs[:count], refs[count:]
    so_far, refs = (None, refs) if first else (refs[0], refs[1:])
    dqs, dkv_any, refs = refs[:count], refs[count], refs[count + 1 :]
    kv, held, dq, dkv, keys_t, probs, d_scores, q_rows, d_rows, acc, sems = refs
    tokens = dqs[0].shape[0]
    block = BATCH_HEADS * tokens
    fetch_kv = pltpu.make_async_copy(kv_any, kv, sems.at[2 * count])
    fetch_kv.start()
    for k in range(count):
        pltpu.make_async_copy(pieces[k], held.at[k], sems.at[k]).start()
    if not first:
        fetch_sums = pltpu.make_async_copy(so_far, acc, sems.at[2 * count + 1])
        fetch_sums.start()
    fetch_kv.wait()
    keys_t[...] = kv[:, :WIDTH].T
    if first:
        acc[...] = jnp.zeros_like(acc)
    else:
        fetch_sums.wait()
    factor = jnp.tanh(gate[...])
    transposed = (((1,), (1,)), ((), ()))

    def work(step, carry):
        pltpu.make_async_copy(pieces[0], held.at[step], sems.at[step]).wait()
        for h in range(GROUP):
            rows, columns = slice(h * tokens, (h + 1) * tokens), slice(h * WIDTH, (h + 1) * WIDTH)
            q_rows[rows] = held[step, :tokens, columns]
            wide = held[step, tokens : 2 * tokens, columns].astype(jnp.float32)
            d_rows[rows] = (wide * factor).astype(jnp.bfloat16)
        spans = held[step, 2 * tokens :, :tokens].astype(jnp.float32)
        low = jnp.concatenate([spans[0:1]] * BATCH_HEADS, axis=1)
        high = jnp.concatenate([spans[1:2]] * BATCH_HEADS, axis=1)
        seen = [(low <= j) & (j < high) for j in range(IMAGES)]
        for at in range(0, GROUP * tokens, block):
            rows = slice(at, at + block)
            scores = lax.dot_general(
                kv[:, :WIDTH], q_rows[rows], transposed, preferred_element_type=jnp.float32
            )
            d_probs = lax.dot_general(
                kv[:, WIDTH:], d_rows[rows], transposed, preferred_element_type=jnp.float32
            )
            probs[:, rows], d_scores[:, rows] = softmax_gradients(scores, d_probs, seen)
        acc[:, :WIDTH] += jnp.dot(d_scores[...], q_rows[...], preferred_element_type=jnp.float32)
        acc[:, WIDTH:] += jnp.dot(probs[...], d_rows[...], preferred_element_type=jnp.float32)
        dq_t = jnp.dot(keys_t[...], d_scores[...], preferred_element_type=jnp.float32) * SCALE
        dq_rows = dq_t.T.astype(jnp.bfloat16)
        for h in range(GROUP):
            dq[step, :, h * WIDTH : (h + 1) * WIDTH] = dq_rows[h * tokens : (h + 1) * tokens]
        for k in range(count):

            @pl.when(step == k)
            def _():
                pltpu.make_async_copy(dq.at[k], dqs[k], sems.at[count + k]).start()

        return carry

    lax.fori_loop(0, count, work, 0)
    if last:
        dkv[:, :WIDTH] = (acc[:, :WIDTH] * SCALE).astype(jnp.bfloat16)
        dkv[:, WIDTH:] = acc[:, WIDTH:].astype(jnp.bfloat16)
    give = pltpu.make_async_copy(dkv if last else acc, dkv_any, sems.at[2 * count])
    give.start()
    for k in range(count):
        pltpu.make_async_copy(dq.at[k], dqs[k], sems.at[count + k]).wait()
    give.wait()


def gradients(gate, kv, pieces, so_far=None, last=True):
    key_rows = kv.shape[0]
    count = len(pieces)
    first = so_far is None
    tokens = (pieces[0].shape[0] - PAD) // 2
    width = pieces[0].shape[1]
    rows = GROUP * tokens
    in_hbm = pl.BlockSpec(memory_space=HBM)
    operands = list(pieces) + ([] if first else [so_far])
    return pl.pallas_call(
        functools.partial(grad_kernel, count, first, last),
        in_specs=[pl.BlockSpec(memory_space=VMEM)] + [in_hbm] * (len(operands) + 1),
        out_specs=[in_hbm] * (count + 1),
        out_shape=[jax.ShapeDtypeStruct((tokens, width), jnp.bfloat16)] * count
        + [jax.ShapeDtypeStruct(kv.shape, jnp.bfloat16 if last else jnp.float32)],
        scratch_shapes=[
            pltpu.VMEM(kv.shape, jnp.bfloat16),
            pltpu.VMEM((count,) + pieces[0].shape, jnp.bfloat16),
            pltpu.VMEM((count, tokens, width), jnp.bfloat16),
            pltpu.VMEM(kv.shape, jnp.bfloat16),
            pltpu.VMEM((WIDTH, key_rows), jnp.bfloat16),
            pltpu.VMEM((key_rows, rows), jnp.bfloat16),
            pltpu.VMEM((key_rows, rows), jnp.bfloat16),
            pltpu.VMEM((rows, WIDTH), jnp.bfloat16),
            pltpu.VMEM((rows, WIDTH), jnp.bfloat16),
            pltpu.VMEM(kv.shape, jnp.float32),
            pltpu.SemaphoreType.DMA((2 * count + 2,)),
        ],
        compiler_params=pltpu.CompilerParams(vmem_limit_bytes=GRADIENT_VMEM),
        cost_estimate=pl.CostEstimate(
            flops=10 * count * rows * key_rows * WIDTH,
            bytes_accessed=4 * 1024 * 1024,
            transcendentals=count * rows * key_rows,
        ),
        name="gradients",
    )(gate, kv, *operands)


def sum_kernel(slots, got, out):
    doc, _ = place_in_block()
    out[...] = jnp.zeros_like(out)
    for j in range(IMAGES):
        owner = slots[doc * IMAGES + j] // IMAGES
        for c in range(KV_HEADS):
            total = 0.0
            place = jnp.where(doc % 2 == 0, c, 3 - c)
            for y in range(0, GRID, 2):
                for z in range(0, GRID, 2):
                    at = (place // 2 + y) * GRID + place % 2 + z
                    total += got[at, j].astype(jnp.float32)
            out[owner, :, c * WIDTH : (c + 1) * WIDTH] = total[:, :WIDTH].astype(jnp.bfloat16)
            out[owner, :, KEY_COLUMNS + c * WIDTH : KEY_COLUMNS + (c + 1) * WIDTH] = total[
                :, WIDTH:
            ].astype(jnp.bfloat16)


def place_kernel(docs, slots, got, out):
    doc_here, _ = place_in_block()
    for s in range(IMAGES):
        doc = 0
        for d in range(docs):
            for j in range(IMAGES):
                doc += jnp.where(slots[d * IMAGES + j] == doc_here * IMAGES + s, d, 0)
        out[s] = got[doc].astype(jnp.float32)


def small(kernel, out_shape, name):
    return pl.pallas_call(
        kernel,
        in_specs=[
            pl.BlockSpec(memory_space=SMEM),
            pl.BlockSpec(memory_space=VMEM),
        ],
        out_specs=pl.BlockSpec(memory_space=VMEM),
        out_shape=out_shape,
        compiler_params=pltpu.CompilerParams(vmem_limit_bytes=VMEM_LIMIT),
        name=name,
    )


def swap(docs, k):
    pairs = []
    for d in range(docs):
        for y in range(GRID):
            for z in range(GRID):
                v, w = (y + d % 2) ^ (k // 2), (z + d % 2) ^ (k % 2)
                to = (v - d % 2) % GRID * GRID + (w - d % 2) % GRID
                pairs.append((d * GRID * GRID + y * GRID + z, d * GRID * GRID + to))
    return pairs


def shards(queries, image_kv, d_out, attn_gate, image_slots, spans):
    docs = lax.axis_size("doc")
    texts = lax.axis_size("ctx")
    images, rows, columns = image_kv.shape
    tokens, width = queries.shape[1], queries.shape[2] // KV_HEADS
    both = ("doc", "ctx")
    in_hbm = pl.BlockSpec(memory_space=HBM)
    in_vmem = pl.BlockSpec(memory_space=VMEM)
    params = pltpu.CompilerParams(vmem_limit_bytes=VMEM_LIMIT)
    block = jax.ShapeDtypeStruct((docs, rows, columns), jnp.bfloat16)
    send = pl.pallas_call(
        functools.partial(pack_kernel, docs),
        in_specs=[in_hbm, in_hbm],
        out_specs=in_hbm,
        out_shape=block,
        scratch_shapes=[
            pltpu.SMEM(image_slots.shape, jnp.int32),
            pltpu.VMEM(image_kv.shape, jnp.bfloat16),
            pltpu.SemaphoreType.DMA((docs + 2,)),
        ],
        name="pack",
    )(image_slots, image_kv)
    got = lax.all_to_all(send, "doc", 0, 0)
    pieces = pl.pallas_call(
        payload_kernel,
        in_specs=[in_hbm, in_hbm, in_hbm],
        out_specs=[in_hbm] * BLOCK,
        out_shape=[jax.ShapeDtypeStruct((2 * tokens + PAD, width), jnp.bfloat16)] * BLOCK,
        scratch_shapes=[
            pltpu.VMEM((BLOCK, 2 * tokens + PAD, width), jnp.bfloat16),
            pltpu.VMEM((2, tokens), jnp.int32),
            pltpu.SemaphoreType.DMA((3 * BLOCK + 1,)),
        ],
        name="payload",
    )(queries[0], d_out[0], spans[0].T)
    one_head = jax.ShapeDtypeStruct((texts, images, rows, 2 * WIDTH), jnp.bfloat16)
    send = small(pick_kernel, one_head, "pick")(image_slots, got)
    own, *others = pieces
    beside, above = [lax.ppermute(others[k - 1], both, swap(docs, k)) for k in (1, 2)]
    across, send = lax.optimization_barrier((others[2], send))
    across = lax.ppermute(across, both, swap(docs, 3))
    kv = lax.all_to_all(send, "ctx", 0, 0).reshape(texts * images * rows, 2 * WIDTH)
    gate = attn_gate.reshape(1, 1)
    dq_own, dq_beside, dq_above, sums = gradients(gate, kv, [own, beside, above], last=False)
    dq_across, dkv = gradients(gate, kv, [across], so_far=sums)
    dq_beside = lax.ppermute(dq_beside, both, swap(docs, 1))
    dq_above = lax.ppermute(dq_above, both, swap(docs, 2))
    dq_across = lax.ppermute(dq_across, both, swap(docs, 3))
    parts = lax.all_to_all(dkv.reshape(texts, images, rows, 2 * WIDTH), "ctx", 0, 0)
    send = small(sum_kernel, block, "sum")(image_slots, parts)
    got = lax.all_to_all(send, "doc", 0, 0)
    dqs = [dq_own, dq_beside, dq_above, dq_across]
    d_image_kv = small(
        functools.partial(place_kernel, docs),
        jax.ShapeDtypeStruct(image_kv.shape, jnp.float32),
        "place",
    )(image_slots, got)
    d_queries = pl.pallas_call(
        merge_kernel,
        in_specs=[in_vmem] * BLOCK,
        out_specs=in_vmem,
        out_shape=jax.ShapeDtypeStruct(queries.shape[1:], jnp.bfloat16),
        compiler_params=params,
        name="merge",
    )(*dqs)
    return d_queries[None], d_image_kv


def solution(mesh):
    return jax.shard_map(
        shards,
        mesh=mesh,
        in_specs=(
            P("doc", "ctx", None),
            P("doc", "ctx", None),
            P("doc", "ctx", None),
            P(),
            P(),
            P("doc", "ctx", None),
        ),
        out_specs=(P("doc", "ctx", None), P("doc", "ctx", None)),
        check_vma=False,
    )
```

```python
import functools

import jax
import jax.numpy as jnp
from jax import lax
from jax.experimental import pallas as pl
from jax.experimental.pallas import tpu as pltpu
from jax.sharding import PartitionSpec as P

KV_HEADS = 4
WIDTH = 128
GROUP = 8
KEY_COLUMNS = 512
IMAGES = 4
LOW = -1e30
SCALE = WIDTH ** (-0.5)
LOG2E = 1.4426950408889634
GRID = 4
BLOCK = 4
BATCH_HEADS = 2
PAD = 16
VMEM_LIMIT = 48 * 1024 * 1024
GRADIENT_VMEM = 60 * 1024 * 1024

SMEM = pltpu.MemorySpace.SMEM
VMEM = pltpu.MemorySpace.VMEM
HBM = pltpu.MemorySpace.HBM


def place_in_block():
    doc, text = lax.axis_index("doc"), lax.axis_index("ctx")
    place = (text // GRID % 2) * 2 + text % GRID % 2
    return doc, jnp.where(doc % 2 == 0, place, 3 - place)


def prepare_kernel(docs, slots_any, kv, q, d_out, spans_any, *refs):
    send, pieces, (slots, rows, held, spans, sems) = refs[0], refs[1:BLOCK], refs[BLOCK:]
    tokens = q.shape[0]
    width = q.shape[1] // KV_HEADS
    doc, place = place_in_block()
    fetch_slots = pltpu.make_async_copy(slots_any, slots, sems.at[docs])
    fetch_rows = pltpu.make_async_copy(kv, rows, sems.at[docs + 1])
    fetch_spans = pltpu.make_async_copy(spans_any, spans, sems.at[docs + 2])
    fetch_slots.start()
    fetch_rows.start()
    fetch_spans.start()
    at = docs + 3
    fetches = []
    for k in range(1, BLOCK):
        columns = pl.ds(pl.multiple_of((place ^ k) * width, WIDTH), width)
        pair = [
            pltpu.make_async_copy(q.at[:, columns], held.at[k - 1, :tokens], sems.at[at]),
            pltpu.make_async_copy(
                d_out.at[:, columns], held.at[k - 1, tokens : 2 * tokens], sems.at[at + 1]
            ),
        ]
        for copy in pair:
            copy.start()
        fetches.append(pair)
        at += 2
    fetch_slots.wait()
    copies = []
    for d in range(docs):
        local = 0
        for j in range(IMAGES):
            s = slots[d * IMAGES + j]
            local += jnp.where(s // IMAGES == doc, s % IMAGES, 0)
        copies.append(pltpu.make_async_copy(rows.at[local], send.at[d], sems.at[d]))
    fetch_rows.wait()
    for copy in copies:
        copy.start()
    fetch_spans.wait()
    for k in range(1, BLOCK):
        held[k - 1, 2 * tokens :] = jnp.zeros_like(held[k - 1, 2 * tokens :])
        held[k - 1, 2 * tokens : 2 * tokens + 2, :tokens] = spans[...].astype(jnp.bfloat16)
    for k, pair in zip(range(1, BLOCK), fetches):
        for copy in pair:
            copy.wait()
        copies.append(pltpu.make_async_copy(held.at[k - 1], pieces[k - 1], sems.at[at]))
        copies[-1].start()
        at += 1
    for copy in copies:
        copy.wait()


def pick_kernel(slots, got, out, heads):
    doc, _ = place_in_block()
    for j in range(IMAGES):
        owner = slots[doc * IMAGES + j] // IMAGES
        for c in range(KV_HEADS):
            columns = slice(c * WIDTH, (c + 1) * WIDTH)
            heads[c, j, :, :WIDTH] = got[owner, :, columns]
            columns = slice(KEY_COLUMNS + c * WIDTH, KEY_COLUMNS + (c + 1) * WIDTH)
            heads[c, j, :, WIDTH:] = got[owner, :, columns]
    for y in range(GRID):
        for z in range(GRID):
            place = y % 2 * 2 + z % 2
            out[y * GRID + z] = heads[jnp.where(doc % 2 == 0, place, 3 - place)]


def merge_kernel(*refs):
    _, place = place_in_block()
    *parts, out = refs
    width = out.shape[1] // KV_HEADS
    for k, part in enumerate(parts):
        columns = pl.ds(pl.multiple_of((place ^ k) * width, WIDTH), width)
        out[:, columns] = part[...]


def softmax_gradients(scores, d_probs, seen):
    keys, rows = scores.shape
    scores = scores.reshape(-1, IMAGES, 16, rows)
    d_probs = d_probs.reshape(-1, IMAGES, 16, rows)
    row_max = None
    for j in range(IMAGES):
        top = jnp.max(jnp.max(scores[:, j], axis=0), axis=0, keepdims=True)
        top = jnp.where(seen[j], top, LOW)
        row_max = top if row_max is None else jnp.maximum(row_max, top)
    row_max = row_max * SCALE
    terms = []
    lows = []
    total = 0.0
    dots = 0.0
    for j in range(IMAGES):
        term = jnp.exp(scores[:, j] * SCALE - jnp.where(seen[j], row_max, -LOW))
        total += jnp.sum(jnp.sum(term, axis=0), axis=0, keepdims=True)
        dots += jnp.sum(jnp.sum(term * d_probs[:, j], axis=0), axis=0, keepdims=True)
        terms.append(term)
        lows.append(d_probs[:, j].astype(jnp.bfloat16))
    inverse = 1.0 / total
    delta = (dots * inverse).astype(jnp.bfloat16)
    low_probs = []
    d_scores = []
    for j in range(IMAGES):
        probs = (terms[j] * inverse).astype(jnp.bfloat16)
        low_probs.append(probs[:, None])
        d_scores.append((probs * (lows[j] - delta))[:, None])
    low_probs = jnp.concatenate(low_probs, axis=1).reshape(keys, rows)
    d_scores = jnp.concatenate(d_scores, axis=1).reshape(keys, rows)
    return low_probs, d_scores


def grad_kernel(gate, kv_any, q, d_out, spans_any, *refs):
    pieces, dqs, dkv_any, refs = refs[: BLOCK - 1], refs[BLOCK - 1 : 2 * BLOCK - 1], refs[2 * BLOCK - 1], refs[2 * BLOCK :]
    kv, held, own_spans, dq, dkv, keys_t, probs, d_scores, q_rows, d_rows, acc, sems = refs
    tokens = dqs[0].shape[0]
    width = dqs[0].shape[1]
    block = BATCH_HEADS * tokens
    _, place = place_in_block()
    fetch_kv = pltpu.make_async_copy(kv_any, kv, sems.at[2 * BLOCK])
    fetch_kv.start()
    columns = pl.ds(pl.multiple_of(place * width, WIDTH), width)
    fetch_own = [
        pltpu.make_async_copy(q.at[:, columns], held.at[0, :tokens], sems.at[0]),
        pltpu.make_async_copy(
            d_out.at[:, columns], held.at[0, tokens : 2 * tokens], sems.at[2 * BLOCK + 1]
        ),
        pltpu.make_async_copy(spans_any, own_spans, sems.at[2 * BLOCK + 2]),
    ]
    for copy in fetch_own:
        copy.start()
    for k in range(1, BLOCK):
        pltpu.make_async_copy(pieces[k - 1], held.at[k], sems.at[k]).start()
    acc[...] = jnp.zeros_like(acc)
    fetch_kv.wait()
    keys_t[...] = kv[:, :WIDTH].T
    for copy in fetch_own:
        copy.wait()
    held[0, 2 * tokens :] = jnp.zeros_like(held[0, 2 * tokens :])
    held[0, 2 * tokens : 2 * tokens + 2, :tokens] = own_spans[...].astype(jnp.bfloat16)
    factor = jnp.tanh(gate[...])
    transposed = (((1,), (1,)), ((), ()))

    def work(step, carry):
        @pl.when(step > 0)
        def _():
            pltpu.make_async_copy(pieces[0], held.at[step], sems.at[step]).wait()

        for h in range(GROUP):
            rows, columns = slice(h * tokens, (h + 1) * tokens), slice(h * WIDTH, (h + 1) * WIDTH)
            q_rows[rows] = held[step, :tokens, columns]
            wide = held[step, tokens : 2 * tokens, columns].astype(jnp.float32)
            d_rows[rows] = (wide * factor).astype(jnp.bfloat16)
        spans = held[step, 2 * tokens :, :tokens].astype(jnp.float32)
        low = jnp.concatenate([spans[0:1]] * BATCH_HEADS, axis=1)
        high = jnp.concatenate([spans[1:2]] * BATCH_HEADS, axis=1)
        seen = [(low <= j) & (j < high) for j in range(IMAGES)]
        for at in range(0, GROUP * tokens, block):
            rows = slice(at, at + block)
            scores = lax.dot_general(
                kv[:, :WIDTH], q_rows[rows], transposed, preferred_element_type=jnp.float32
            )
            d_probs = lax.dot_general(
                kv[:, WIDTH:], d_rows[rows], transposed, preferred_element_type=jnp.float32
            )
            probs[:, rows], d_scores[:, rows] = softmax_gradients(scores, d_probs, seen)
        acc[:, :WIDTH] += jnp.dot(d_scores[...], q_rows[...], preferred_element_type=jnp.float32)
        acc[:, WIDTH:] += jnp.dot(probs[...], d_rows[...], preferred_element_type=jnp.float32)
        dq_t = jnp.dot(keys_t[...], d_scores[...], preferred_element_type=jnp.float32) * SCALE
        dq_rows = dq_t.T.astype(jnp.bfloat16)
        for h in range(GROUP):
            dq[step, :, h * WIDTH : (h + 1) * WIDTH] = dq_rows[h * tokens : (h + 1) * tokens]
        for k in range(BLOCK):

            @pl.when(step == k)
            def _():
                pltpu.make_async_copy(dq.at[k], dqs[k], sems.at[BLOCK + k]).start()

        return carry

    lax.fori_loop(0, BLOCK, work, 0)
    dkv[:, :WIDTH] = (acc[:, :WIDTH] * SCALE).astype(jnp.bfloat16)
    dkv[:, WIDTH:] = acc[:, WIDTH:].astype(jnp.bfloat16)
    give = pltpu.make_async_copy(dkv, dkv_any, sems.at[2 * BLOCK])
    give.start()
    for k in range(BLOCK):
        pltpu.make_async_copy(dq.at[k], dqs[k], sems.at[BLOCK + k]).wait()
    give.wait()


def gradients(gate, kv, q, d_out, spans, pieces):
    key_rows = kv.shape[0]
    tokens = q.shape[0]
    width = pieces[0].shape[1]
    rows = GROUP * tokens
    in_hbm = pl.BlockSpec(memory_space=HBM)
    return pl.pallas_call(
        grad_kernel,
        in_specs=[pl.BlockSpec(memory_space=VMEM)] + [in_hbm] * (BLOCK + 3),
        out_specs=[in_hbm] * (BLOCK + 1),
        out_shape=[jax.ShapeDtypeStruct((tokens, width), jnp.bfloat16)] * BLOCK
        + [jax.ShapeDtypeStruct(kv.shape, jnp.bfloat16)],
        scratch_shapes=[
            pltpu.VMEM(kv.shape, jnp.bfloat16),
            pltpu.VMEM((BLOCK,) + pieces[0].shape, jnp.bfloat16),
            pltpu.VMEM(spans.shape, jnp.int32),
            pltpu.VMEM((BLOCK, tokens, width), jnp.bfloat16),
            pltpu.VMEM(kv.shape, jnp.bfloat16),
            pltpu.VMEM((WIDTH, key_rows), jnp.bfloat16),
            pltpu.VMEM((key_rows, rows), jnp.bfloat16),
            pltpu.VMEM((key_rows, rows), jnp.bfloat16),
            pltpu.VMEM((rows, WIDTH), jnp.bfloat16),
            pltpu.VMEM((rows, WIDTH), jnp.bfloat16),
            pltpu.VMEM(kv.shape, jnp.float32),
            pltpu.SemaphoreType.DMA((2 * BLOCK + 3,)),
        ],
        compiler_params=pltpu.CompilerParams(vmem_limit_bytes=GRADIENT_VMEM),
        cost_estimate=pl.CostEstimate(
            flops=10 * BLOCK * rows * key_rows * WIDTH,
            bytes_accessed=4 * 1024 * 1024,
            transcendentals=BLOCK * rows * key_rows,
        ),
        name="gradients",
    )(gate, kv, q, d_out, spans, *pieces)


def sum_kernel(slots, got, out):
    doc, _ = place_in_block()
    out[...] = jnp.zeros_like(out)
    for j in range(IMAGES):
        owner = slots[doc * IMAGES + j] // IMAGES
        for c in range(KV_HEADS):
            total = 0.0
            place = jnp.where(doc % 2 == 0, c, 3 - c)
            for y in range(0, GRID, 2):
                for z in range(0, GRID, 2):
                    at = (place // 2 + y) * GRID + place % 2 + z
                    total += got[at, j].astype(jnp.float32)
            out[owner, :, c * WIDTH : (c + 1) * WIDTH] = total[:, :WIDTH].astype(jnp.bfloat16)
            out[owner, :, KEY_COLUMNS + c * WIDTH : KEY_COLUMNS + (c + 1) * WIDTH] = total[
                :, WIDTH:
            ].astype(jnp.bfloat16)


def place_kernel(docs, slots, got, out):
    doc_here, _ = place_in_block()
    for s in range(IMAGES):
        doc = 0
        for d in range(docs):
            for j in range(IMAGES):
                doc += jnp.where(slots[d * IMAGES + j] == doc_here * IMAGES + s, d, 0)
        out[s] = got[doc].astype(jnp.float32)


def small(kernel, out_shape, name, scratch=()):
    return pl.pallas_call(
        kernel,
        in_specs=[
            pl.BlockSpec(memory_space=SMEM),
            pl.BlockSpec(memory_space=VMEM),
        ],
        out_specs=pl.BlockSpec(memory_space=VMEM),
        out_shape=out_shape,
        scratch_shapes=scratch,
        compiler_params=pltpu.CompilerParams(vmem_limit_bytes=VMEM_LIMIT),
        name=name,
    )


def swap(docs, k):
    pairs = []
    for d in range(docs):
        for y in range(GRID):
            for z in range(GRID):
                v, w = (y + d % 2) ^ (k // 2), (z + d % 2) ^ (k % 2)
                to = (v - d % 2) % GRID * GRID + (w - d % 2) % GRID
                pairs.append((d * GRID * GRID + y * GRID + z, d * GRID * GRID + to))
    return pairs


def shards(queries, image_kv, d_out, attn_gate, image_slots, spans):
    docs = lax.axis_size("doc")
    texts = lax.axis_size("ctx")
    images, rows, columns = image_kv.shape
    tokens, width = queries.shape[1], queries.shape[2] // KV_HEADS
    both = ("doc", "ctx")
    in_hbm = pl.BlockSpec(memory_space=HBM)
    in_vmem = pl.BlockSpec(memory_space=VMEM)
    params = pltpu.CompilerParams(vmem_limit_bytes=VMEM_LIMIT)
    block = jax.ShapeDtypeStruct((docs, rows, columns), jnp.bfloat16)
    span_rows = spans[0].T
    piece = jax.ShapeDtypeStruct((2 * tokens + PAD, width), jnp.bfloat16)
    send, *pieces = pl.pallas_call(
        functools.partial(prepare_kernel, docs),
        in_specs=[in_hbm] * 5,
        out_specs=[in_hbm] * BLOCK,
        out_shape=[block] + [piece] * (BLOCK - 1),
        scratch_shapes=[
            pltpu.SMEM(image_slots.shape, jnp.int32),
            pltpu.VMEM(image_kv.shape, jnp.bfloat16),
            pltpu.VMEM((BLOCK - 1,) + piece.shape, jnp.bfloat16),
            pltpu.VMEM(span_rows.shape, jnp.int32),
            pltpu.SemaphoreType.DMA((docs + 3 * BLOCK,)),
        ],
        name="prepare",
    )(image_slots, image_kv, queries[0], d_out[0], span_rows)
    got = lax.all_to_all(send, "doc", 0, 0)
    one_head = jax.ShapeDtypeStruct((texts, images, rows, 2 * WIDTH), jnp.bfloat16)
    send = small(
        pick_kernel,
        one_head,
        "pick",
        [pltpu.VMEM((KV_HEADS, images, rows, 2 * WIDTH), jnp.bfloat16)],
    )(image_slots, got)
    pieces = [lax.ppermute(pieces[k - 1], both, swap(docs, k)) for k in range(1, BLOCK)]
    kv = lax.all_to_all(send, "ctx", 0, 0).reshape(texts * images * rows, 2 * WIDTH)
    *dqs, dkv = gradients(
        attn_gate.reshape(1, 1), kv, queries[0], d_out[0], span_rows, pieces
    )
    dqs = [dqs[0]] + [lax.ppermute(dqs[k], both, swap(docs, k)) for k in range(1, BLOCK)]
    parts = lax.all_to_all(dkv.reshape(texts, images, rows, 2 * WIDTH), "ctx", 0, 0)
    send = small(sum_kernel, block, "sum")(image_slots, parts)
    got = lax.all_to_all(send, "doc", 0, 0)
    d_image_kv = small(
        functools.partial(place_kernel, docs),
        jax.ShapeDtypeStruct(image_kv.shape, jnp.float32),
        "place",
    )(image_slots, got)
    d_queries = pl.pallas_call(
        merge_kernel,
        in_specs=[in_vmem] * BLOCK,
        out_specs=in_vmem,
        out_shape=jax.ShapeDtypeStruct(queries.shape[1:], jnp.bfloat16),
        compiler_params=params,
        name="merge",
    )(*dqs)
    return d_queries[None], d_image_kv


def solution(mesh):
    return jax.shard_map(
        shards,
        mesh=mesh,
        in_specs=(
            P("doc", "ctx", None),
            P("doc", "ctx", None),
            P("doc", "ctx", None),
            P(),
            P(),
            P("doc", "ctx", None),
        ),
        out_specs=(P("doc", "ctx", None), P("doc", "ctx", None)),
        check_vma=False,
    )
```

```python
import functools

import jax
import jax.numpy as jnp
from jax import lax
from jax.experimental import pallas as pl
from jax.experimental.pallas import tpu as pltpu
from jax.sharding import PartitionSpec as P

KV_HEADS = 4
WIDTH = 128
GROUP = 8
KEY_COLUMNS = 512
IMAGES = 4
LOW = -1e30
SAFE_SCORE = 68.0
SCALE = WIDTH ** (-0.5)
LOG2E = 1.4426950408889634
GRID = 4
BLOCK = 4
BATCH_HEADS = 2
PAD = 16
VMEM_LIMIT = 48 * 1024 * 1024
GRADIENT_VMEM = 60 * 1024 * 1024

SMEM = pltpu.MemorySpace.SMEM
VMEM = pltpu.MemorySpace.VMEM
HBM = pltpu.MemorySpace.HBM


def place_in_block():
    doc, text = lax.axis_index("doc"), lax.axis_index("ctx")
    place = (text // GRID % 2) * 2 + text % GRID % 2
    return doc, jnp.where(doc % 2 == 0, place, 3 - place)


def prepare_kernel(docs, slots_any, kv, q, d_out, spans_any, *refs):
    send, pieces, (slots, rows, held, spans, sems) = refs[0], refs[1:BLOCK], refs[BLOCK:]
    tokens = q.shape[0]
    width = q.shape[1] // KV_HEADS
    doc, place = place_in_block()
    fetch_slots = pltpu.make_async_copy(slots_any, slots, sems.at[docs])
    fetch_rows = pltpu.make_async_copy(kv, rows, sems.at[docs + 1])
    fetch_spans = pltpu.make_async_copy(spans_any, spans, sems.at[docs + 2])
    fetch_slots.start()
    fetch_rows.start()
    fetch_spans.start()
    at = docs + 3
    fetches = []
    for k in range(1, BLOCK):
        columns = pl.ds(pl.multiple_of((place ^ k) * width, WIDTH), width)
        pair = [
            pltpu.make_async_copy(q.at[:, columns], held.at[k - 1, :tokens], sems.at[at]),
            pltpu.make_async_copy(
                d_out.at[:, columns], held.at[k - 1, tokens : 2 * tokens], sems.at[at + 1]
            ),
        ]
        for copy in pair:
            copy.start()
        fetches.append(pair)
        at += 2
    fetch_slots.wait()
    copies = []
    for d in range(docs):
        local = 0
        for j in range(IMAGES):
            s = slots[d * IMAGES + j]
            local += jnp.where(s // IMAGES == doc, s % IMAGES, 0)
        copies.append(pltpu.make_async_copy(rows.at[local], send.at[d], sems.at[d]))
    fetch_rows.wait()
    for copy in copies:
        copy.start()
    fetch_spans.wait()
    for k in range(1, BLOCK):
        held[k - 1, 2 * tokens :] = jnp.zeros_like(held[k - 1, 2 * tokens :])
        held[k - 1, 2 * tokens : 2 * tokens + 2, :tokens] = spans[...].astype(jnp.bfloat16)
    for k, pair in zip(range(1, BLOCK), fetches):
        for copy in pair:
            copy.wait()
        copies.append(pltpu.make_async_copy(held.at[k - 1], pieces[k - 1], sems.at[at]))
        copies[-1].start()
        at += 1
    for copy in copies:
        copy.wait()


def pick_kernel(slots, got, out, heads):
    doc, _ = place_in_block()
    for j in range(IMAGES):
        owner = slots[doc * IMAGES + j] // IMAGES
        for c in range(KV_HEADS):
            columns = slice(c * WIDTH, (c + 1) * WIDTH)
            heads[c, j, :, :WIDTH] = got[owner, :, columns]
            columns = slice(KEY_COLUMNS + c * WIDTH, KEY_COLUMNS + (c + 1) * WIDTH)
            heads[c, j, :, WIDTH:] = got[owner, :, columns]
    for y in range(GRID):
        for z in range(GRID):
            place = y % 2 * 2 + z % 2
            out[y * GRID + z] = heads[jnp.where(doc % 2 == 0, place, 3 - place)]


def merge_kernel(*refs):
    _, place = place_in_block()
    *parts, out = refs
    width = out.shape[1] // KV_HEADS
    for k, part in enumerate(parts):
        columns = pl.ds(pl.multiple_of((place ^ k) * width, WIDTH), width)
        out[:, columns] = part[...]


def softmax_gradients(scores, d_probs, seen, shifted):
    keys, rows = scores.shape
    scores = scores.reshape(-1, IMAGES, 16, rows)
    d_probs = d_probs.reshape(-1, IMAGES, 16, rows)
    shifts = [jnp.where(seen[j], 0.0, -LOW) for j in range(IMAGES)]
    if shifted:
        row_max = None
        for j in range(IMAGES):
            top = jnp.max(jnp.max(scores[:, j], axis=0), axis=0, keepdims=True)
            top = jnp.where(seen[j], top, LOW)
            row_max = top if row_max is None else jnp.maximum(row_max, top)
        row_max = row_max * SCALE
        shifts = [jnp.where(seen[j], row_max, -LOW) for j in range(IMAGES)]
    terms = []
    lows = []
    total = 0.0
    dots = 0.0
    for j in range(IMAGES):
        term = jnp.exp(scores[:, j] * SCALE - shifts[j])
        total += jnp.sum(jnp.sum(term, axis=0), axis=0, keepdims=True)
        dots += jnp.sum(jnp.sum(term * d_probs[:, j], axis=0), axis=0, keepdims=True)
        terms.append(term)
        lows.append(d_probs[:, j].astype(jnp.bfloat16))
    inverse = 1.0 / total
    delta = (dots * inverse).astype(jnp.bfloat16)
    low_probs = []
    d_scores = []
    for j in range(IMAGES):
        probs = (terms[j] * inverse).astype(jnp.bfloat16)
        low_probs.append(probs[:, None])
        d_scores.append((probs * (lows[j] - delta))[:, None])
    low_probs = jnp.concatenate(low_probs, axis=1).reshape(keys, rows)
    d_scores = jnp.concatenate(d_scores, axis=1).reshape(keys, rows)
    return low_probs, d_scores


def grad_kernel(gate, kv_any, q, d_out, spans_any, *refs):
    pieces, dqs, dkv_any, refs = refs[: BLOCK - 1], refs[BLOCK - 1 : 2 * BLOCK - 1], refs[2 * BLOCK - 1], refs[2 * BLOCK :]
    kv, held, own_spans, dq, dkv, keys_t, probs, d_scores, q_rows, d_rows, acc, sems = refs
    tokens = dqs[0].shape[0]
    width = dqs[0].shape[1]
    block = BATCH_HEADS * tokens
    _, place = place_in_block()
    fetch_kv = pltpu.make_async_copy(kv_any, kv, sems.at[2 * BLOCK])
    fetch_kv.start()
    columns = pl.ds(pl.multiple_of(place * width, WIDTH), width)
    fetch_own = [
        pltpu.make_async_copy(q.at[:, columns], held.at[0, :tokens], sems.at[0]),
        pltpu.make_async_copy(
            d_out.at[:, columns], held.at[0, tokens : 2 * tokens], sems.at[2 * BLOCK + 1]
        ),
        pltpu.make_async_copy(spans_any, own_spans, sems.at[2 * BLOCK + 2]),
    ]
    for copy in fetch_own:
        copy.start()
    for k in range(1, BLOCK):
        pltpu.make_async_copy(pieces[k - 1], held.at[k], sems.at[k]).start()
    acc[...] = jnp.zeros_like(acc)
    fetch_kv.wait()
    keys_t[...] = kv[:, :WIDTH].T
    for copy in fetch_own:
        copy.wait()
    held[0, 2 * tokens :] = jnp.zeros_like(held[0, 2 * tokens :])
    held[0, 2 * tokens : 2 * tokens + 2, :tokens] = own_spans[...].astype(jnp.bfloat16)
    factor = jnp.tanh(gate[...])
    transposed = (((1,), (1,)), ((), ()))

    for k in range(1, BLOCK):
        pltpu.make_async_copy(pieces[k - 1], held.at[k], sems.at[k]).wait()
    key_squares = jnp.square(keys_t[...].astype(jnp.float32))
    key_bound = jnp.max(jnp.sum(key_squares, axis=0, keepdims=True))
    largest = 0.0
    for k in range(BLOCK):
        largest = jnp.maximum(
            largest, jnp.max(jnp.abs(held[k, :tokens].astype(jnp.float32)), axis=0, keepdims=True)
        )
    column = largest[:, :WIDTH]
    for h in range(1, GROUP):
        column = jnp.maximum(column, largest[:, h * WIDTH : (h + 1) * WIDTH])
    query_bound = jnp.sum(jnp.square(column))
    safe = query_bound * key_bound * SCALE * SCALE < SAFE_SCORE * SAFE_SCORE

    def work(shifted, step, carry):
        for h in range(GROUP):
            rows, columns = slice(h * tokens, (h + 1) * tokens), slice(h * WIDTH, (h + 1) * WIDTH)
            q_rows[rows] = held[step, :tokens, columns]
            wide = held[step, tokens : 2 * tokens, columns].astype(jnp.float32)
            d_rows[rows] = (wide * factor).astype(jnp.bfloat16)
        spans = held[step, 2 * tokens :, :tokens].astype(jnp.float32)
        low = jnp.concatenate([spans[0:1]] * BATCH_HEADS, axis=1)
        high = jnp.concatenate([spans[1:2]] * BATCH_HEADS, axis=1)
        seen = [(low <= j) & (j < high) for j in range(IMAGES)]
        for at in range(0, GROUP * tokens, block):
            rows = slice(at, at + block)
            scores = lax.dot_general(
                kv[:, :WIDTH], q_rows[rows], transposed, preferred_element_type=jnp.float32
            )
            d_probs = lax.dot_general(
                kv[:, WIDTH:], d_rows[rows], transposed, preferred_element_type=jnp.float32
            )
            probs[:, rows], d_scores[:, rows] = softmax_gradients(
                scores, d_probs, seen, shifted
            )
        acc[:, :WIDTH] += jnp.dot(d_scores[...], q_rows[...], preferred_element_type=jnp.float32)
        acc[:, WIDTH:] += jnp.dot(probs[...], d_rows[...], preferred_element_type=jnp.float32)
        dq_t = jnp.dot(keys_t[...], d_scores[...], preferred_element_type=jnp.float32) * SCALE
        dq_rows = dq_t.T.astype(jnp.bfloat16)
        for h in range(GROUP):
            dq[step, :, h * WIDTH : (h + 1) * WIDTH] = dq_rows[h * tokens : (h + 1) * tokens]
        for k in range(BLOCK):

            @pl.when(step == k)
            def _():
                pltpu.make_async_copy(dq.at[k], dqs[k], sems.at[BLOCK + k]).start()

        return carry

    @pl.when(safe)
    def _():
        lax.fori_loop(0, BLOCK, functools.partial(work, False), 0)

    @pl.when(jnp.logical_not(safe))
    def _():
        lax.fori_loop(0, BLOCK, functools.partial(work, True), 0)

    dkv[:, :WIDTH] = (acc[:, :WIDTH] * SCALE).astype(jnp.bfloat16)
    dkv[:, WIDTH:] = acc[:, WIDTH:].astype(jnp.bfloat16)
    give = pltpu.make_async_copy(dkv, dkv_any, sems.at[2 * BLOCK])
    give.start()
    for k in range(BLOCK):
        pltpu.make_async_copy(dq.at[k], dqs[k], sems.at[BLOCK + k]).wait()
    give.wait()


def gradients(gate, kv, q, d_out, spans, pieces):
    key_rows = kv.shape[0]
    tokens = q.shape[0]
    width = pieces[0].shape[1]
    rows = GROUP * tokens
    in_hbm = pl.BlockSpec(memory_space=HBM)
    return pl.pallas_call(
        grad_kernel,
        in_specs=[pl.BlockSpec(memory_space=VMEM)] + [in_hbm] * (BLOCK + 3),
        out_specs=[in_hbm] * (BLOCK + 1),
        out_shape=[jax.ShapeDtypeStruct((tokens, width), jnp.bfloat16)] * BLOCK
        + [jax.ShapeDtypeStruct(kv.shape, jnp.bfloat16)],
        scratch_shapes=[
            pltpu.VMEM(kv.shape, jnp.bfloat16),
            pltpu.VMEM((BLOCK,) + pieces[0].shape, jnp.bfloat16),
            pltpu.VMEM(spans.shape, jnp.int32),
            pltpu.VMEM((BLOCK, tokens, width), jnp.bfloat16),
            pltpu.VMEM(kv.shape, jnp.bfloat16),
            pltpu.VMEM((WIDTH, key_rows), jnp.bfloat16),
            pltpu.VMEM((key_rows, rows), jnp.bfloat16),
            pltpu.VMEM((key_rows, rows), jnp.bfloat16),
            pltpu.VMEM((rows, WIDTH), jnp.bfloat16),
            pltpu.VMEM((rows, WIDTH), jnp.bfloat16),
            pltpu.VMEM(kv.shape, jnp.float32),
            pltpu.SemaphoreType.DMA((2 * BLOCK + 3,)),
        ],
        compiler_params=pltpu.CompilerParams(vmem_limit_bytes=GRADIENT_VMEM),
        cost_estimate=pl.CostEstimate(
            flops=10 * BLOCK * rows * key_rows * WIDTH,
            bytes_accessed=4 * 1024 * 1024,
            transcendentals=BLOCK * rows * key_rows,
        ),
        name="gradients",
    )(gate, kv, q, d_out, spans, *pieces)


def sum_kernel(slots, got, out):
    doc, _ = place_in_block()
    out[...] = jnp.zeros_like(out)
    for j in range(IMAGES):
        owner = slots[doc * IMAGES + j] // IMAGES
        for c in range(KV_HEADS):
            total = 0.0
            place = jnp.where(doc % 2 == 0, c, 3 - c)
            for y in range(0, GRID, 2):
                for z in range(0, GRID, 2):
                    at = (place // 2 + y) * GRID + place % 2 + z
                    total += got[at, j].astype(jnp.float32)
            out[owner, :, c * WIDTH : (c + 1) * WIDTH] = total[:, :WIDTH].astype(jnp.bfloat16)
            out[owner, :, KEY_COLUMNS + c * WIDTH : KEY_COLUMNS + (c + 1) * WIDTH] = total[
                :, WIDTH:
            ].astype(jnp.bfloat16)


def place_kernel(docs, slots, got, out):
    doc_here, _ = place_in_block()
    for s in range(IMAGES):
        doc = 0
        for d in range(docs):
            for j in range(IMAGES):
                doc += jnp.where(slots[d * IMAGES + j] == doc_here * IMAGES + s, d, 0)
        out[s] = got[doc].astype(jnp.float32)


def small(kernel, out_shape, name, scratch=()):
    return pl.pallas_call(
        kernel,
        in_specs=[
            pl.BlockSpec(memory_space=SMEM),
            pl.BlockSpec(memory_space=VMEM),
        ],
        out_specs=pl.BlockSpec(memory_space=VMEM),
        out_shape=out_shape,
        scratch_shapes=scratch,
        compiler_params=pltpu.CompilerParams(vmem_limit_bytes=VMEM_LIMIT),
        name=name,
    )


def swap(docs, k):
    pairs = []
    for d in range(docs):
        for y in range(GRID):
            for z in range(GRID):
                v, w = (y + d % 2) ^ (k // 2), (z + d % 2) ^ (k % 2)
                to = (v - d % 2) % GRID * GRID + (w - d % 2) % GRID
                pairs.append((d * GRID * GRID + y * GRID + z, d * GRID * GRID + to))
    return pairs


def shards(queries, image_kv, d_out, attn_gate, image_slots, spans):
    docs = lax.axis_size("doc")
    texts = lax.axis_size("ctx")
    images, rows, columns = image_kv.shape
    tokens, width = queries.shape[1], queries.shape[2] // KV_HEADS
    both = ("doc", "ctx")
    in_hbm = pl.BlockSpec(memory_space=HBM)
    in_vmem = pl.BlockSpec(memory_space=VMEM)
    params = pltpu.CompilerParams(vmem_limit_bytes=VMEM_LIMIT)
    block = jax.ShapeDtypeStruct((docs, rows, columns), jnp.bfloat16)
    span_rows = spans[0].T
    piece = jax.ShapeDtypeStruct((2 * tokens + PAD, width), jnp.bfloat16)
    send, *pieces = pl.pallas_call(
        functools.partial(prepare_kernel, docs),
        in_specs=[in_hbm] * 5,
        out_specs=[in_hbm] * BLOCK,
        out_shape=[block] + [piece] * (BLOCK - 1),
        scratch_shapes=[
            pltpu.SMEM(image_slots.shape, jnp.int32),
            pltpu.VMEM(image_kv.shape, jnp.bfloat16),
            pltpu.VMEM((BLOCK - 1,) + piece.shape, jnp.bfloat16),
            pltpu.VMEM(span_rows.shape, jnp.int32),
            pltpu.SemaphoreType.DMA((docs + 3 * BLOCK,)),
        ],
        name="prepare",
    )(image_slots, image_kv, queries[0], d_out[0], span_rows)
    got = lax.all_to_all(send, "doc", 0, 0)
    one_head = jax.ShapeDtypeStruct((texts, images, rows, 2 * WIDTH), jnp.bfloat16)
    send = small(
        pick_kernel,
        one_head,
        "pick",
        [pltpu.VMEM((KV_HEADS, images, rows, 2 * WIDTH), jnp.bfloat16)],
    )(image_slots, got)
    pieces = [lax.ppermute(pieces[k - 1], both, swap(docs, k)) for k in range(1, BLOCK)]
    kv = lax.all_to_all(send, "ctx", 0, 0).reshape(texts * images * rows, 2 * WIDTH)
    *dqs, dkv = gradients(
        attn_gate.reshape(1, 1), kv, queries[0], d_out[0], span_rows, pieces
    )
    dqs = [dqs[0]] + [lax.ppermute(dqs[k], both, swap(docs, k)) for k in range(1, BLOCK)]
    parts = lax.all_to_all(dkv.reshape(texts, images, rows, 2 * WIDTH), "ctx", 0, 0)
    send = small(sum_kernel, block, "sum")(image_slots, parts)
    got = lax.all_to_all(send, "doc", 0, 0)
    d_image_kv = small(
        functools.partial(place_kernel, docs),
        jax.ShapeDtypeStruct(image_kv.shape, jnp.float32),
        "place",
    )(image_slots, got)
    d_queries = pl.pallas_call(
        merge_kernel,
        in_specs=[in_vmem] * BLOCK,
        out_specs=in_vmem,
        out_shape=jax.ShapeDtypeStruct(queries.shape[1:], jnp.bfloat16),
        compiler_params=params,
        name="merge",
    )(*dqs)
    return d_queries[None], d_image_kv


def solution(mesh):
    return jax.shard_map(
        shards,
        mesh=mesh,
        in_specs=(
            P("doc", "ctx", None),
            P("doc", "ctx", None),
            P("doc", "ctx", None),
            P(),
            P(),
            P("doc", "ctx", None),
        ),
        out_specs=(P("doc", "ctx", None), P("doc", "ctx", None)),
        check_vma=False,
    )
```

```python
import functools

import jax
import jax.numpy as jnp
from jax import lax
from jax.experimental import pallas as pl
from jax.experimental.pallas import tpu as pltpu
from jax.sharding import PartitionSpec as P

KV_HEADS = 4
WIDTH = 128
GROUP = 8
KEY_COLUMNS = 512
IMAGES = 4
LOW = -1e30
SAFE_SCORE = 68.0
SCALE = WIDTH ** (-0.5)
GRID = 4
BLOCK = 4
BATCH_HEADS = 2
PAD = 16
VMEM_LIMIT = 48 * 1024 * 1024
GRADIENT_VMEM = 60 * 1024 * 1024

SMEM = pltpu.MemorySpace.SMEM
VMEM = pltpu.MemorySpace.VMEM
HBM = pltpu.MemorySpace.HBM


def place_in_block():
    doc, text = lax.axis_index("doc"), lax.axis_index("ctx")
    place = (text // GRID % 2) * 2 + text % GRID % 2
    return doc, jnp.where(doc % 2 == 0, place, 3 - place)


def prepare_kernel(docs, slots_any, kv, q, d_out, spans_any, *refs):
    send, pieces, (slots, rows, held, spans, sems) = refs[0], refs[1:BLOCK], refs[BLOCK:]
    tokens = q.shape[0]
    width = q.shape[1] // KV_HEADS
    doc, place = place_in_block()
    fetch_slots = pltpu.make_async_copy(slots_any, slots, sems.at[docs])
    fetch_rows = pltpu.make_async_copy(kv, rows, sems.at[docs + 1])
    fetch_spans = pltpu.make_async_copy(spans_any, spans, sems.at[docs + 2])
    fetch_slots.start()
    fetch_rows.start()
    fetch_spans.start()
    at = docs + 3
    fetches = []
    for k in range(1, BLOCK):
        columns = pl.ds(pl.multiple_of((place ^ k) * width, WIDTH), width)
        pair = [
            pltpu.make_async_copy(q.at[:, columns], held.at[k - 1, :tokens], sems.at[at]),
            pltpu.make_async_copy(
                d_out.at[:, columns], held.at[k - 1, tokens : 2 * tokens], sems.at[at + 1]
            ),
        ]
        for copy in pair:
            copy.start()
        fetches.append(pair)
        at += 2
    fetch_slots.wait()
    copies = []
    for d in range(docs):
        local = 0
        for j in range(IMAGES):
            s = slots[d * IMAGES + j]
            local += jnp.where(s // IMAGES == doc, s % IMAGES, 0)
        copies.append(pltpu.make_async_copy(rows.at[local], send.at[d], sems.at[d]))
    fetch_rows.wait()
    for copy in copies:
        copy.start()
    fetch_spans.wait()
    for k in range(1, BLOCK):
        held[k - 1, 2 * tokens :] = jnp.zeros_like(held[k - 1, 2 * tokens :])
        held[k - 1, 2 * tokens : 2 * tokens + 2, :tokens] = spans[...].astype(jnp.bfloat16)
    for k, pair in zip(range(1, BLOCK), fetches):
        for copy in pair:
            copy.wait()
        copies.append(pltpu.make_async_copy(held.at[k - 1], pieces[k - 1], sems.at[at]))
        copies[-1].start()
        at += 1
    for copy in copies:
        copy.wait()


def pick_kernel(slots, got, out, heads):
    doc, _ = place_in_block()
    for j in range(IMAGES):
        owner = slots[doc * IMAGES + j] // IMAGES
        for c in range(KV_HEADS):
            columns = slice(c * WIDTH, (c + 1) * WIDTH)
            heads[c, j, :, :WIDTH] = got[owner, :, columns]
            columns = slice(KEY_COLUMNS + c * WIDTH, KEY_COLUMNS + (c + 1) * WIDTH)
            heads[c, j, :, WIDTH:] = got[owner, :, columns]
    for y in range(GRID):
        for z in range(GRID):
            place = y % 2 * 2 + z % 2
            out[y * GRID + z] = heads[jnp.where(doc % 2 == 0, place, 3 - place)]


def merge_kernel(*refs):
    _, place = place_in_block()
    *parts, out = refs
    width = out.shape[1] // KV_HEADS
    for k, part in enumerate(parts):
        columns = pl.ds(pl.multiple_of((place ^ k) * width, WIDTH), width)
        out[:, columns] = part[...]


def softmax_gradients(scores, d_probs, seen, shifted):
    keys, rows = scores.shape
    scores = scores.reshape(-1, IMAGES, 16, rows)
    d_probs = d_probs.reshape(-1, IMAGES, 16, rows)
    shifts = [jnp.where(seen[j], 0.0, -LOW) for j in range(IMAGES)]
    if shifted:
        row_max = None
        for j in range(IMAGES):
            top = jnp.max(jnp.max(scores[:, j], axis=0), axis=0, keepdims=True)
            top = jnp.where(seen[j], top, LOW)
            row_max = top if row_max is None else jnp.maximum(row_max, top)
        row_max = row_max * SCALE
        shifts = [jnp.where(seen[j], row_max, -LOW) for j in range(IMAGES)]
    terms = []
    lows = []
    total = 0.0
    dots = 0.0
    for j in range(IMAGES):
        term = jnp.exp(scores[:, j] * SCALE - shifts[j])
        total += jnp.sum(jnp.sum(term, axis=0), axis=0, keepdims=True)
        dots += jnp.sum(jnp.sum(term * d_probs[:, j], axis=0), axis=0, keepdims=True)
        terms.append(term)
        lows.append(d_probs[:, j].astype(jnp.bfloat16))
    inverse = 1.0 / total
    delta = (dots * inverse).astype(jnp.bfloat16)
    low_probs = []
    d_scores = []
    for j in range(IMAGES):
        probs = (terms[j] * inverse).astype(jnp.bfloat16)
        low_probs.append(probs[:, None])
        d_scores.append((probs * (lows[j] - delta))[:, None])
    low_probs = jnp.concatenate(low_probs, axis=1).reshape(keys, rows)
    d_scores = jnp.concatenate(d_scores, axis=1).reshape(keys, rows)
    return low_probs, d_scores


def grad_kernel(gate, kv_any, q, d_out, spans_any, *refs):
    pieces, dqs, dkv_any, refs = refs[: BLOCK - 1], refs[BLOCK - 1 : 2 * BLOCK - 1], refs[2 * BLOCK - 1], refs[2 * BLOCK :]
    kv, held, own_spans, dq, dkv, keys_t, probs, d_scores, q_rows, d_rows, acc, sems = refs
    tokens = dqs[0].shape[0]
    width = dqs[0].shape[1]
    block = BATCH_HEADS * tokens
    _, place = place_in_block()
    fetch_kv = pltpu.make_async_copy(kv_any, kv, sems.at[2 * BLOCK])
    fetch_kv.start()
    columns = pl.ds(pl.multiple_of(place * width, WIDTH), width)
    fetch_own = [
        pltpu.make_async_copy(q.at[:, columns], held.at[0, :tokens], sems.at[0]),
        pltpu.make_async_copy(
            d_out.at[:, columns], held.at[0, tokens : 2 * tokens], sems.at[2 * BLOCK + 1]
        ),
        pltpu.make_async_copy(spans_any, own_spans, sems.at[2 * BLOCK + 2]),
    ]
    for copy in fetch_own:
        copy.start()
    for k in range(1, BLOCK):
        pltpu.make_async_copy(pieces[k - 1], held.at[k], sems.at[k]).start()
    acc[...] = jnp.zeros_like(acc)
    fetch_kv.wait()
    keys_t[...] = kv[:, :WIDTH].T
    for copy in fetch_own:
        copy.wait()
    held[0, 2 * tokens :] = jnp.zeros_like(held[0, 2 * tokens :])
    held[0, 2 * tokens : 2 * tokens + 2, :tokens] = own_spans[...].astype(jnp.bfloat16)
    factor = jnp.tanh(gate[...])
    transposed = (((1,), (1,)), ((), ()))

    for k in range(1, BLOCK):
        pltpu.make_async_copy(pieces[k - 1], held.at[k], sems.at[k]).wait()
    key_squares = jnp.square(keys_t[...].astype(jnp.float32))
    key_bound = jnp.max(jnp.sum(key_squares, axis=0, keepdims=True))
    largest = 0.0
    for k in range(BLOCK):
        largest = jnp.maximum(
            largest, jnp.max(jnp.abs(held[k, :tokens].astype(jnp.float32)), axis=0, keepdims=True)
        )
    column = largest[:, :WIDTH]
    for h in range(1, GROUP):
        column = jnp.maximum(column, largest[:, h * WIDTH : (h + 1) * WIDTH])
    query_bound = jnp.sum(jnp.square(column))
    safe = query_bound * key_bound * SCALE * SCALE < SAFE_SCORE * SAFE_SCORE

    def work(step, carry):
        for h in range(GROUP):
            rows, columns = slice(h * tokens, (h + 1) * tokens), slice(h * WIDTH, (h + 1) * WIDTH)
            q_rows[rows] = held[step, :tokens, columns]
            wide = held[step, tokens : 2 * tokens, columns].astype(jnp.float32)
            d_rows[rows] = (wide * factor).astype(jnp.bfloat16)
        spans = held[step, 2 * tokens :, :tokens].astype(jnp.float32)
        low = jnp.concatenate([spans[0:1]] * BATCH_HEADS, axis=1)
        high = jnp.concatenate([spans[1:2]] * BATCH_HEADS, axis=1)
        seen = [(low <= j) & (j < high) for j in range(IMAGES)]
        for at in range(0, GROUP * tokens, block):
            rows = slice(at, at + block)
            scores = lax.dot_general(
                kv[:, :WIDTH], q_rows[rows], transposed, preferred_element_type=jnp.float32
            )
            d_probs = lax.dot_general(
                kv[:, WIDTH:], d_rows[rows], transposed, preferred_element_type=jnp.float32
            )
            probs[:, rows], d_scores[:, rows] = softmax_gradients(
                scores, d_probs, seen, False
            )
        acc[:, :WIDTH] += jnp.dot(d_scores[...], q_rows[...], preferred_element_type=jnp.float32)
        acc[:, WIDTH:] += jnp.dot(probs[...], d_rows[...], preferred_element_type=jnp.float32)
        dq_t = jnp.dot(keys_t[...], d_scores[...], preferred_element_type=jnp.float32) * SCALE
        dq_rows = dq_t.T.astype(jnp.bfloat16)
        for h in range(GROUP):
            dq[step, :, h * WIDTH : (h + 1) * WIDTH] = dq_rows[h * tokens : (h + 1) * tokens]
        for k in range(BLOCK):

            @pl.when(step == k)
            def _():
                pltpu.make_async_copy(dq.at[k], dqs[k], sems.at[BLOCK + k]).start()

        return carry

    def careful_work(index, carry):
        step, h = index // GROUP, index % GROUP
        columns = pl.ds(pl.multiple_of(h * WIDTH, WIDTH), WIDTH)
        q_one = held[step, :tokens, columns]
        wide = held[step, tokens : 2 * tokens, columns].astype(jnp.float32)
        d_one = (wide * factor).astype(jnp.bfloat16)
        spans = held[step, 2 * tokens :, :tokens].astype(jnp.float32)
        seen = [(spans[0:1] <= j) & (j < spans[1:2]) for j in range(IMAGES)]
        scores = lax.dot_general(
            kv[:, :WIDTH], q_one, transposed, preferred_element_type=jnp.float32
        )
        d_probs = lax.dot_general(
            kv[:, WIDTH:], d_one, transposed, preferred_element_type=jnp.float32
        )
        probs_one, d_scores_one = softmax_gradients(scores, d_probs, seen, True)
        acc[:, :WIDTH] += jnp.dot(d_scores_one, q_one, preferred_element_type=jnp.float32)
        acc[:, WIDTH:] += jnp.dot(probs_one, d_one, preferred_element_type=jnp.float32)
        dq_t = jnp.dot(keys_t[...], d_scores_one, preferred_element_type=jnp.float32) * SCALE
        dq[step, :, columns] = dq_t.T.astype(jnp.bfloat16)
        return carry

    @pl.when(safe)
    def _():
        lax.fori_loop(0, BLOCK, work, 0)

    @pl.when(jnp.logical_not(safe))
    def _():
        lax.fori_loop(0, BLOCK * GROUP, careful_work, 0)
        for k in range(BLOCK):
            pltpu.make_async_copy(dq.at[k], dqs[k], sems.at[BLOCK + k]).start()

    dkv[:, :WIDTH] = (acc[:, :WIDTH] * SCALE).astype(jnp.bfloat16)
    dkv[:, WIDTH:] = acc[:, WIDTH:].astype(jnp.bfloat16)
    give = pltpu.make_async_copy(dkv, dkv_any, sems.at[2 * BLOCK])
    give.start()
    for k in range(BLOCK):
        pltpu.make_async_copy(dq.at[k], dqs[k], sems.at[BLOCK + k]).wait()
    give.wait()


def gradients(gate, kv, q, d_out, spans, pieces):
    key_rows = kv.shape[0]
    tokens = q.shape[0]
    width = pieces[0].shape[1]
    rows = GROUP * tokens
    in_hbm = pl.BlockSpec(memory_space=HBM)
    return pl.pallas_call(
        grad_kernel,
        in_specs=[pl.BlockSpec(memory_space=VMEM)] + [in_hbm] * (BLOCK + 3),
        out_specs=[in_hbm] * (BLOCK + 1),
        out_shape=[jax.ShapeDtypeStruct((tokens, width), jnp.bfloat16)] * BLOCK
        + [jax.ShapeDtypeStruct(kv.shape, jnp.bfloat16)],
        scratch_shapes=[
            pltpu.VMEM(kv.shape, jnp.bfloat16),
            pltpu.VMEM((BLOCK,) + pieces[0].shape, jnp.bfloat16),
            pltpu.VMEM(spans.shape, jnp.int32),
            pltpu.VMEM((BLOCK, tokens, width), jnp.bfloat16),
            pltpu.VMEM(kv.shape, jnp.bfloat16),
            pltpu.VMEM((WIDTH, key_rows), jnp.bfloat16),
            pltpu.VMEM((key_rows, rows), jnp.bfloat16),
            pltpu.VMEM((key_rows, rows), jnp.bfloat16),
            pltpu.VMEM((rows, WIDTH), jnp.bfloat16),
            pltpu.VMEM((rows, WIDTH), jnp.bfloat16),
            pltpu.VMEM(kv.shape, jnp.float32),
            pltpu.SemaphoreType.DMA((2 * BLOCK + 3,)),
        ],
        compiler_params=pltpu.CompilerParams(vmem_limit_bytes=GRADIENT_VMEM),
        cost_estimate=pl.CostEstimate(
            flops=10 * BLOCK * rows * key_rows * WIDTH,
            bytes_accessed=4 * 1024 * 1024,
            transcendentals=BLOCK * rows * key_rows,
        ),
        name="gradients",
    )(gate, kv, q, d_out, spans, *pieces)


def sum_kernel(slots, got, out):
    doc, _ = place_in_block()
    out[...] = jnp.zeros_like(out)
    for j in range(IMAGES):
        owner = slots[doc * IMAGES + j] // IMAGES
        for c in range(KV_HEADS):
            total = 0.0
            place = jnp.where(doc % 2 == 0, c, 3 - c)
            for y in range(0, GRID, 2):
                for z in range(0, GRID, 2):
                    at = (place // 2 + y) * GRID + place % 2 + z
                    total += got[at, j].astype(jnp.float32)
            out[owner, :, c * WIDTH : (c + 1) * WIDTH] = total[:, :WIDTH].astype(jnp.bfloat16)
            out[owner, :, KEY_COLUMNS + c * WIDTH : KEY_COLUMNS + (c + 1) * WIDTH] = total[
                :, WIDTH:
            ].astype(jnp.bfloat16)


def place_kernel(docs, slots, got, out):
    doc_here, _ = place_in_block()
    for s in range(IMAGES):
        doc = 0
        for d in range(docs):
            for j in range(IMAGES):
                doc += jnp.where(slots[d * IMAGES + j] == doc_here * IMAGES + s, d, 0)
        out[s] = got[doc].astype(jnp.float32)


def small(kernel, out_shape, name, scratch=()):
    return pl.pallas_call(
        kernel,
        in_specs=[
            pl.BlockSpec(memory_space=SMEM),
            pl.BlockSpec(memory_space=VMEM),
        ],
        out_specs=pl.BlockSpec(memory_space=VMEM),
        out_shape=out_shape,
        scratch_shapes=scratch,
        compiler_params=pltpu.CompilerParams(vmem_limit_bytes=VMEM_LIMIT),
        name=name,
    )


def swap(docs, k):
    pairs = []
    for d in range(docs):
        for y in range(GRID):
            for z in range(GRID):
                v, w = (y + d % 2) ^ (k // 2), (z + d % 2) ^ (k % 2)
                to = (v - d % 2) % GRID * GRID + (w - d % 2) % GRID
                pairs.append((d * GRID * GRID + y * GRID + z, d * GRID * GRID + to))
    return pairs


def shards(queries, image_kv, d_out, attn_gate, image_slots, spans):
    docs = lax.axis_size("doc")
    texts = lax.axis_size("ctx")
    images, rows, columns = image_kv.shape
    tokens, width = queries.shape[1], queries.shape[2] // KV_HEADS
    both = ("doc", "ctx")
    in_hbm = pl.BlockSpec(memory_space=HBM)
    in_vmem = pl.BlockSpec(memory_space=VMEM)
    params = pltpu.CompilerParams(vmem_limit_bytes=VMEM_LIMIT)
    block = jax.ShapeDtypeStruct((docs, rows, columns), jnp.bfloat16)
    span_rows = spans[0].T
    piece = jax.ShapeDtypeStruct((2 * tokens + PAD, width), jnp.bfloat16)
    send, *pieces = pl.pallas_call(
        functools.partial(prepare_kernel, docs),
        in_specs=[in_hbm] * 5,
        out_specs=[in_hbm] * BLOCK,
        out_shape=[block] + [piece] * (BLOCK - 1),
        scratch_shapes=[
            pltpu.SMEM(image_slots.shape, jnp.int32),
            pltpu.VMEM(image_kv.shape, jnp.bfloat16),
            pltpu.VMEM((BLOCK - 1,) + piece.shape, jnp.bfloat16),
            pltpu.VMEM(span_rows.shape, jnp.int32),
            pltpu.SemaphoreType.DMA((docs + 3 * BLOCK,)),
        ],
        name="prepare",
    )(image_slots, image_kv, queries[0], d_out[0], span_rows)
    got = lax.all_to_all(send, "doc", 0, 0)
    one_head = jax.ShapeDtypeStruct((texts, images, rows, 2 * WIDTH), jnp.bfloat16)
    send = small(
        pick_kernel,
        one_head,
        "pick",
        [pltpu.VMEM((KV_HEADS, images, rows, 2 * WIDTH), jnp.bfloat16)],
    )(image_slots, got)
    pieces = [lax.ppermute(pieces[k - 1], both, swap(docs, k)) for k in range(1, BLOCK)]
    kv = lax.all_to_all(send, "ctx", 0, 0).reshape(texts * images * rows, 2 * WIDTH)
    *dqs, dkv = gradients(
        attn_gate.reshape(1, 1), kv, queries[0], d_out[0], span_rows, pieces
    )
    dqs = [dqs[0]] + [lax.ppermute(dqs[k], both, swap(docs, k)) for k in range(1, BLOCK)]
    parts = lax.all_to_all(dkv.reshape(texts, images, rows, 2 * WIDTH), "ctx", 0, 0)
    send = small(sum_kernel, block, "sum")(image_slots, parts)
    got = lax.all_to_all(send, "doc", 0, 0)
    d_image_kv = small(
        functools.partial(place_kernel, docs),
        jax.ShapeDtypeStruct(image_kv.shape, jnp.float32),
        "place",
    )(image_slots, got)
    d_queries = pl.pallas_call(
        merge_kernel,
        in_specs=[in_vmem] * BLOCK,
        out_specs=in_vmem,
        out_shape=jax.ShapeDtypeStruct(queries.shape[1:], jnp.bfloat16),
        compiler_params=params,
        name="merge",
    )(*dqs)
    return d_queries[None], d_image_kv


def solution(mesh):
    return jax.shard_map(
        shards,
        mesh=mesh,
        in_specs=(
            P("doc", "ctx", None),
            P("doc", "ctx", None),
            P("doc", "ctx", None),
            P(),
            P(),
            P("doc", "ctx", None),
        ),
        out_specs=(P("doc", "ctx", None), P("doc", "ctx", None)),
        check_vma=False,
    )
```

```python
import functools

import jax
import jax.numpy as jnp
from jax import lax
from jax.experimental import pallas as pl
from jax.experimental.pallas import tpu as pltpu
from jax.sharding import PartitionSpec as P

KV_HEADS = 4
WIDTH = 128
GROUP = 8
KEY_COLUMNS = 512
IMAGES = 4
LOW = -1e30
SAFE_SCORE = 68.0
SCALE = WIDTH ** (-0.5)
GRID = 4
BLOCK = 4
BATCH_HEADS = 2
PAD = 16
VMEM_LIMIT = 48 * 1024 * 1024
GRADIENT_VMEM = 60 * 1024 * 1024

SMEM = pltpu.MemorySpace.SMEM
VMEM = pltpu.MemorySpace.VMEM
HBM = pltpu.MemorySpace.HBM


def place_in_block():
    doc, text = lax.axis_index("doc"), lax.axis_index("ctx")
    place = (text // GRID % 2) * 2 + text % GRID % 2
    return doc, jnp.where(doc % 2 == 0, place, 3 - place)


def prepare_kernel(docs, slots_any, kv, q, d_out, spans_any, *refs):
    send, pieces, (slots, rows, held, spans, padded, sems) = refs[0], refs[1:BLOCK], refs[BLOCK:]
    tokens = q.shape[0]
    width = q.shape[1] // KV_HEADS
    doc, place = place_in_block()
    fetch_slots = pltpu.make_async_copy(slots_any, slots, sems.at[docs])
    fetch_rows = pltpu.make_async_copy(kv, rows, sems.at[docs + 1])
    fetch_spans = pltpu.make_async_copy(spans_any, spans, sems.at[docs + 2])
    fetch_slots.start()
    fetch_rows.start()
    fetch_spans.start()
    at = docs + 3
    fetches = []
    for k in range(1, BLOCK):
        columns = pl.ds(pl.multiple_of((place ^ k) * width, WIDTH), width)
        pair = [
            pltpu.make_async_copy(q.at[:, columns], held.at[k - 1, :tokens], sems.at[at]),
            pltpu.make_async_copy(
                d_out.at[:, columns], held.at[k - 1, tokens : 2 * tokens], sems.at[at + 1]
            ),
        ]
        for copy in pair:
            copy.start()
        fetches.append(pair)
        at += 2
    fetch_slots.wait()
    copies = []
    for d in range(docs):
        local = 0
        for j in range(IMAGES):
            s = slots[d * IMAGES + j]
            local += jnp.where(s // IMAGES == doc, s % IMAGES, 0)
        copies.append(pltpu.make_async_copy(rows.at[local], send.at[d], sems.at[d]))
    fetch_rows.wait()
    for copy in copies:
        copy.start()
    fetch_spans.wait()
    padded[...] = jnp.zeros_like(padded)
    padded[:2] = spans[...].astype(jnp.float32)
    for k in range(1, BLOCK):
        held[k - 1, 2 * tokens :] = jnp.zeros_like(held[k - 1, 2 * tokens :])
        held[k - 1, 2 * tokens :, :tokens] = padded[...].astype(jnp.bfloat16)
    for k, pair in zip(range(1, BLOCK), fetches):
        for copy in pair:
            copy.wait()
        copies.append(pltpu.make_async_copy(held.at[k - 1], pieces[k - 1], sems.at[at]))
        copies[-1].start()
        at += 1
    for copy in copies:
        copy.wait()


def pick_kernel(slots, got, out, heads):
    doc, _ = place_in_block()
    for j in range(IMAGES):
        owner = slots[doc * IMAGES + j] // IMAGES
        for c in range(KV_HEADS):
            columns = slice(c * WIDTH, (c + 1) * WIDTH)
            heads[c, j, :, :WIDTH] = got[owner, :, columns]
            columns = slice(KEY_COLUMNS + c * WIDTH, KEY_COLUMNS + (c + 1) * WIDTH)
            heads[c, j, :, WIDTH:] = got[owner, :, columns]
    for y in range(GRID):
        for z in range(GRID):
            place = y % 2 * 2 + z % 2
            out[y * GRID + z] = heads[jnp.where(doc % 2 == 0, place, 3 - place)]


def merge_kernel(*refs):
    _, place = place_in_block()
    *parts, out = refs
    width = out.shape[1] // KV_HEADS
    for k, part in enumerate(parts):
        columns = pl.ds(pl.multiple_of((place ^ k) * width, WIDTH), width)
        out[:, columns] = part[...]


def softmax_gradients(scores, d_probs, seen, shifted):
    keys, rows = scores.shape
    scores = scores.reshape(-1, IMAGES, 16, rows)
    d_probs = d_probs.reshape(-1, IMAGES, 16, rows)
    shifts = [jnp.where(seen[j], 0.0, -LOW) for j in range(IMAGES)]
    if shifted:
        row_max = None
        for j in range(IMAGES):
            top = jnp.max(jnp.max(scores[:, j], axis=0), axis=0, keepdims=True)
            top = jnp.where(seen[j], top, LOW)
            row_max = top if row_max is None else jnp.maximum(row_max, top)
        row_max = row_max * SCALE
        shifts = [jnp.where(seen[j], row_max, -LOW) for j in range(IMAGES)]
    terms = []
    lows = []
    total = 0.0
    dots = 0.0
    for j in range(IMAGES):
        term = jnp.exp(scores[:, j] * SCALE - shifts[j])
        total += jnp.sum(jnp.sum(term, axis=0), axis=0, keepdims=True)
        dots += jnp.sum(jnp.sum(term * d_probs[:, j], axis=0), axis=0, keepdims=True)
        terms.append(term)
        lows.append(d_probs[:, j].astype(jnp.bfloat16))
    inverse = 1.0 / total
    delta = (dots * inverse).astype(jnp.bfloat16)
    low_probs = []
    d_scores = []
    for j in range(IMAGES):
        probs = (terms[j] * inverse).astype(jnp.bfloat16)
        low_probs.append(probs[:, None])
        d_scores.append((probs * (lows[j] - delta))[:, None])
    low_probs = jnp.concatenate(low_probs, axis=1).reshape(keys, rows)
    d_scores = jnp.concatenate(d_scores, axis=1).reshape(keys, rows)
    return low_probs, d_scores


def grad_kernel(gate, kv_any, q, d_out, spans_any, *refs):
    pieces, dqs, dkv_any, refs = refs[: BLOCK - 1], refs[BLOCK - 1 : 2 * BLOCK - 1], refs[2 * BLOCK - 1], refs[2 * BLOCK :]
    kv, held, own_spans, padded, dq, dkv, keys_t, probs, d_scores, q_rows, d_rows, acc, sems = refs
    tokens = dqs[0].shape[0]
    width = dqs[0].shape[1]
    block = BATCH_HEADS * tokens
    _, place = place_in_block()
    fetch_kv = pltpu.make_async_copy(kv_any, kv, sems.at[2 * BLOCK])
    fetch_kv.start()
    columns = pl.ds(pl.multiple_of(place * width, WIDTH), width)
    fetch_own = [
        pltpu.make_async_copy(q.at[:, columns], held.at[0, :tokens], sems.at[0]),
        pltpu.make_async_copy(
            d_out.at[:, columns], held.at[0, tokens : 2 * tokens], sems.at[2 * BLOCK + 1]
        ),
        pltpu.make_async_copy(spans_any, own_spans, sems.at[2 * BLOCK + 2]),
    ]
    for copy in fetch_own:
        copy.start()
    for k in range(1, BLOCK):
        pltpu.make_async_copy(pieces[k - 1], held.at[k], sems.at[k]).start()
    acc[...] = jnp.zeros_like(acc)
    fetch_kv.wait()
    keys_t[...] = kv[:, :WIDTH].T
    for copy in fetch_own:
        copy.wait()
    padded[...] = jnp.zeros_like(padded)
    padded[:2] = own_spans[...].astype(jnp.float32)
    held[0, 2 * tokens :, :tokens] = padded[...].astype(jnp.bfloat16)
    factor = jnp.tanh(gate[...])
    transposed = (((1,), (1,)), ((), ()))

    for k in range(1, BLOCK):
        pltpu.make_async_copy(pieces[k - 1], held.at[k], sems.at[k]).wait()
    key_squares = jnp.square(keys_t[...].astype(jnp.float32))
    key_bound = jnp.max(jnp.sum(key_squares, axis=0, keepdims=True))
    largest = 0.0
    for k in range(BLOCK):
        largest = jnp.maximum(
            largest, jnp.max(jnp.abs(held[k, :tokens].astype(jnp.float32)), axis=0, keepdims=True)
        )
    column = largest[:, :WIDTH]
    for h in range(1, GROUP):
        column = jnp.maximum(column, largest[:, h * WIDTH : (h + 1) * WIDTH])
    query_bound = jnp.sum(jnp.square(column))
    safe = query_bound * key_bound * SCALE * SCALE < SAFE_SCORE * SAFE_SCORE

    def work(step, carry):
        for h in range(GROUP):
            rows, columns = slice(h * tokens, (h + 1) * tokens), slice(h * WIDTH, (h + 1) * WIDTH)
            q_rows[rows] = held[step, :tokens, columns]
            wide = held[step, tokens : 2 * tokens, columns].astype(jnp.float32)
            d_rows[rows] = (wide * factor).astype(jnp.bfloat16)
        spans = held[step, 2 * tokens :, :tokens].astype(jnp.float32)
        low = jnp.concatenate([spans[0:1]] * BATCH_HEADS, axis=1)
        high = jnp.concatenate([spans[1:2]] * BATCH_HEADS, axis=1)
        seen = [(low <= j) & (j < high) for j in range(IMAGES)]
        for at in range(0, GROUP * tokens, block):
            rows = slice(at, at + block)
            scores = lax.dot_general(
                kv[:, :WIDTH], q_rows[rows], transposed, preferred_element_type=jnp.float32
            )
            d_probs = lax.dot_general(
                kv[:, WIDTH:], d_rows[rows], transposed, preferred_element_type=jnp.float32
            )
            probs[:, rows], d_scores[:, rows] = softmax_gradients(
                scores, d_probs, seen, False
            )
        acc[:, :WIDTH] += jnp.dot(d_scores[...], q_rows[...], preferred_element_type=jnp.float32)
        acc[:, WIDTH:] += jnp.dot(probs[...], d_rows[...], preferred_element_type=jnp.float32)
        dq_t = jnp.dot(keys_t[...], d_scores[...], preferred_element_type=jnp.float32) * SCALE
        dq_rows = dq_t.T.astype(jnp.bfloat16)
        for h in range(GROUP):
            dq[step, :, h * WIDTH : (h + 1) * WIDTH] = dq_rows[h * tokens : (h + 1) * tokens]
        for k in range(BLOCK):

            @pl.when(step == k)
            def _():
                pltpu.make_async_copy(dq.at[k], dqs[k], sems.at[BLOCK + k]).start()

        return carry

    def careful_work(index, carry):
        step, h = index // GROUP, index % GROUP
        columns = pl.ds(pl.multiple_of(h * WIDTH, WIDTH), WIDTH)
        q_one = held[step, :tokens, columns]
        wide = held[step, tokens : 2 * tokens, columns].astype(jnp.float32)
        d_one = (wide * factor).astype(jnp.bfloat16)
        spans = held[step, 2 * tokens :, :tokens].astype(jnp.float32)
        seen = [(spans[0:1] <= j) & (j < spans[1:2]) for j in range(IMAGES)]
        scores = lax.dot_general(
            kv[:, :WIDTH], q_one, transposed, preferred_element_type=jnp.float32
        )
        d_probs = lax.dot_general(
            kv[:, WIDTH:], d_one, transposed, preferred_element_type=jnp.float32
        )
        probs_one, d_scores_one = softmax_gradients(scores, d_probs, seen, True)
        acc[:, :WIDTH] += jnp.dot(d_scores_one, q_one, preferred_element_type=jnp.float32)
        acc[:, WIDTH:] += jnp.dot(probs_one, d_one, preferred_element_type=jnp.float32)
        dq_t = jnp.dot(keys_t[...], d_scores_one, preferred_element_type=jnp.float32) * SCALE
        dq[step, :, columns] = dq_t.T.astype(jnp.bfloat16)
        return carry

    @pl.when(safe)
    def _():
        lax.fori_loop(0, BLOCK, work, 0)

    @pl.when(jnp.logical_not(safe))
    def _():
        lax.fori_loop(0, BLOCK * GROUP, careful_work, 0)
        for k in range(BLOCK):
            pltpu.make_async_copy(dq.at[k], dqs[k], sems.at[BLOCK + k]).start()

    dkv[:, :WIDTH] = (acc[:, :WIDTH] * SCALE).astype(jnp.bfloat16)
    dkv[:, WIDTH:] = acc[:, WIDTH:].astype(jnp.bfloat16)
    give = pltpu.make_async_copy(dkv, dkv_any, sems.at[2 * BLOCK])
    give.start()
    for k in range(BLOCK):
        pltpu.make_async_copy(dq.at[k], dqs[k], sems.at[BLOCK + k]).wait()
    give.wait()


def gradients(gate, kv, q, d_out, spans, pieces):
    key_rows = kv.shape[0]
    tokens = q.shape[0]
    width = pieces[0].shape[1]
    rows = GROUP * tokens
    in_hbm = pl.BlockSpec(memory_space=HBM)
    return pl.pallas_call(
        grad_kernel,
        in_specs=[pl.BlockSpec(memory_space=VMEM)] + [in_hbm] * (BLOCK + 3),
        out_specs=[in_hbm] * (BLOCK + 1),
        out_shape=[jax.ShapeDtypeStruct((tokens, width), jnp.bfloat16)] * BLOCK
        + [jax.ShapeDtypeStruct(kv.shape, jnp.bfloat16)],
        scratch_shapes=[
            pltpu.VMEM(kv.shape, jnp.bfloat16),
            pltpu.VMEM((BLOCK,) + pieces[0].shape, jnp.bfloat16),
            pltpu.VMEM(spans.shape, jnp.int32),
            pltpu.VMEM((PAD, tokens), jnp.float32),
            pltpu.VMEM((BLOCK, tokens, width), jnp.bfloat16),
            pltpu.VMEM(kv.shape, jnp.bfloat16),
            pltpu.VMEM((WIDTH, key_rows), jnp.bfloat16),
            pltpu.VMEM((key_rows, rows), jnp.bfloat16),
            pltpu.VMEM((key_rows, rows), jnp.bfloat16),
            pltpu.VMEM((rows, WIDTH), jnp.bfloat16),
            pltpu.VMEM((rows, WIDTH), jnp.bfloat16),
            pltpu.VMEM(kv.shape, jnp.float32),
            pltpu.SemaphoreType.DMA((2 * BLOCK + 3,)),
        ],
        compiler_params=pltpu.CompilerParams(vmem_limit_bytes=GRADIENT_VMEM),
        cost_estimate=pl.CostEstimate(
            flops=10 * BLOCK * rows * key_rows * WIDTH,
            bytes_accessed=4 * 1024 * 1024,
            transcendentals=BLOCK * rows * key_rows,
        ),
        name="gradients",
    )(gate, kv, q, d_out, spans, *pieces)


def sum_kernel(slots, got, out):
    doc, _ = place_in_block()
    out[...] = jnp.zeros_like(out)
    for j in range(IMAGES):
        owner = slots[doc * IMAGES + j] // IMAGES
        for c in range(KV_HEADS):
            total = 0.0
            place = jnp.where(doc % 2 == 0, c, 3 - c)
            for y in range(0, GRID, 2):
                for z in range(0, GRID, 2):
                    at = (place // 2 + y) * GRID + place % 2 + z
                    total += got[at, j].astype(jnp.float32)
            out[owner, :, c * WIDTH : (c + 1) * WIDTH] = total[:, :WIDTH].astype(jnp.bfloat16)
            out[owner, :, KEY_COLUMNS + c * WIDTH : KEY_COLUMNS + (c + 1) * WIDTH] = total[
                :, WIDTH:
            ].astype(jnp.bfloat16)


def place_kernel(docs, slots, got, out):
    doc_here, _ = place_in_block()
    for s in range(IMAGES):
        doc = 0
        for d in range(docs):
            for j in range(IMAGES):
                doc += jnp.where(slots[d * IMAGES + j] == doc_here * IMAGES + s, d, 0)
        out[s] = got[doc].astype(jnp.float32)


def small(kernel, out_shape, name, scratch=()):
    return pl.pallas_call(
        kernel,
        in_specs=[
            pl.BlockSpec(memory_space=SMEM),
            pl.BlockSpec(memory_space=VMEM),
        ],
        out_specs=pl.BlockSpec(memory_space=VMEM),
        out_shape=out_shape,
        scratch_shapes=scratch,
        compiler_params=pltpu.CompilerParams(vmem_limit_bytes=VMEM_LIMIT),
        name=name,
    )


def swap(docs, k):
    pairs = []
    for d in range(docs):
        for y in range(GRID):
            for z in range(GRID):
                v, w = (y + d % 2) ^ (k // 2), (z + d % 2) ^ (k % 2)
                to = (v - d % 2) % GRID * GRID + (w - d % 2) % GRID
                pairs.append((d * GRID * GRID + y * GRID + z, d * GRID * GRID + to))
    return pairs


def shards(queries, image_kv, d_out, attn_gate, image_slots, spans):
    docs = lax.axis_size("doc")
    texts = lax.axis_size("ctx")
    images, rows, columns = image_kv.shape
    tokens, width = queries.shape[1], queries.shape[2] // KV_HEADS
    both = ("doc", "ctx")
    in_hbm = pl.BlockSpec(memory_space=HBM)
    in_vmem = pl.BlockSpec(memory_space=VMEM)
    params = pltpu.CompilerParams(vmem_limit_bytes=VMEM_LIMIT)
    block = jax.ShapeDtypeStruct((docs, rows, columns), jnp.bfloat16)
    span_rows = spans[0].T
    piece = jax.ShapeDtypeStruct((2 * tokens + PAD, width), jnp.bfloat16)
    send, *pieces = pl.pallas_call(
        functools.partial(prepare_kernel, docs),
        in_specs=[in_hbm] * 5,
        out_specs=[in_hbm] * BLOCK,
        out_shape=[block] + [piece] * (BLOCK - 1),
        scratch_shapes=[
            pltpu.SMEM(image_slots.shape, jnp.int32),
            pltpu.VMEM(image_kv.shape, jnp.bfloat16),
            pltpu.VMEM((BLOCK - 1,) + piece.shape, jnp.bfloat16),
            pltpu.VMEM(span_rows.shape, jnp.int32),
            pltpu.VMEM((PAD, tokens), jnp.float32),
            pltpu.SemaphoreType.DMA((docs + 3 * BLOCK,)),
        ],
        name="prepare",
    )(image_slots, image_kv, queries[0], d_out[0], span_rows)
    got = lax.all_to_all(send, "doc", 0, 0)
    one_head = jax.ShapeDtypeStruct((texts, images, rows, 2 * WIDTH), jnp.bfloat16)
    send = small(
        pick_kernel,
        one_head,
        "pick",
        [pltpu.VMEM((KV_HEADS, images, rows, 2 * WIDTH), jnp.bfloat16)],
    )(image_slots, got)
    pieces = [lax.ppermute(pieces[k - 1], both, swap(docs, k)) for k in range(1, BLOCK)]
    kv = lax.all_to_all(send, "ctx", 0, 0).reshape(texts * images * rows, 2 * WIDTH)
    *dqs, dkv = gradients(
        attn_gate.reshape(1, 1), kv, queries[0], d_out[0], span_rows, pieces
    )
    dqs = [dqs[0]] + [lax.ppermute(dqs[k], both, swap(docs, k)) for k in range(1, BLOCK)]
    parts = lax.all_to_all(dkv.reshape(texts, images, rows, 2 * WIDTH), "ctx", 0, 0)
    send = small(sum_kernel, block, "sum")(image_slots, parts)
    got = lax.all_to_all(send, "doc", 0, 0)
    d_image_kv = small(
        functools.partial(place_kernel, docs),
        jax.ShapeDtypeStruct(image_kv.shape, jnp.float32),
        "place",
    )(image_slots, got)
    d_queries = pl.pallas_call(
        merge_kernel,
        in_specs=[in_vmem] * BLOCK,
        out_specs=in_vmem,
        out_shape=jax.ShapeDtypeStruct(queries.shape[1:], jnp.bfloat16),
        compiler_params=params,
        name="merge",
    )(*dqs)
    return d_queries[None], d_image_kv


def solution(mesh):
    return jax.shard_map(
        shards,
        mesh=mesh,
        in_specs=(
            P("doc", "ctx", None),
            P("doc", "ctx", None),
            P("doc", "ctx", None),
            P(),
            P(),
            P("doc", "ctx", None),
        ),
        out_specs=(P("doc", "ctx", None), P("doc", "ctx", None)),
        check_vma=False,
    )
```

```python
import functools

import jax
import jax.numpy as jnp
from jax import lax
from jax.experimental import pallas as pl
from jax.experimental.pallas import tpu as pltpu
from jax.sharding import PartitionSpec as P

KV_HEADS = 4
WIDTH = 128
GROUP = 8
KEY_COLUMNS = 512
IMAGES = 4
LOW = -1e30
SAFE_SCORE = 68.0
SCALE = WIDTH ** (-0.5)
GRID = 4
BLOCK = 4
BATCH_HEADS = 4
PAD = 16
VMEM_LIMIT = 48 * 1024 * 1024
GRADIENT_VMEM = 60 * 1024 * 1024

SMEM = pltpu.MemorySpace.SMEM
VMEM = pltpu.MemorySpace.VMEM
HBM = pltpu.MemorySpace.HBM


def place_in_block():
    doc, text = lax.axis_index("doc"), lax.axis_index("ctx")
    place = (text // GRID % 2) * 2 + text % GRID % 2
    return doc, jnp.where(doc % 2 == 0, place, 3 - place)


def prepare_kernel(docs, slots_any, kv, q, d_out, spans_any, *refs):
    send, pieces, (slots, rows, held, spans, padded, sems) = refs[0], refs[1:BLOCK], refs[BLOCK:]
    tokens = q.shape[0]
    width = q.shape[1] // KV_HEADS
    doc, place = place_in_block()
    fetch_slots = pltpu.make_async_copy(slots_any, slots, sems.at[docs])
    fetch_rows = pltpu.make_async_copy(kv, rows, sems.at[docs + 1])
    fetch_spans = pltpu.make_async_copy(spans_any, spans, sems.at[docs + 2])
    fetch_slots.start()
    fetch_rows.start()
    fetch_spans.start()
    at = docs + 3
    fetches = []
    for k in range(1, BLOCK):
        columns = pl.ds(pl.multiple_of((place ^ k) * width, WIDTH), width)
        pair = [
            pltpu.make_async_copy(q.at[:, columns], held.at[k - 1, :tokens], sems.at[at]),
            pltpu.make_async_copy(
                d_out.at[:, columns], held.at[k - 1, tokens : 2 * tokens], sems.at[at + 1]
            ),
        ]
        for copy in pair:
            copy.start()
        fetches.append(pair)
        at += 2
    fetch_slots.wait()
    copies = []
    for d in range(docs):
        local = 0
        for j in range(IMAGES):
            s = slots[d * IMAGES + j]
            local += jnp.where(s // IMAGES == doc, s % IMAGES, 0)
        copies.append(pltpu.make_async_copy(rows.at[local], send.at[d], sems.at[d]))
    fetch_rows.wait()
    for copy in copies:
        copy.start()
    fetch_spans.wait()
    padded[...] = jnp.zeros_like(padded)
    padded[:2] = spans[...].astype(jnp.float32)
    for k in range(1, BLOCK):
        held[k - 1, 2 * tokens :] = jnp.zeros_like(held[k - 1, 2 * tokens :])
        held[k - 1, 2 * tokens :, :tokens] = padded[...].astype(jnp.bfloat16)
    for k, pair in zip(range(1, BLOCK), fetches):
        for copy in pair:
            copy.wait()
        copies.append(pltpu.make_async_copy(held.at[k - 1], pieces[k - 1], sems.at[at]))
        copies[-1].start()
        at += 1
    for copy in copies:
        copy.wait()


def pick_kernel(slots, got, out, heads):
    doc, _ = place_in_block()
    for j in range(IMAGES):
        owner = slots[doc * IMAGES + j] // IMAGES
        for c in range(KV_HEADS):
            columns = slice(c * WIDTH, (c + 1) * WIDTH)
            heads[c, j, :, :WIDTH] = got[owner, :, columns]
            columns = slice(KEY_COLUMNS + c * WIDTH, KEY_COLUMNS + (c + 1) * WIDTH)
            heads[c, j, :, WIDTH:] = got[owner, :, columns]
    for y in range(GRID):
        for z in range(GRID):
            place = y % 2 * 2 + z % 2
            out[y * GRID + z] = heads[jnp.where(doc % 2 == 0, place, 3 - place)]


def merge_kernel(*refs):
    _, place = place_in_block()
    *parts, out = refs
    width = out.shape[1] // KV_HEADS
    for k, part in enumerate(parts):
        columns = pl.ds(pl.multiple_of((place ^ k) * width, WIDTH), width)
        out[:, columns] = part[...]


def softmax_gradients(scores, d_probs, seen, shifted):
    keys, rows = scores.shape
    scores = scores.reshape(-1, IMAGES, 16, rows)
    d_probs = d_probs.reshape(-1, IMAGES, 16, rows)
    shifts = [jnp.where(seen[j], 0.0, -LOW) for j in range(IMAGES)]
    if shifted:
        row_max = None
        for j in range(IMAGES):
            top = jnp.max(jnp.max(scores[:, j], axis=0), axis=0, keepdims=True)
            top = jnp.where(seen[j], top, LOW)
            row_max = top if row_max is None else jnp.maximum(row_max, top)
        row_max = row_max * SCALE
        shifts = [jnp.where(seen[j], row_max, -LOW) for j in range(IMAGES)]
    terms = []
    lows = []
    total = 0.0
    dots = 0.0
    for j in range(IMAGES):
        term = jnp.exp(scores[:, j] * SCALE - shifts[j])
        total += jnp.sum(jnp.sum(term, axis=0), axis=0, keepdims=True)
        dots += jnp.sum(jnp.sum(term * d_probs[:, j], axis=0), axis=0, keepdims=True)
        terms.append(term)
        lows.append(d_probs[:, j].astype(jnp.bfloat16))
    inverse = 1.0 / total
    delta = (dots * inverse).astype(jnp.bfloat16)
    low_probs = []
    d_scores = []
    for j in range(IMAGES):
        probs = (terms[j] * inverse).astype(jnp.bfloat16)
        low_probs.append(probs[:, None])
        d_scores.append((probs * (lows[j] - delta))[:, None])
    low_probs = jnp.concatenate(low_probs, axis=1).reshape(keys, rows)
    d_scores = jnp.concatenate(d_scores, axis=1).reshape(keys, rows)
    return low_probs, d_scores


def grad_kernel(gate, kv_any, q, d_out, spans_any, *refs):
    pieces, dqs, dkv_any, refs = refs[: BLOCK - 1], refs[BLOCK - 1 : 2 * BLOCK - 1], refs[2 * BLOCK - 1], refs[2 * BLOCK :]
    kv, held, own_spans, padded, dq, dkv, keys_t, probs, d_scores, q_rows, d_rows, acc, sems = refs
    tokens = dqs[0].shape[0]
    width = dqs[0].shape[1]
    block = BATCH_HEADS * tokens
    _, place = place_in_block()
    fetch_kv = pltpu.make_async_copy(kv_any, kv, sems.at[2 * BLOCK])
    fetch_kv.start()
    columns = pl.ds(pl.multiple_of(place * width, WIDTH), width)
    fetch_own = [
        pltpu.make_async_copy(q.at[:, columns], held.at[0, :tokens], sems.at[0]),
        pltpu.make_async_copy(
            d_out.at[:, columns], held.at[0, tokens : 2 * tokens], sems.at[2 * BLOCK + 1]
        ),
        pltpu.make_async_copy(spans_any, own_spans, sems.at[2 * BLOCK + 2]),
    ]
    for copy in fetch_own:
        copy.start()
    for k in range(1, BLOCK):
        pltpu.make_async_copy(pieces[k - 1], held.at[k], sems.at[k]).start()
    acc[...] = jnp.zeros_like(acc)
    fetch_kv.wait()
    keys_t[...] = kv[:, :WIDTH].T
    for copy in fetch_own:
        copy.wait()
    padded[...] = jnp.zeros_like(padded)
    padded[:2] = own_spans[...].astype(jnp.float32)
    held[0, 2 * tokens :, :tokens] = padded[...].astype(jnp.bfloat16)
    factor = jnp.tanh(gate[...])
    transposed = (((1,), (1,)), ((), ()))

    for k in range(1, BLOCK):
        pltpu.make_async_copy(pieces[k - 1], held.at[k], sems.at[k]).wait()
    key_squares = jnp.square(keys_t[...].astype(jnp.float32))
    key_bound = jnp.max(jnp.sum(key_squares, axis=0, keepdims=True))
    largest = 0.0
    for k in range(BLOCK):
        largest = jnp.maximum(
            largest, jnp.max(jnp.abs(held[k, :tokens].astype(jnp.float32)), axis=0, keepdims=True)
        )
    column = largest[:, :WIDTH]
    for h in range(1, GROUP):
        column = jnp.maximum(column, largest[:, h * WIDTH : (h + 1) * WIDTH])
    query_bound = jnp.sum(jnp.square(column))
    safe = query_bound * key_bound * SCALE * SCALE < SAFE_SCORE * SAFE_SCORE

    def work(step, carry):
        for h in range(GROUP):
            rows, columns = slice(h * tokens, (h + 1) * tokens), slice(h * WIDTH, (h + 1) * WIDTH)
            q_rows[rows] = held[step, :tokens, columns]
            wide = held[step, tokens : 2 * tokens, columns].astype(jnp.float32)
            d_rows[rows] = (wide * factor).astype(jnp.bfloat16)
        spans = held[step, 2 * tokens :, :tokens].astype(jnp.float32)
        low = jnp.concatenate([spans[0:1]] * BATCH_HEADS, axis=1)
        high = jnp.concatenate([spans[1:2]] * BATCH_HEADS, axis=1)
        seen = [(low <= j) & (j < high) for j in range(IMAGES)]
        for at in range(0, GROUP * tokens, block):
            rows = slice(at, at + block)
            scores = lax.dot_general(
                kv[:, :WIDTH], q_rows[rows], transposed, preferred_element_type=jnp.float32
            )
            d_probs = lax.dot_general(
                kv[:, WIDTH:], d_rows[rows], transposed, preferred_element_type=jnp.float32
            )
            probs[:, rows], d_scores[:, rows] = softmax_gradients(
                scores, d_probs, seen, False
            )
        acc[:, :WIDTH] += jnp.dot(d_scores[...], q_rows[...], preferred_element_type=jnp.float32)
        acc[:, WIDTH:] += jnp.dot(probs[...], d_rows[...], preferred_element_type=jnp.float32)
        dq_t = jnp.dot(keys_t[...], d_scores[...], preferred_element_type=jnp.float32) * SCALE
        dq_rows = dq_t.T.astype(jnp.bfloat16)
        for h in range(GROUP):
            dq[step, :, h * WIDTH : (h + 1) * WIDTH] = dq_rows[h * tokens : (h + 1) * tokens]
        for k in range(BLOCK):

            @pl.when(step == k)
            def _():
                pltpu.make_async_copy(dq.at[k], dqs[k], sems.at[BLOCK + k]).start()

        return carry

    def careful_work(index, carry):
        step, h = index // GROUP, index % GROUP
        columns = pl.ds(pl.multiple_of(h * WIDTH, WIDTH), WIDTH)
        q_one = held[step, :tokens, columns]
        wide = held[step, tokens : 2 * tokens, columns].astype(jnp.float32)
        d_one = (wide * factor).astype(jnp.bfloat16)
        spans = held[step, 2 * tokens :, :tokens].astype(jnp.float32)
        seen = [(spans[0:1] <= j) & (j < spans[1:2]) for j in range(IMAGES)]
        scores = lax.dot_general(
            kv[:, :WIDTH], q_one, transposed, preferred_element_type=jnp.float32
        )
        d_probs = lax.dot_general(
            kv[:, WIDTH:], d_one, transposed, preferred_element_type=jnp.float32
        )
        probs_one, d_scores_one = softmax_gradients(scores, d_probs, seen, True)
        acc[:, :WIDTH] += jnp.dot(d_scores_one, q_one, preferred_element_type=jnp.float32)
        acc[:, WIDTH:] += jnp.dot(probs_one, d_one, preferred_element_type=jnp.float32)
        dq_t = jnp.dot(keys_t[...], d_scores_one, preferred_element_type=jnp.float32) * SCALE
        dq[step, :, columns] = dq_t.T.astype(jnp.bfloat16)
        return carry

    @pl.when(safe)
    def _():
        lax.fori_loop(0, BLOCK, work, 0)

    @pl.when(jnp.logical_not(safe))
    def _():
        lax.fori_loop(0, BLOCK * GROUP, careful_work, 0)
        for k in range(BLOCK):
            pltpu.make_async_copy(dq.at[k], dqs[k], sems.at[BLOCK + k]).start()

    dkv[:, :WIDTH] = (acc[:, :WIDTH] * SCALE).astype(jnp.bfloat16)
    dkv[:, WIDTH:] = acc[:, WIDTH:].astype(jnp.bfloat16)
    give = pltpu.make_async_copy(dkv, dkv_any, sems.at[2 * BLOCK])
    give.start()
    for k in range(BLOCK):
        pltpu.make_async_copy(dq.at[k], dqs[k], sems.at[BLOCK + k]).wait()
    give.wait()


def gradients(gate, kv, q, d_out, spans, pieces):
    key_rows = kv.shape[0]
    tokens = q.shape[0]
    width = pieces[0].shape[1]
    rows = GROUP * tokens
    in_hbm = pl.BlockSpec(memory_space=HBM)
    return pl.pallas_call(
        grad_kernel,
        in_specs=[pl.BlockSpec(memory_space=VMEM)] + [in_hbm] * (BLOCK + 3),
        out_specs=[in_hbm] * (BLOCK + 1),
        out_shape=[jax.ShapeDtypeStruct((tokens, width), jnp.bfloat16)] * BLOCK
        + [jax.ShapeDtypeStruct(kv.shape, jnp.bfloat16)],
        scratch_shapes=[
            pltpu.VMEM(kv.shape, jnp.bfloat16),
            pltpu.VMEM((BLOCK,) + pieces[0].shape, jnp.bfloat16),
            pltpu.VMEM(spans.shape, jnp.int32),
            pltpu.VMEM((PAD, tokens), jnp.float32),
            pltpu.VMEM((BLOCK, tokens, width), jnp.bfloat16),
            pltpu.VMEM(kv.shape, jnp.bfloat16),
            pltpu.VMEM((WIDTH, key_rows), jnp.bfloat16),
            pltpu.VMEM((key_rows, rows), jnp.bfloat16),
            pltpu.VMEM((key_rows, rows), jnp.bfloat16),
            pltpu.VMEM((rows, WIDTH), jnp.bfloat16),
            pltpu.VMEM((rows, WIDTH), jnp.bfloat16),
            pltpu.VMEM(kv.shape, jnp.float32),
            pltpu.SemaphoreType.DMA((2 * BLOCK + 3,)),
        ],
        compiler_params=pltpu.CompilerParams(vmem_limit_bytes=GRADIENT_VMEM),
        cost_estimate=pl.CostEstimate(
            flops=10 * BLOCK * rows * key_rows * WIDTH,
            bytes_accessed=4 * 1024 * 1024,
            transcendentals=BLOCK * rows * key_rows,
        ),
        name="gradients",
    )(gate, kv, q, d_out, spans, *pieces)


def sum_kernel(slots, got, out):
    doc, _ = place_in_block()
    out[...] = jnp.zeros_like(out)
    for j in range(IMAGES):
        owner = slots[doc * IMAGES + j] // IMAGES
        for c in range(KV_HEADS):
            total = 0.0
            place = jnp.where(doc % 2 == 0, c, 3 - c)
            for y in range(0, GRID, 2):
                for z in range(0, GRID, 2):
                    at = (place // 2 + y) * GRID + place % 2 + z
                    total += got[at, j].astype(jnp.float32)
            out[owner, :, c * WIDTH : (c + 1) * WIDTH] = total[:, :WIDTH].astype(jnp.bfloat16)
            out[owner, :, KEY_COLUMNS + c * WIDTH : KEY_COLUMNS + (c + 1) * WIDTH] = total[
                :, WIDTH:
            ].astype(jnp.bfloat16)


def place_kernel(docs, slots, got, out):
    doc_here, _ = place_in_block()
    for s in range(IMAGES):
        doc = 0
        for d in range(docs):
            for j in range(IMAGES):
                doc += jnp.where(slots[d * IMAGES + j] == doc_here * IMAGES + s, d, 0)
        out[s] = got[doc].astype(jnp.float32)


def small(kernel, out_shape, name, scratch=()):
    return pl.pallas_call(
        kernel,
        in_specs=[
            pl.BlockSpec(memory_space=SMEM),
            pl.BlockSpec(memory_space=VMEM),
        ],
        out_specs=pl.BlockSpec(memory_space=VMEM),
        out_shape=out_shape,
        scratch_shapes=scratch,
        compiler_params=pltpu.CompilerParams(vmem_limit_bytes=VMEM_LIMIT),
        name=name,
    )


def swap(docs, k):
    pairs = []
    for d in range(docs):
        for y in range(GRID):
            for z in range(GRID):
                v, w = (y + d % 2) ^ (k // 2), (z + d % 2) ^ (k % 2)
                to = (v - d % 2) % GRID * GRID + (w - d % 2) % GRID
                pairs.append((d * GRID * GRID + y * GRID + z, d * GRID * GRID + to))
    return pairs


def shards(queries, image_kv, d_out, attn_gate, image_slots, spans):
    docs = lax.axis_size("doc")
    texts = lax.axis_size("ctx")
    images, rows, columns = image_kv.shape
    tokens, width = queries.shape[1], queries.shape[2] // KV_HEADS
    both = ("doc", "ctx")
    in_hbm = pl.BlockSpec(memory_space=HBM)
    in_vmem = pl.BlockSpec(memory_space=VMEM)
    params = pltpu.CompilerParams(vmem_limit_bytes=VMEM_LIMIT)
    block = jax.ShapeDtypeStruct((docs, rows, columns), jnp.bfloat16)
    span_rows = spans[0].T
    piece = jax.ShapeDtypeStruct((2 * tokens + PAD, width), jnp.bfloat16)
    send, *pieces = pl.pallas_call(
        functools.partial(prepare_kernel, docs),
        in_specs=[in_hbm] * 5,
        out_specs=[in_hbm] * BLOCK,
        out_shape=[block] + [piece] * (BLOCK - 1),
        scratch_shapes=[
            pltpu.SMEM(image_slots.shape, jnp.int32),
            pltpu.VMEM(image_kv.shape, jnp.bfloat16),
            pltpu.VMEM((BLOCK - 1,) + piece.shape, jnp.bfloat16),
            pltpu.VMEM(span_rows.shape, jnp.int32),
            pltpu.VMEM((PAD, tokens), jnp.float32),
            pltpu.SemaphoreType.DMA((docs + 3 * BLOCK,)),
        ],
        name="prepare",
    )(image_slots, image_kv, queries[0], d_out[0], span_rows)
    got = lax.all_to_all(send, "doc", 0, 0)
    one_head = jax.ShapeDtypeStruct((texts, images, rows, 2 * WIDTH), jnp.bfloat16)
    send = small(
        pick_kernel,
        one_head,
        "pick",
        [pltpu.VMEM((KV_HEADS, images, rows, 2 * WIDTH), jnp.bfloat16)],
    )(image_slots, got)
    pieces = [lax.ppermute(pieces[k - 1], both, swap(docs, k)) for k in range(1, BLOCK)]
    kv = lax.all_to_all(send, "ctx", 0, 0).reshape(texts * images * rows, 2 * WIDTH)
    *dqs, dkv = gradients(
        attn_gate.reshape(1, 1), kv, queries[0], d_out[0], span_rows, pieces
    )
    dqs = [dqs[0]] + [lax.ppermute(dqs[k], both, swap(docs, k)) for k in range(1, BLOCK)]
    parts = lax.all_to_all(dkv.reshape(texts, images, rows, 2 * WIDTH), "ctx", 0, 0)
    send = small(sum_kernel, block, "sum")(image_slots, parts)
    got = lax.all_to_all(send, "doc", 0, 0)
    d_image_kv = small(
        functools.partial(place_kernel, docs),
        jax.ShapeDtypeStruct(image_kv.shape, jnp.float32),
        "place",
    )(image_slots, got)
    d_queries = pl.pallas_call(
        merge_kernel,
        in_specs=[in_vmem] * BLOCK,
        out_specs=in_vmem,
        out_shape=jax.ShapeDtypeStruct(queries.shape[1:], jnp.bfloat16),
        compiler_params=params,
        name="merge",
    )(*dqs)
    return d_queries[None], d_image_kv


def solution(mesh):
    return jax.shard_map(
        shards,
        mesh=mesh,
        in_specs=(
            P("doc", "ctx", None),
            P("doc", "ctx", None),
            P("doc", "ctx", None),
            P(),
            P(),
            P("doc", "ctx", None),
        ),
        out_specs=(P("doc", "ctx", None), P("doc", "ctx", None)),
        check_vma=False,
    )
```
